32 devices in a mesh: gx: 8 (over z, x), gy: 4 (over y, core).
Axes of the slice: x: 2, y: 2, z: 4, core: 2. Of those that a mesh axis runs over, the one named last changes fastest.
Arguments:
- state: float32 [4, 256, 512, 128], P(None, 'gx', 'gy'), may hold values from -6 to 6
- velocity: float32 [3, 256, 512, 128], P(None, 'gx', 'gy'), may hold values from -6 to 6
- threshold: float32 [8, 512], P('gx', 'gy'), may hold values from 0.5 to 3
- tile_owner: int32 [4, 256, 1], P('gy', 'gx'), may hold values from 0 to 7; in each aligned block of 32 rows (0 to 31, 32 to 63, ..., all dimensions but the last counted through in order) at most 8 rows name the same one
- parcel_owner: int32 [4, 256, 1], P('gy', 'gx'), may hold values from 0 to 7; in each aligned block of 32 rows (0 to 31, 32 to 63, ..., all dimensions but the last counted through in order) at most 8 rows name the same one
- parcel_count: int32 [4, 256], P('gy', 'gx'), may hold values from 1 to 128, as said below
- parcel_share: float32 [4, 256, 128], P('gy', 'gx'), may hold values from 0.2 to 1
Outputs:
- fields: float32 [4, 256, 512, 128], P(None, 'gx', 'gy')
- ground_flux: float32 [8, 512], P('gx', 'gy')
The draws below stay inside these ranges and needn't reach their ends.
Inputs may be any that keep to these rules, and one draw needn't show every extreme that they name: `tile_owner`: among the 32 tiles of one device no owner is named more than 8 times, and that count is reached. `parcel_owner`: among the 32 rows of one owner no destination is named more than 8 times, and that count is reached. `parcel_count`: the first row of every owner has 128 live parcels.
All inputs are finite; a program needn't handle non-finite values.
Results may differ from the reference program's by a relative error of at most 0.0003.
Values sent between devices are 32-bit elements; how exact they have to be, the bound alone decides.
No kernel may reach another device: no remote copies, remote signals or barrier semaphores. Data moves between devices by JAX's collectives and lax.ppermute only.
A program may use at most 256 MiB of HBM per device.

```python
import math
import jax
import jax.numpy as jnp
import numpy as np
from jax import lax

CX = 32
CY = 128
LEVELS = 4
ROWS_DEV = 32
STEPS = 2
CAP = 8
RCAP = 8
NX = 256
NY = 512
NZ = 128
ROWS = 256
N_GX = 8
N_GY = 4


def draw_parcel_count(key, part):
    values = jax.random.randint(key, (N_GY, ROWS), 1, CY + 1)
    column = jnp.arange(ROWS)[None, :] % ROWS_DEV
    return jnp.where(column == 0, CY, values).astype(jnp.int32)


def block_levels(stream_key, dims, shards, low, top_value):
    def one(axis_at, parts):
        steps = jax.random.uniform(jax.random.fold_in(jax.random.fold_in(stream_key, 6), axis_at), (parts,), jnp.float32, low / len(shards), top_value / len(shards))
        return jnp.repeat(jnp.exp(steps), dims[axis_at] // parts).reshape((-1,) + (1,) * (len(dims) - axis_at - 1))

    level = one(*shards[0])
    for cut in shards[1:]:
        level = level * one(*cut)
    return level


def shared_out(stream_key, own, number, rows, count, top, bound, lean):
    order = jax.random.permutation(stream_key, count)
    heavy_load, usual = portions_of(count, rows * top, bound, lean, True), portions_of(count, rows * top, bound, lean, False)
    places = jnp.arange(count)

    def named(lengths, turn):
        used = int((lengths > 0).sum())
        fixed = max(1, used // 4)
        moved = fixed + (places - fixed + turn * (used - fixed)) % max(1, count - fixed)
        return jnp.zeros((count,), jnp.int32).at[order[jnp.where(places < fixed, places, moved)]].set(jnp.asarray(lengths, jnp.int32))

    lengths = jnp.where(number % 4 == 0, named(heavy_load, number // 4), named(usual, number - number // 4 - 1))
    mixed = jax.random.permutation(jax.random.fold_in(own, 3), count)
    donor, receiver = mixed[0:count // 2 * 2:2], mixed[1:count // 2 * 2:2]
    margin = jnp.minimum(lengths[donor] - 1, bound - lengths[receiver]) // 2
    margin = jnp.where((donor == order[0]) | (receiver == order[0]) | (lengths[receiver] == 0), 0, jnp.maximum(margin, 0))
    moved = jax.random.randint(jax.random.fold_in(own, 4), (count // 2,), 0, 1 << 20) % (margin + 1)
    lengths = lengths.at[donor].add(-moved).at[receiver].add(moved)
    labels = jnp.searchsorted(jnp.cumsum(lengths), jnp.arange(rows * top), side="right").astype(jnp.int32)
    grid = labels.reshape(top, rows).T
    grid = grid[jax.random.permutation(jax.random.fold_in(own, 1), rows)]
    turn = jax.random.randint(jax.random.fold_in(own, 2), (rows, 1), 0, top)
    return jnp.take_along_axis(grid, (jnp.arange(top)[None, :] + turn) % top, axis=1)


def portions_of(number_of, total, most, slope, full):
    loads = [(1 << 20) // math.isqrt(standing ** slope) + 1 for standing in range(1, number_of + 1)]
    largest = most if full else min(most, max(-(-total // number_of), total * loads[0] // sum(loads)))
    least = 1 if total - largest >= number_of - 1 else 0
    given, rest = [largest] + [least] * (number_of - 1), total - largest - least * (number_of - 1)
    while rest > 0:
        movable = [i for i in range(1, number_of) if given[i] < largest] or [i for i in range(1, number_of) if given[i] < most]
        whole, budget = sum([loads[i] for i in movable]), rest
        for i in movable:
            addition = min(most - given[i], max(1, budget * loads[i] // whole), rest)
            given[i] = given[i] + addition
            rest = rest - addition
    return np.array(given)


def noise(rng, dims, scale, most, pieces=(), dtype=jnp.bfloat16):
    result = scale * jax.random.normal(rng, dims, jnp.float32)
    if pieces:
        result = result * block_levels(rng, dims, pieces, -0.22, 0.18)
    return jnp.clip(result, -most, most).astype(dtype)


def setup_inputs(seed: int = 0) -> dict:
    seeds = jax.random.split(jax.random.key(seed), 8)
    state = noise(seeds[0], (4, NX, NY, NZ), 1.0, 6.0, ((1, 8), (2, 4)), jnp.float32)
    velocity = noise(seeds[1], (3, NX, NY, NZ), 1.0, 6.0, ((1, 8), (2, 4)), jnp.float32)
    threshold = jnp.clip(jnp.exp(math.log(3.0) - 1.7917595 * jax.random.uniform(seeds[2], (N_GX, NY), jnp.float32) ** block_levels(seeds[2], (N_GX, NY), ((0, 8), (1, 4)), -0.2, 0.2)), 0.5, 3.0)
    tile_owner_keys = jax.random.split(jax.random.fold_in(seeds[3], 1), N_GY * NX // CX)
    tile_owner_turns = jax.random.permutation(jax.random.fold_in(seeds[3], 3), N_GY * NX // CX)
    tile_owner = jax.vmap(lambda own, number: shared_out(jax.random.fold_in(seeds[3], 2), own, number, CX, N_GX, 1, CAP, 2))(tile_owner_keys, tile_owner_turns).reshape((N_GY, NX, 1))
    parcel_owner_keys = jax.random.split(jax.random.fold_in(seeds[4], 1), N_GY * ROWS // ROWS_DEV)
    parcel_owner_turns = jax.random.permutation(jax.random.fold_in(seeds[4], 3), N_GY * ROWS // ROWS_DEV)
    parcel_owner = jax.vmap(lambda own, number: shared_out(jax.random.fold_in(seeds[4], 2), own, number, ROWS_DEV, N_GX, 1, RCAP, 2))(parcel_owner_keys, parcel_owner_turns).reshape((N_GY, ROWS, 1))
    parcel_count = draw_parcel_count(jax.random.fold_in(seeds[7], 71), 0)
    parcel_share = jnp.clip(0.2 + 0.8 * jax.random.uniform(seeds[6], (N_GY, ROWS, CY), jnp.float32) ** block_levels(seeds[6], (N_GY, ROWS, CY), ((0, 4), (1, 8)), -0.2, 0.2), 0.2, 1.0)
    return {"state": state, "velocity": velocity, "threshold": threshold, "tile_owner": tile_owner, "parcel_owner": parcel_owner, "parcel_count": parcel_count, "parcel_share": parcel_share}


profile_weights = (0.4, 0.3, 0.2, 0.1)
time_step = 0.1


def friction(east, north):
    total = profile_weights[0] * (east[..., 0, :] * east[..., 0, :] + north[..., 0, :] * north[..., 0, :])
    for level in range(1, east.shape[-2]):
        total = total + profile_weights[level] * (east[..., level, :] * east[..., level, :] + north[..., level, :] * north[..., level, :])
    return total


def minmod(first, second):
    return jnp.where(first * second > 0, jnp.sign(first) * jnp.minimum(jnp.abs(first), jnp.abs(second)), 0.0)


def section(array, axis, start, stop):
    return lax.slice_in_dim(array, start, stop, axis=axis)


def divergence(field, speed, axis):
    count = field.shape[axis] - 4
    behind = section(field, axis, 0, count + 1)
    here = section(field, axis, 1, count + 2)
    ahead = section(field, axis, 2, count + 3)
    beyond = section(field, axis, 3, count + 4)
    face_speed = 0.5 * (section(speed, axis, 1, count + 2) + section(speed, axis, 2, count + 3))
    upwind = face_speed * (here + 0.5 * minmod(ahead - here, here - behind))
    downwind = face_speed * (ahead - 0.5 * minmod(beyond - ahead, ahead - here))
    fluxes = jnp.where(face_speed > 0, upwind, downwind)
    return section(fluxes, axis, 1, count + 1) - section(fluxes, axis, 0, count)


def advance(padded, wind):
    inner = padded[:, 2:-2, 2:-2, 2:-2]
    along_x = divergence(padded[:, :, 2:-2, 2:-2], wind[0:1, :, 2:-2, 2:-2], 1)
    along_y = divergence(padded[:, 2:-2, :, 2:-2], wind[1:2, 2:-2, :, 2:-2], 2)
    along_z = divergence(padded[:, 2:-2, 2:-2, :], wind[2:3, 2:-2, 2:-2, :], 3)
    return inner - time_step * (along_x + along_y + along_z)


def reference(state, velocity, threshold, tile_owner, parcel_owner, parcel_count, parcel_share):
    highest = lax.Precision.HIGHEST
    east = velocity[0, :, :, 0:LEVELS].reshape(NX, N_GY, CY, LEVELS).transpose(1, 0, 3, 2)
    north = velocity[1, :, :, 0:LEVELS].reshape(NX, N_GY, CY, LEVELS).transpose(1, 0, 3, 2)
    stress = friction(east, north)
    owners = tile_owner[:, :, 0]
    choose = (owners[:, :, None] == jnp.arange(N_GX)[None, None, :]).astype(jnp.float32)
    limits = threshold.reshape(N_GX, N_GY, CY).transpose(1, 0, 2)
    tile_limit = jnp.einsum("yxo,yoj->yxj", choose, limits, precision=highest)
    lifting = jnp.maximum(stress - tile_limit, 0.0)
    patch = jnp.einsum("yxo,yxj->yoj", choose, lifting, precision=highest) / CX
    ground_flux = patch.transpose(1, 0, 2).reshape(N_GX, NY)
    source = jnp.arange(ROWS) // ROWS_DEV
    row_flux = patch[:, source, :]
    reach = (jnp.arange(CY)[None, None, :] < parcel_count[:, :, None]).astype(jnp.float32)
    masses = row_flux * parcel_share * reach
    landing_x = parcel_owner[:, :, 0] * CX + source[None, :] % CX
    place = (landing_x[:, :, None] == jnp.arange(NX)[None, None, :]).astype(jnp.float32)
    deposit = jnp.einsum("yrx,yrj->yxj", place, masses, precision=highest)
    deposit = deposit.transpose(1, 0, 2).reshape(NX, NY)
    fields = state.at[3, :, :, 0].add(deposit)
    wind = jnp.pad(velocity, ((0, 0), (2, 2), (2, 2), (2, 2)))
    for substep in range(STEPS):
        fields = lax.map(lambda component: advance(jnp.pad(component, 2)[None], wind)[0], fields)
    return fields, ground_flux
```

```python
import functools

import jax
import jax.numpy as jnp
from jax import lax
from jax.experimental import pallas as pl
from jax.experimental.pallas import tpu as pltpu
from jax.sharding import PartitionSpec as P

LEVELS = 4
profile_weights = (0.4, 0.3, 0.2, 0.1)
time_step = 0.1
FACTOR = 0.25 * time_step

VMEM_LIMIT = 48 * 1024 * 1024
PAD = 8
CHUNK = 4
HIGHEST = lax.Precision.HIGHEST
ANY = pl.BlockSpec(memory_space=pl.ANY)
VMEM = pl.BlockSpec(memory_space=pltpu.VMEM)
SMEM = pl.BlockSpec(memory_space=pltpu.SMEM)


def params():
    return pltpu.CompilerParams(vmem_limit_bytes=VMEM_LIMIT)


def cost(flops, moved):
    return pl.CostEstimate(flops=int(flops), bytes_accessed=int(moved), transcendentals=0)


def minmod(a, b):
    return jnp.maximum(jnp.minimum(a, b), jnp.minimum(jnp.maximum(a, b), 0.0))


def tile_rows(row, count):
    return pl.ds(PAD + row, 8, stride=count)


class Fields:
    def __init__(self, q, u, v, w, fx, lx, block, comps, rows, u_at, v_at):
        self.q, self.u, self.v, self.w, self.fx, self.lx = q, u, v, w, fx, lx
        self.block, self.comps, self.u_at, self.v_at = block, comps, u_at, v_at
        self.tiles = rows // 8

    def field(self, c, slab, row):
        return self.q[self.block, c, slab, tile_rows(row, self.tiles), :]

    def east(self, slab, row):
        return self.u[self.block, slab + self.u_at, pl.ds(row, 8, stride=self.tiles), :]

    def north(self, slab, row):
        return self.v[self.block, slab + self.v_at, tile_rows(row, self.tiles), :]

    def up(self, slab, row):
        return self.w[self.block, slab + self.v_at, pl.ds(row, 8, stride=self.tiles), :]


def first_face(f):
    for t in range(f.tiles):
        speed = FACTOR * (f.east(0, t) + f.east(1, t))
        right = speed > 0
        for c in range(f.comps):
            a, b, q0, q1 = [f.field(c, s, t) for s in range(4)]
            middle = q0 - b
            left_state = (b + b) + minmod(middle, b - a)
            slope = minmod(q1 - q0, middle)
            twice = q0 + q0
            f.fx[t, c] = speed * jnp.where(right, left_state, twice - slope)
            f.lx[t, c] = twice + slope


def slab_step(f, k, put):
    slab = k + 2
    lane = lax.broadcasted_iota(jnp.int32, (8, f.q.shape[-1]), 1)
    top = f.q.shape[-1] - 1
    is_first, is_last = lane == 0, lane == top
    carry = []
    north_here = f.north(k, 0)
    speed = FACTOR * (f.north(k, -1) + north_here)
    for c in range(f.comps):
        a, b, q0, q1 = [f.field(c, slab, r) for r in (-2, -1, 0, 1)]
        middle, ahead = q0 - b, q1 - q0
        left_state = (b + b) + minmod(middle, b - a)
        slope = minmod(ahead, middle)
        twice = q0 + q0
        flux = speed * jnp.where(speed > 0, left_state, twice - slope)
        carry.append((q0, q1, ahead, twice, twice + slope, flux))
    for t in range(f.tiles):
        speed_x = FACTOR * (f.east(k + 1, t) + f.east(k + 2, t))
        north_next = f.north(k, t + 1)
        speed_y = FACTOR * (north_here + north_next)
        north_here = north_next
        rise = FACTOR * f.up(k, t)
        speed_z = rise + pltpu.roll(rise, top, 1)
        speed_z = jnp.where(is_last, jnp.maximum(rise, 0.0), speed_z)
        ground = jnp.minimum(rise, 0.0)
        go_x, go_y, go_z = speed_x > 0, speed_y > 0, speed_z > 0
        for c in range(f.comps):
            q0, y1, ahead, twice, left_y, flux_y = carry[c]
            y2 = f.field(c, slab, t + 2)
            beyond = y2 - y1
            slope = minmod(beyond, ahead)
            twice_y = y1 + y1
            flux_next = speed_y * jnp.where(go_y, left_y, twice_y - slope)
            total = flux_next - flux_y
            carry[c] = (y1, y2, beyond, twice_y, twice_y + slope, flux_next)
            x1, x2 = f.field(c, slab + 1, t), f.field(c, slab + 2, t)
            slope = minmod(x2 - x1, x1 - q0)
            twice_x = x1 + x1
            flux_x = speed_x * jnp.where(go_x, f.lx[t, c], twice_x - slope)
            total = total + (flux_x - f.fx[t, c])
            f.fx[t, c] = flux_x
            f.lx[t, c] = twice_x + slope
            d = jnp.where(is_last, 0.0, pltpu.roll(q0, top, 1)) - q0
            below = jnp.where(is_first, q0, pltpu.roll(d, 1, 1))
            slope = minmod(d, below)
            lower = twice - slope
            flux_z = speed_z * jnp.where(go_z, twice + slope, pltpu.roll(lower, top, 1))
            flux_below = jnp.where(is_first, ground * lower, pltpu.roll(flux_z, 1, 1))
            total = total + (flux_z - flux_below)
            put(c, t, q0 - total)


def insert_y_halo(q, v, block, slab, v_slab, x, below, above, v_below, v_above, comps, rows):
    for c in range(comps):
        for r in range(2):
            q[block, c, slab, PAD - 2 + r : PAD - 1 + r, :] = below[2 * c + r, pl.ds(x, 1), :]
            q[block, c, slab, PAD + rows + r : PAD + rows + r + 1, :] = above[2 * c + r, pl.ds(x, 1), :]
    if v_slab is not None:
        v[block, v_slab, PAD - 1 : PAD, :] = v_below[0, pl.ds(x, 1), :]
        v[block, v_slab, PAD + rows : PAD + rows + 1, :] = v_above[0, pl.ds(x, 1), :]


def add_deposit(q, block, c, slab, column, deposit, rows):
    lanes = deposit.shape[-1]
    lane = lax.broadcasted_iota(jnp.int32, (rows, lanes), 1)
    turned = pltpu.roll(deposit[...], lanes - column, 1)
    here = q[block, c, slab, PAD : PAD + rows, :]
    q[block, c, slab, PAD : PAD + rows, :] = here + jnp.where(lane == 0, turned, 0.0)


def interior_kernel(sources, dusty, pack, count, *refs):
    refs = list(refs)
    fields, velocity = refs[:count], refs[count]
    below, above, v_below, v_above = refs[count + 1 : count + 5]
    del refs[: count + 5]
    deposit = refs.pop(0) if dusty else None
    out = refs.pop(0)
    if pack:
        pack_low, pack_high = refs.pop(0), refs.pop(0)
    q, u, v, w, fx, lx, stage, in_sem, out_sem = refs
    comps = len(sources)
    slabs, rows = q.shape[2], stage.shape[2]
    chunks = slabs // CHUNK
    inner = pl.ds(PAD, rows)

    def start(source, target, sem):
        pltpu.make_async_copy(source, target, sem).start()

    for j in range(chunks):
        at = j * CHUNK
        for c, (number, part, low, high, edge_part) in enumerate(sources):
            begin, end = at, at + CHUNK
            if low is not None and j == 0:
                begin += 2
                start(fields[low].at[edge_part], q.at[0, c, pl.ds(0, 2), inner], in_sem.at[j, c])
            if high is not None and j == chunks - 1:
                end -= 2
                start(fields[high].at[edge_part], q.at[0, c, pl.ds(slabs - 2, 2), inner], in_sem.at[j, c])
            span = pl.ds(begin, end - begin)
            start(fields[number].at[part, span], q.at[0, c, span, inner], in_sem.at[j, c])
        span = pl.ds(at, CHUNK)
        start(velocity.at[0, span], u.at[0, span], in_sem.at[j, comps])
        start(velocity.at[1, span], v.at[0, span, inner], in_sem.at[j, comps + 1])
        start(velocity.at[2, span], w.at[0, span], in_sem.at[j, comps + 2])

    def arrive(j):
        span = pl.ds(j * CHUNK, CHUNK)
        spots = [q.at[0, c, span, inner] for c in range(comps)]
        spots += [u.at[0, span], v.at[0, span, inner], w.at[0, span]]
        for n, spot in enumerate(spots):
            pltpu.make_async_copy(spot, spot, in_sem.at[j, n]).wait()

        def complete(x, _):
            insert_y_halo(q, v, 0, x, x, x, below, above, v_below, v_above, comps, rows)
            if dusty:
                add_deposit(q, 0, comps - 1, x, x + 2, deposit, rows)
            return 0

        lax.fori_loop(j * CHUNK, (j + 1) * CHUNK, complete, 0)

    f = Fields(q, u, v, w, fx, lx, 0, comps, rows, 1, 2)
    arrive(0)
    first_face(f)

    def step(k, _):
        @pl.when(k % CHUNK == 0)
        def _():
            arrive(k // CHUNK + 1)

        def put(c, t, value):
            stage[c, k, pl.ds(t, 8, stride=f.tiles), :] = value

        slab_step(f, k, put)
        pltpu.make_async_copy(stage.at[:, k], out.at[:, k + 2], out_sem).start()
        if pack:
            for c in range(comps):
                for r in range(2):
                    pack_low[2 * c + r, pl.ds(k + 2, 1), :] = stage[c, k, r : r + 1, :]
                    pack_high[2 * c + r, pl.ds(k + 2, 1), :] = stage[c, k, rows - 2 + r : rows - 1 + r, :]
        return 0

    if pack:
        pack_low[...] = jnp.zeros_like(pack_low)
        pack_high[...] = jnp.zeros_like(pack_high)
    lax.fori_loop(0, slabs - 4, step, 0)
    pltpu.make_async_copy(stage, out.at[:, pl.ds(2, slabs - 4)], out_sem).wait()


def interior(fields, sources, velocity, below, above, v_below, v_above, deposit, pack):
    comps = len(sources)
    _, slabs, rows, lanes = velocity.shape
    out_shape = [jax.ShapeDtypeStruct((comps, slabs, rows, lanes), jnp.float32)]
    out_specs = [ANY]
    if pack:
        out_shape += [jax.ShapeDtypeStruct((2 * comps, slabs, lanes), jnp.float32)] * 2
        out_specs += [VMEM] * 2
    operands = list(fields) + [velocity, below, above, v_below, v_above]
    specs = [ANY] * (len(fields) + 1) + [VMEM] * 4
    if deposit is not None:
        operands.append(deposit)
        specs.append(VMEM)
    high = rows + 2 * PAD
    cells = comps * (slabs - 4) * rows * lanes
    return pl.pallas_call(
        functools.partial(interior_kernel, sources, deposit is not None, pack, len(fields)),
        out_shape=tuple(out_shape),
        in_specs=specs,
        out_specs=tuple(out_specs),
        scratch_shapes=[
            pltpu.VMEM((1, comps, slabs, high, lanes), jnp.float32),
            pltpu.VMEM((1, slabs, rows, lanes), jnp.float32),
            pltpu.VMEM((1, slabs, high, lanes), jnp.float32),
            pltpu.VMEM((1, slabs, rows, lanes), jnp.float32),
            pltpu.VMEM((rows // 8, comps, 8, lanes), jnp.float32),
            pltpu.VMEM((rows // 8, comps, 8, lanes), jnp.float32),
            pltpu.VMEM((comps, slabs - 4, rows, lanes), jnp.float32),
            pltpu.SemaphoreType.DMA((slabs // CHUNK, comps + 3)),
            pltpu.SemaphoreType.DMA,
        ],
        compiler_params=params(),
        cost_estimate=cost(45 * cells, 4 * (2 * cells + 3 * slabs * rows * lanes)),
        name="interior",
    )(*operands)


def boundary_kernel(pieces, count, last, slabs, *refs):
    refs = list(refs)
    fields, velocity, u_low, u_high = refs[:count], refs[count], refs[count + 1], refs[count + 2]
    below, above, v_below, v_above = refs[count + 3 : count + 7]
    del refs[: count + 7]
    if last:
        out = refs[1]
        del refs[:2]
    else:
        deposit, packed, ends, packs = refs[0], refs[1:5], refs[5:7], refs[7:9]
        del refs[:9]
    q, u, v, w, fx, lx, stage, in_sem, out_sem = refs
    comps, rows = q.shape[1], u.shape[2]
    inner = pl.ds(PAD, rows)

    def start(source, target, sem):
        pltpu.make_async_copy(source, target, sem).start()

    for block, c, first, number, index, size in pieces:
        start(fields[number].at[index], q.at[block, c, pl.ds(first, size), inner], in_sem.at[block, 0])
    edge = u_low.shape[0] - 1
    start(u_low.at[pl.ds(edge, 1)], u.at[0, pl.ds(0, 1)], in_sem.at[0, 1])
    start(velocity.at[0, pl.ds(0, 3)], u.at[0, pl.ds(1, 3)], in_sem.at[0, 1])
    start(velocity.at[0, pl.ds(slabs - 3, 3)], u.at[1, pl.ds(0, 3)], in_sem.at[1, 1])
    start(u_high.at[pl.ds(edge, 1)], u.at[1, pl.ds(3, 1)], in_sem.at[1, 1])
    for block in range(2):
        span = pl.ds(block * (slabs - 2), 2)
        start(velocity.at[1, span], v.at[block, :, inner], in_sem.at[block, 2])
        start(velocity.at[2, span], w.at[block], in_sem.at[block, 3])
    if not last:
        for target, parts in ((packs[0], packed[0::2]), (packs[1], packed[1::2])):
            at = 0
            for part in parts:
                target[at : at + part.shape[0]] = part[...]
                at += part.shape[0]

    def one(block, _):
        spots = [q.at[block, :, :, inner], u.at[block], v.at[block, :, inner], w.at[block]]
        for n, spot in enumerate(spots):
            pltpu.make_async_copy(spot, spot, in_sem.at[block, n]).wait()
        begin = block * (slabs - 2)

        def complete(k, _):
            insert_y_halo(q, v, block, k + 2, k, begin + k, below, above, v_below, v_above, comps, rows)
            return 0

        lax.fori_loop(0, 2, complete, 0)
        if not last:

            def dust(slab, _):
                add_deposit(q, block, comps - 1, slab, begin + slab, deposit, rows)
                return 0

            lax.fori_loop(0, 6, dust, 0)
        f = Fields(q, u, v, w, fx, lx, block, comps, rows, 0, 0)
        first_face(f)

        def step(k, _):
            def put(c, t, value):
                stage[block, c, k, pl.ds(t, 8, stride=f.tiles), :] = value

            slab_step(f, k, put)
            if not last:
                x = pl.ds(begin + k, 1)
                for c in range(comps):
                    for r in range(2):
                        packs[0][2 * c + r, x, :] = stage[block, c, k, r : r + 1, :]
                        packs[1][2 * c + r, x, :] = stage[block, c, k, rows - 2 + r : rows - 1 + r, :]
            return 0

        lax.fori_loop(0, 2, step, 0)
        return 0

    lax.fori_loop(0, 2, one, 0)
    copies = []
    for block in range(2):
        target = out.at[:, pl.ds(block * (slabs - 2), 2)] if last else ends[block]
        copies.append(pltpu.make_async_copy(stage.at[block], target, out_sem.at[block]))
    for copy in copies:
        copy.start()
    for copy in copies:
        copy.wait()


def boundary(fields, pieces, velocity, u_low, u_high, below, above, v_below, v_above, *, deposit=None, packed=None, out=None):
    last = out is not None
    _, slabs, rows, lanes = velocity.shape
    comps = 4
    operands = list(fields) + [velocity, u_low, u_high, below, above, v_below, v_above]
    specs = [ANY] * (len(fields) + 3) + [VMEM] * 4
    if last:
        aliases = {len(operands): 0}
        operands.append(out)
        specs.append(ANY)
        out_shape = jax.ShapeDtypeStruct(out.shape, out.dtype)
        out_specs = ANY
    else:
        aliases = {}
        operands += [deposit, *packed]
        specs += [VMEM] * 5
        out_shape = (jax.ShapeDtypeStruct((comps, 2, rows, lanes), jnp.float32),) * 2
        out_shape += (jax.ShapeDtypeStruct((2 * comps, slabs, lanes), jnp.float32),) * 2
        out_specs = (ANY, ANY, VMEM, VMEM)
    high = rows + 2 * PAD
    cells = comps * 4 * rows * lanes
    return pl.pallas_call(
        functools.partial(boundary_kernel, pieces, len(fields), last, slabs),
        out_shape=out_shape,
        in_specs=specs,
        out_specs=out_specs,
        scratch_shapes=[
            pltpu.VMEM((2, comps, 6, high, lanes), jnp.float32),
            pltpu.VMEM((2, 4, rows, lanes), jnp.float32),
            pltpu.VMEM((2, 2, high, lanes), jnp.float32),
            pltpu.VMEM((2, 2, rows, lanes), jnp.float32),
            pltpu.VMEM((rows // 8, comps, 8, lanes), jnp.float32),
            pltpu.VMEM((rows // 8, comps, 8, lanes), jnp.float32),
            pltpu.VMEM((2, comps, 2, rows, lanes), jnp.float32),
            pltpu.SemaphoreType.DMA((2, 4)),
            pltpu.SemaphoreType.DMA((2,)),
        ],
        input_output_aliases=aliases,
        compiler_params=params(),
        cost_estimate=cost(50 * cells, 4 * 6 * cells),
        name="boundary",
    )(*operands)


def pack_x_kernel(state, velocity, low, high, sems):
    comps, slabs = state.shape[0], state.shape[1]
    copies = []
    for n, (target, first, edge) in enumerate(((low, 0, 0), (high, slabs - 2, slabs - 1))):
        for c in range(comps):
            copies.append(
                pltpu.make_async_copy(
                    state.at[c, pl.ds(first, 2)], target.at[pl.ds(2 * c, 2)], sems.at[n, c]
                )
            )
        copies.append(
            pltpu.make_async_copy(
                velocity.at[0, pl.ds(edge, 1)], target.at[pl.ds(2 * comps, 1)], sems.at[n, comps]
            )
        )
    for copy in copies:
        copy.start()
    for copy in copies:
        copy.wait()


def pack_x(state, velocity):
    comps, _, rows, lanes = state.shape
    shape = jax.ShapeDtypeStruct((2 * comps + 1, rows, lanes), jnp.float32)
    return pl.pallas_call(
        pack_x_kernel,
        out_shape=(shape, shape),
        in_specs=[ANY, ANY],
        out_specs=(ANY, ANY),
        scratch_shapes=[pltpu.SemaphoreType.DMA((2, comps + 1))],
        compiler_params=params(),
        cost_estimate=cost(0, 4 * 4 * (2 * comps + 1) * rows * lanes),
        name="pack_x",
    )(state, velocity)


def as_row(column, width):
    shape = (column.shape[0], width)
    same = lax.broadcasted_iota(jnp.int32, shape, 0) == lax.broadcasted_iota(jnp.int32, shape, 1)
    return jnp.sum(jnp.where(same, column, 0.0), axis=0, keepdims=True)


def as_column(row):
    count = row.shape[1]
    shape = (count, count)
    same = lax.broadcasted_iota(jnp.int32, shape, 0) == lax.broadcasted_iota(jnp.int32, shape, 1)
    return jnp.sum(jnp.where(same, row, 0.0), axis=1, keepdims=True)


def survey_kernel(
    groups, low_in, high_in, v_low, v_high, wind, threshold, tile_owner, parcel_owner, count, share,
    low, high, payload, gathered,
):
    step, steps = pl.program_id(0), pl.num_programs(0)
    comps, part, rows, lanes = low_in.shape[0], wind.shape[1], wind.shape[2], wind.shape[3]
    slabs = share.shape[1]
    for x in range(part):
        for c in range(comps):
            for r in range(2):
                low[2 * c + r, x : x + 1, :] = low_in[c, x, r : r + 1, :]
                high[2 * c + r, x : x + 1, :] = high_in[c, x, 6 + r : 7 + r, :]
        low[2 * comps, x : x + 1, :] = v_low[0, x, 0:1, :]
        high[2 * comps, x : x + 1, :] = v_high[0, x, 7:8, :]
    lane = lax.broadcasted_iota(jnp.int32, (rows, lanes), 1)
    weight = jnp.zeros((rows, lanes), jnp.float32)
    for level, value in enumerate(profile_weights):
        weight = jnp.where(lane == level, value, weight)
    total = jnp.zeros((rows, lanes), jnp.float32)
    for x in range(part):
        east, north = wind[0, x], wind[1, x]
        friction = jnp.where(lane < LEVELS, weight * (east * east + north * north), 0.0)
        total = total + pltpu.roll(friction, LEVELS * x, 1) if x else friction

    @pl.when(step == 0)
    def _():
        gathered[...] = total

    @pl.when(step > 0)
    def _():
        gathered[...] += pltpu.roll(total, LEVELS * part * step, 1)

    @pl.when(step == steps - 1)
    def _():
        turned = gathered[...].T
        shape = (slabs, lanes)
        pick = (
            lax.broadcasted_iota(jnp.int32, shape, 1) // LEVELS == lax.broadcasted_iota(jnp.int32, shape, 0)
        ).astype(jnp.float32)
        payload[0:slabs] = jnp.dot(pick, turned, precision=HIGHEST, preferred_element_type=jnp.float32)
        payload[slabs : slabs + 8] = jnp.zeros((8, lanes), jnp.float32)
        payload[slabs : slabs + 1] = threshold[...]
        payload[slabs + 1 : slabs + 2] = as_row(tile_owner[0].astype(jnp.float32), lanes)
        owners = as_row(parcel_owner[0].astype(jnp.float32), slabs)
        shape = (groups, slabs)
        place = (owners == lax.broadcasted_iota(jnp.int32, shape, 0).astype(jnp.float32)).astype(jnp.float32)
        live = as_column(count[...].astype(jnp.float32))
        shape = (slabs, lanes)
        reach = lax.broadcasted_iota(jnp.int32, shape, 1).astype(jnp.float32) < live
        masses = jnp.where(reach, share[0], 0.0)
        payload[slabs + 8 : slabs + 8 + groups] = jnp.dot(
            place, masses, precision=HIGHEST, preferred_element_type=jnp.float32
        )


def survey(groups, state, velocity, threshold, tile_owner, parcel_owner, count, share):
    comps, slabs, rows, lanes = state.shape
    part = 8
    last = rows // 8 - 1

    def whole(array):
        return pl.BlockSpec(array.shape, lambda i: (0,) * array.ndim)

    packed = jax.ShapeDtypeStruct((2 * comps + 1, slabs, lanes), jnp.float32)
    packed_spec = pl.BlockSpec((2 * comps + 1, part, lanes), lambda i: (0, i, 0))
    height = slabs + 8 + groups
    return pl.pallas_call(
        functools.partial(survey_kernel, groups),
        grid=(slabs // part,),
        out_shape=(packed, packed, jax.ShapeDtypeStruct((height, lanes), jnp.float32)),
        in_specs=[
            pl.BlockSpec((comps, part, 8, lanes), lambda i: (0, i, 0, 0)),
            pl.BlockSpec((comps, part, 8, lanes), lambda i: (0, i, last, 0)),
            pl.BlockSpec((1, part, 8, lanes), lambda i: (1, i, 0, 0)),
            pl.BlockSpec((1, part, 8, lanes), lambda i: (1, i, last, 0)),
            pl.BlockSpec((2, part, rows, lanes), lambda i: (0, i, 0, 0)),
            whole(threshold),
            whole(tile_owner),
            whole(parcel_owner),
            whole(count),
            whole(share),
        ],
        out_specs=(packed_spec, packed_spec, pl.BlockSpec((height, lanes), lambda i: (0, 0))),
        scratch_shapes=[pltpu.VMEM((rows, lanes), jnp.float32)],
        compiler_params=params(),
        cost_estimate=cost(10 * slabs * rows * lanes, 10 * slabs * rows * lanes),
        name="survey",
    )(state, state, velocity, velocity, velocity, threshold, tile_owner, parcel_owner, count, share)


def deposit_kernel(slabs, me, gathered, low_in, high_in, flux_out, deposit, low, high, flux, dropped):
    groups, lanes = gathered.shape[0], gathered.shape[2]
    here = me[0]
    limits = jnp.concatenate([gathered[g, slabs : slabs + 1] for g in range(groups)], axis=0)
    total = jnp.zeros((groups, lanes), jnp.float32)
    shape = (groups, slabs)
    numbers = lax.broadcasted_iota(jnp.int32, shape, 0).astype(jnp.float32)
    for g in range(groups):
        owners = gathered[g, slabs + 1 : slabs + 2, 0:slabs]
        stress = gathered[g, 0:slabs]
        named = (owners == numbers).astype(jnp.float32)
        limit = lax.dot_general(
            named, limits, (((0,), (0,)), ((), ())), precision=HIGHEST, preferred_element_type=jnp.float32
        )
        lifting = jnp.maximum(stress - limit, 0.0)
        total = total + jnp.dot(named, lifting, precision=HIGHEST, preferred_element_type=jnp.float32)
    flux[...] = total / slabs
    flux_out[...] = flux[pl.ds(here, 1), :]
    dropped[...] = jnp.zeros_like(dropped)
    before, after = jnp.maximum(here - 1, 0), jnp.minimum(here + 1, groups - 1)
    has_before, has_after = here > 0, here < groups - 1
    base = slabs + 8
    for p in range(groups):
        x = p % slabs
        row = flux[p : p + 1, :]
        dropped[x + 2 : x + 3] += row * gathered[p, pl.ds(base + here, 1), :]
        if x >= slabs - 2:
            mass = row * gathered[p, pl.ds(base + before, 1), :]
            dropped[x - slabs + 2 : x - slabs + 3] += jnp.where(has_before, mass, 0.0)
        if x < 2:
            mass = row * gathered[p, pl.ds(base + after, 1), :]
            dropped[x + slabs + 2 : x + slabs + 3] += jnp.where(has_after, mass, 0.0)
    deposit[...] = dropped[...].T
    own = dropped[2 : 2 + slabs, :]
    lane = lax.broadcasted_iota(jnp.int32, (slabs, lanes), 1)
    rows = lanes
    for r in range(2):
        low[r] = low_in[r] + jnp.where(lane == 0, own[:, r : r + 1], 0.0)
        high[r] = high_in[r] + jnp.where(lane == 0, own[:, rows - 2 + r : rows - 1 + r], 0.0)


def settle(me, gathered, low, high, slabs):
    groups, _, lanes = gathered.shape
    edge = jax.ShapeDtypeStruct(low.shape, jnp.float32)
    return pl.pallas_call(
        functools.partial(deposit_kernel, slabs),
        out_shape=(
            jax.ShapeDtypeStruct((1, lanes), jnp.float32),
            jax.ShapeDtypeStruct((lanes, lanes), jnp.float32),
            edge,
            edge,
        ),
        in_specs=[SMEM, VMEM, VMEM, VMEM],
        out_specs=(VMEM, VMEM, VMEM, VMEM),
        scratch_shapes=[
            pltpu.VMEM((groups, lanes), jnp.float32),
            pltpu.VMEM((lanes, lanes), jnp.float32),
        ],
        compiler_params=params(),
        cost_estimate=cost(10**6, 10**6),
        name="settle",
    )(me, gathered, low, high)


def exchange(low, high, axis):
    count = lax.axis_size(axis)
    forward = [(i, i + 1) for i in range(count - 1)]
    backward = [(target, source) for source, target in forward]
    return lax.ppermute(high, axis, forward), lax.ppermute(low, axis, backward)


def shards(state, velocity, threshold, tile_owner, parcel_owner, parcel_count, parcel_share):
    groups = lax.axis_size("gx")
    slabs = state.shape[1]
    me = lax.axis_index("gx").astype(jnp.int32).reshape(1)

    x_low, x_high = exchange(*pack_x(state, velocity), "gx")
    low, high, payload = survey(
        groups, state, velocity, threshold, tile_owner, parcel_owner, parcel_count, parcel_share
    )
    v_low, v_high = low[8:9], high[8:9]
    keep = jnp.concatenate
    below, above = exchange(keep([low[0:6], v_low]), keep([high[0:6], v_high]), "gy")
    v_below, v_above = below[6:7], above[6:7]
    gathered = lax.all_gather(payload, "gx")
    flux, deposit, dust_low, dust_high = settle(me, gathered, low[6:8], high[6:8], slabs)
    dust_below, dust_above = exchange(dust_low, dust_high, "gy")

    sources = [(0, c, None, None, None) for c in range(3)]
    first, pack_low, pack_high = interior(
        [state], sources, velocity, below, above, v_below, v_above, None, True
    )
    sources = [(0, 3, None, None, None)]
    dust, dust_pack_low, dust_pack_high = interior(
        [state], sources, velocity, dust_below, dust_above, v_below, v_above, deposit, True
    )
    pieces = []
    for c in range(4):
        pieces += [
            (0, c, 0, 1, (pl.ds(2 * c, 2),), 2),
            (0, c, 2, 0, (c, pl.ds(0, 4)), 4),
            (1, c, 0, 0, (c, pl.ds(slabs - 4, 4)), 4),
            (1, c, 4, 2, (pl.ds(2 * c, 2),), 2),
        ]
    all_below, all_above = keep([below[0:6], dust_below]), keep([above[0:6], dust_above])
    end_low, end_high, y_low, y_high = boundary(
        [state, x_low, x_high], pieces, velocity, x_low, x_high, all_below, all_above, v_below, v_above,
        deposit=deposit, packed=(pack_low, pack_high, dust_pack_low, dust_pack_high),
    )
    x2_low, x2_high = exchange(end_low, end_high, "gx")
    below, above = exchange(y_low, y_high, "gy")
    sources = [(0, c, 2, 3, c) for c in range(3)] + [(1, 0, 2, 3, 3)]
    (inside,) = interior(
        [first, dust, end_low, end_high], sources, velocity, below, above, v_below, v_above, None, False
    )
    pieces = []
    for c in range(4):
        number, part = (0, c) if c < 3 else (1, 0)
        pieces += [
            (0, c, 0, 4, (c,), 2),
            (0, c, 2, 2, (c,), 2),
            (0, c, 4, number, (part, pl.ds(2, 2)), 2),
            (1, c, 0, number, (part, pl.ds(slabs - 4, 2)), 2),
            (1, c, 2, 3, (c,), 2),
            (1, c, 4, 5, (c,), 2),
        ]
    fields = boundary(
        [first, dust, end_low, end_high, x2_low, x2_high], pieces, velocity, x_low, x_high, below, above,
        v_below, v_above, out=inside,
    )
    return fields, flux


def solution(mesh):
    return jax.shard_map(
        shards,
        mesh=mesh,
        in_specs=(
            P(None, "gx", "gy", None),
            P(None, "gx", "gy", None),
            P("gx", "gy"),
            P("gy", "gx", None),
            P("gy", "gx", None),
            P("gy", "gx"),
            P("gy", "gx", None),
        ),
        out_specs=(P(None, "gx", "gy", None), P("gx", "gy")),
        check_vma=False,
    )
```

```python
import functools

import jax
import jax.numpy as jnp
from jax import lax
from jax.experimental import pallas as pl
from jax.experimental.pallas import tpu as pltpu
from jax.sharding import PartitionSpec as P

LEVELS = 4
profile_weights = (0.4, 0.3, 0.2, 0.1)
time_step = 0.1
FACTOR = 0.25 * time_step

VMEM_LIMIT = 48 * 1024 * 1024
PAIR = 2
GROUP = 8
CHUNK = 4
AHEAD = 3
HIGHEST = lax.Precision.HIGHEST
ANY = pl.BlockSpec(memory_space=pl.ANY)
VMEM = pl.BlockSpec(memory_space=pltpu.VMEM)
SMEM = pl.BlockSpec(memory_space=pltpu.SMEM)


def params():
    return pltpu.CompilerParams(vmem_limit_bytes=VMEM_LIMIT)


def cost(flops, moved):
    return pl.CostEstimate(flops=int(flops), bytes_accessed=int(moved), transcendentals=0)


def minmod(a, b):
    return jnp.maximum(jnp.minimum(a, b), jnp.minimum(jnp.maximum(a, b), 0.0))


def tile_of(ref, t, tiles):
    return ref[pl.ds(t, 8, stride=tiles), :]


class Slabs:
    def __init__(self, q, u, v, w, fx, lx, block, u_at, v_at):
        self.q, self.u, self.v, self.w, self.fx, self.lx = q, u, v, w, fx, lx
        self.block, self.u_at, self.v_at = block, u_at, v_at
        self.comps, self.tiles, self.lanes = q.shape[1], w.shape[2], q.shape[-1]

    def field(self, c, slab, t):
        return self.q[self.block, c, slab, t + 2]

    def east(self, slab, t):
        return self.u[self.block, slab + self.u_at, t]

    def north(self, slab, t):
        return self.v[self.block, slab + self.v_at, t + 1]

    def up(self, slab, t):
        return self.w[self.block, slab + self.v_at, t]


def each(function, *lists):
    return [function(*items) for items in zip(*lists)]


def minmods(a, b):
    low, high = each(jnp.minimum, a, b), each(jnp.maximum, a, b)
    high = each(lambda x: jnp.minimum(x, 0.0), high)
    return each(jnp.maximum, low, high)


def difference(a, b):
    return each(lambda x, y: x - y, a, b)


def total_of(a, b):
    return each(lambda x, y: x + y, a, b)


def face_flux(speeds, masks, low_side, high_side):
    picked = each(jnp.where, masks, low_side, high_side)
    return each(lambda x, y: x * y, speeds, picked)


def staged(jobs):
    waiting = []
    for job in jobs:
        stores = job()
        for ref, index, value in waiting:
            ref[index] = value
        waiting = stores
    for ref, index, value in waiting:
        ref[index] = value


def first_face(f):
    def job(ts):
        spots = [(t, c) for t in ts for c in range(f.comps)]
        speeds = {t: FACTOR * (f.east(0, t) + f.east(1, t)) for t in ts}
        masks = {t: speeds[t] > 0 for t in ts}
        a, b, q0, q1 = [[f.field(c, slab, t) for t, c in spots] for slab in range(4)]
        middle = difference(q0, b)
        left = total_of(total_of(b, b), minmods(middle, difference(b, a)))
        slope = minmods(difference(q1, q0), middle)
        twice = total_of(q0, q0)
        flux = face_flux([speeds[t] for t, _ in spots], [masks[t] for t, _ in spots], left, difference(twice, slope))
        stores = [(f.fx, spot, x) for spot, x in zip(spots, flux)]
        return stores + [(f.lx, spot, x) for spot, x in zip(spots, total_of(twice, slope))]

    staged([functools.partial(job, range(t, t + PAIR)) for t in range(0, f.tiles, PAIR)])


def slab_step(f, k, put):
    slab = k + 2
    lane = lax.broadcasted_iota(jnp.int32, (8, f.lanes), 1)
    top = f.lanes - 1
    is_first, is_last = lane == 0, lane == top
    carry = []
    north_here = f.north(k, 0)
    speed = FACTOR * (f.north(k, -1) + north_here)
    for c in range(f.comps):
        a, b, q0, q1 = [f.field(c, slab, t) for t in (-2, -1, 0, 1)]
        middle, ahead = q0 - b, q1 - q0
        left_state = (b + b) + minmod(middle, b - a)
        slope = minmod(ahead, middle)
        twice = q0 + q0
        flux = speed * jnp.where(speed > 0, left_state, twice - slope)
        carry.append((q0, q1, ahead, twice, twice + slope, flux))
    states = {}

    def vertical(t):
        for c in range(f.comps):
            q0 = f.field(c, slab, t)
            over = jnp.where(is_last, 0.0, pltpu.roll(q0, top, 1))
            under = jnp.where(is_first, 0.0, pltpu.roll(q0, 1, 1))
            slope = minmod(over - q0, q0 - under)
            twice = q0 + q0
            states[t, c] = (twice - slope, twice + slope)

    held = []
    for t in range(GROUP):
        vertical(t)
    for begin in range(0, f.tiles, GROUP):
        group = range(begin, min(begin + GROUP, f.tiles))
        for t in range(begin + GROUP, min(begin + 2 * GROUP, f.tiles)):
            vertical(t)
        loaded = {}
        for t in group:
            loaded[t] = (f.east(k + 1, t), f.east(k + 2, t), f.north(k, t + 1), f.up(k, t))
            for c in range(f.comps):
                loaded[t, c] = (
                    f.field(c, slab, t + 2), f.field(c, slab + 1, t), f.field(c, slab + 2, t),
                    f.fx[t, c], f.lx[t, c],
                )
        for c, t, flux_x, left_x, value in held:
            f.fx[t, c], f.lx[t, c] = flux_x, left_x
            put(c, t, value)
        held = []
        for t in group:
            east_here, east_next, north_next, rise = loaded[t]
            speed_x = FACTOR * (east_here + east_next)
            speed_y = FACTOR * (north_here + north_next)
            north_here = north_next
            rise = FACTOR * rise
            speed_z = rise + pltpu.roll(rise, top, 1)
            fall = jnp.where(is_first, jnp.minimum(rise, 0.0), pltpu.roll(speed_z, 1, 1))
            speed_z = jnp.where(is_last, jnp.maximum(rise, 0.0), speed_z)
            go_x, go_y, go_z, go_fall = speed_x > 0, speed_y > 0, speed_z > 0, fall > 0
            for c in range(f.comps):
                y2, x1, x2, flux_w, left_w = loaded[t, c]
                q0, y1, ahead, twice, left_y, flux_y = carry[c]
                beyond = y2 - y1
                slope = minmod(beyond, ahead)
                twice_y = y1 + y1
                flux_next = speed_y * jnp.where(go_y, left_y, twice_y - slope)
                total = flux_next - flux_y
                carry[c] = (y1, y2, beyond, twice_y, twice_y + slope, flux_next)
                slope = minmod(x2 - x1, x1 - q0)
                twice_x = x1 + x1
                flux_x = speed_x * jnp.where(go_x, left_w, twice_x - slope)
                left_x = twice_x + slope
                total = total + (flux_x - flux_w)
                lower, upper = states[t, c]
                flux_z = speed_z * jnp.where(go_z, upper, pltpu.roll(lower, top, 1))
                flux_below = fall * jnp.where(go_fall, pltpu.roll(upper, 1, 1), lower)
                total = total + (flux_z - flux_below)
                held.append((c, t, flux_x, left_x, q0 - total))
    for c, t, flux_x, left_x, value in held:
        f.fx[t, c], f.lx[t, c] = flux_x, left_x
        put(c, t, value)


def rotated_edges(tiles, lows, highs):
    row = lax.broadcasted_iota(jnp.int32, tiles[0].shape, 0)
    ahead = [pltpu.roll(tile, 1, 0) for tile in tiles[-len(lows) :]]
    after = [pltpu.roll(tile, 7, 0) for tile in tiles[: len(highs)]]
    ahead = [jnp.where(row == 0, low, tile) for low, tile in zip(lows, ahead)]
    after = [jnp.where(row == 7, high, tile) for high, tile in zip(highs, after)]
    return ahead, after


def field_job(q, block, c, slab, source, dust, below, above, x):
    count = q.shape[3] - 4
    spots = range(count) if source is not None else (0, 1, count - 2, count - 1)
    if source is None:
        tiles = [q[block, c, slab, 2 + t] for t in spots]
    else:
        tiles = [tile_of(source, t, count) for t in spots]
    if below is not None:
        x = pl.ds(x, 1)
        lows = [below[2 * c + r, x, :] for r in range(2)]
        highs = [above[2 * c + r, x, :] for r in range(2)]
    if dust is not None:
        tiles = total_of(tiles, dust(spots))
    stores = []
    if source is not None:
        stores += [(q, (block, c, slab, t + 2), tile) for t, tile in zip(spots, tiles)]
    if below is not None:
        ahead, after = rotated_edges(tiles, lows, highs)
        stores += [(q, (block, c, slab, r), tile) for r, tile in enumerate(ahead)]
        stores += [(q, (block, c, slab, count + 2 + r), tile) for r, tile in enumerate(after)]
    return stores


def north_job(v, block, slab, source, below, above, x):
    count = v.shape[2] - 2
    tiles = [tile_of(source, t, count) for t in range(count)]
    x = pl.ds(x, 1)
    ahead, after = rotated_edges(tiles, [below[8, x, :]], [above[8, x, :]])
    return [(v, (block, slab, t), tile) for t, tile in enumerate(ahead + tiles + after)]


def plain_job(target, block, slab, source):
    count = target.shape[2]
    return [(target, (block, slab, t), tile_of(source, t, count)) for t in range(count)]


def falling(deposit, column, tiles):
    lanes = deposit.shape[-1]

    def dust(spots):
        parts = [pltpu.roll(tile_of(deposit, t, tiles), lanes - column, 1) for t in spots]
        lane = lax.broadcasted_iota(jnp.int32, parts[0].shape, 1)
        return [jnp.where(lane == 0, part, 0.0) for part in parts]

    return dust


def pack_edges(packs, stage_slab, comps, x):
    x = pl.ds(x, 1)
    stores = []
    for c in range(comps):
        tiles = stage_slab(c)
        count = tiles.shape[0]
        for r in range(2):
            stores.append((packs[0], (2 * c + r, x), tiles[r, 0:1, :]))
            stores.append((packs[1], (2 * c + r, x), tiles[count - 2 + r, 7:8, :]))
    staged([lambda: stores])


def start(source, target, sem):
    pltpu.make_async_copy(source, target, sem).start()


def arrived(spot, sem):
    pltpu.make_async_copy(spot, spot, sem).wait()


def interior_kernel(last, count, *refs):
    refs = list(refs)
    fields, velocity = refs[:count], refs[count]
    below, above, v_below, v_above = refs[count + 1 : count + 5]
    del refs[: count + 5]
    deposit = None if last else refs.pop(0)
    out = refs.pop(0)
    packs = None if last else (refs.pop(0), refs.pop(0))
    q, u, v, w, fx, lx, wind, stage, in_sem, out_sem = refs[:10]
    natural = None if last else refs[10]
    comps, slabs, tiles = q.shape[1], q.shape[2], w.shape[2]
    chunks = slabs // CHUNK
    inner = pl.ds(2, tiles)

    def fetch(j, first, final):
        begin, size = j * CHUNK, CHUNK
        span = pl.ds(begin, CHUNK)
        if last:
            middle, low, high = fields
            if first:
                begin, size = begin + 2, size - 2
                start(low, q.at[0, :, pl.ds(0, 2), inner], in_sem.at[j, 0])
            if final:
                size -= 2
                start(high, q.at[0, :, pl.ds(slabs - 2, 2), inner], in_sem.at[j, 0])
            part = pl.ds(begin, size)
            start(middle.at[:, part], q.at[0, :, part, inner], in_sem.at[j, 0])
        else:
            start(fields[0].at[:, span], natural.at[:, span], in_sem.at[j, 0])
        start(velocity.at[:, span], wind.at[:, span], in_sem.at[j, 1])

    for j in range(AHEAD):
        fetch(j, j == 0, False)

    def arrive(j):
        span = pl.ds(j * CHUNK, CHUNK)
        arrived(q.at[0, :, span, inner] if last else natural.at[:, span], in_sem.at[j, 0])
        arrived(wind.at[:, span], in_sem.at[j, 1])
        later = j + AHEAD

        @pl.when(later < chunks - 1)
        def _():
            fetch(later, False, False)

        @pl.when(later == chunks - 1)
        def _():
            fetch(chunks - 1, False, True)

        def complete(x, _):
            jobs = []
            for c in range(comps):
                dust = falling(deposit, x + 2, tiles) if not last and c == comps - 1 else None
                source = None if last else natural.at[c, x]
                jobs.append(functools.partial(field_job, q, 0, c, x, source, dust, below, above, x))
            jobs.append(functools.partial(plain_job, u, 0, x, wind.at[0, x]))
            jobs.append(functools.partial(north_job, v, 0, x, wind.at[1, x], v_below, v_above, x))
            jobs.append(functools.partial(plain_job, w, 0, x, wind.at[2, x]))
            staged(jobs)
            return 0

        lax.fori_loop(j * CHUNK, (j + 1) * CHUNK, complete, 0)

    f = Slabs(q, u, v, w, fx, lx, 0, 1, 2)
    arrive(jnp.int32(0))
    first_face(f)

    def step(k, _):
        @pl.when(k % CHUNK == 0)
        def _():
            arrive(k // CHUNK + 1)

        def put(c, t, value):
            if last:
                stage[c, k, pl.ds(t, 8, stride=tiles), :] = value
            else:
                stage[c, k, t] = value

        slab_step(f, k, put)
        start(stage.at[:, k], out.at[:, k + 2], out_sem)
        if not last:
            pack_edges(packs, lambda c: stage.at[c, k], comps, k + 2)
        return 0

    if not last:
        for pack in packs:
            pack[...] = jnp.zeros_like(pack)
    lax.fori_loop(0, slabs - 4, step, 0)
    pltpu.make_async_copy(stage, out.at[:, pl.ds(2, slabs - 4)], out_sem).wait()


def interior(fields, velocity, below, above, v_below, v_above, deposit=None):
    last = deposit is None
    _, slabs, rows, lanes = velocity.shape
    tiles, comps = rows // 8, fields[0].shape[0]
    operands = list(fields) + [velocity, below, above, v_below, v_above]
    specs = [ANY] * (len(fields) + 1) + [VMEM] * 4
    form = (rows, lanes) if last else (tiles, 8, lanes)
    out_shape = [jax.ShapeDtypeStruct((comps, slabs, *form), jnp.float32)]
    out_specs = [ANY]
    scratch = [
        pltpu.VMEM((1, comps, slabs, tiles + 4, 8, lanes), jnp.float32),
        pltpu.VMEM((1, slabs, tiles, 8, lanes), jnp.float32),
        pltpu.VMEM((1, slabs, tiles + 2, 8, lanes), jnp.float32),
        pltpu.VMEM((1, slabs, tiles, 8, lanes), jnp.float32),
        pltpu.VMEM((tiles, comps, 8, lanes), jnp.float32),
        pltpu.VMEM((tiles, comps, 8, lanes), jnp.float32),
        pltpu.VMEM(velocity.shape, jnp.float32),
        pltpu.VMEM((comps, slabs - 4, *form), jnp.float32),
        pltpu.SemaphoreType.DMA((slabs // CHUNK, 2)),
        pltpu.SemaphoreType.DMA,
    ]
    if not last:
        out_shape += [jax.ShapeDtypeStruct((2 * comps, slabs, lanes), jnp.float32)] * 2
        out_specs += [VMEM] * 2
        operands.append(deposit)
        specs.append(VMEM)
        scratch.append(pltpu.VMEM((comps, slabs, rows, lanes), jnp.float32))
    cells = comps * (slabs - 4) * rows * lanes
    return pl.pallas_call(
        functools.partial(interior_kernel, last, len(fields)),
        out_shape=tuple(out_shape),
        in_specs=specs,
        out_specs=tuple(out_specs),
        scratch_shapes=scratch,
        compiler_params=params(),
        cost_estimate=cost(45 * cells, 4 * (2 * cells + 3 * slabs * rows * lanes)),
        name="interior",
    )(*operands)


def boundary_kernel(last, slabs, *refs):
    refs = list(refs)
    count = 5 if last else 3
    fields, velocity, u_low, u_high = refs[:count], refs[count], refs[count + 1], refs[count + 2]
    below, above, v_below, v_above = refs[count + 3 : count + 7]
    del refs[: count + 7]
    if last:
        out = refs[1]
        del refs[:2]
    else:
        deposit, packed, ends, packs = refs[0], refs[1:3], refs[3:5], refs[5:7]
        del refs[:7]
    q, u, v, w, fx, lx, wind, stage, in_sem, out_sem = refs[:10]
    natural = None if last else refs[10]
    comps, tiles = q.shape[1], w.shape[2]
    inner = pl.ds(2, tiles)

    if last:
        middle, end_low, end_high, x_low, x_high = fields
        for block, at, source in (
            (0, 0, x_low), (0, 2, end_low), (0, 4, middle.at[:, pl.ds(2, 2)]),
            (1, 0, middle.at[:, pl.ds(slabs - 4, 2)]), (1, 2, end_high), (1, 4, x_high),
        ):
            start(source, q.at[block, :, pl.ds(at, 2), inner], in_sem.at[block, 0])
    else:
        state, x_low, x_high = fields
        start(state.at[:, pl.ds(0, 4)], natural.at[0, :, pl.ds(2, 4)], in_sem.at[0, 0])
        start(state.at[:, pl.ds(slabs - 4, 4)], natural.at[1, :, pl.ds(0, 4)], in_sem.at[1, 0])
        for c in range(comps):
            pair = pl.ds(2 * c, 2)
            start(x_low.at[pair], natural.at[0, c, pl.ds(0, 2)], in_sem.at[0, 0])
            start(x_high.at[pair], natural.at[1, c, pl.ds(4, 2)], in_sem.at[1, 0])
    edge = pl.ds(2 * comps, 1)
    start(u_low.at[edge], wind.at[0, 0, pl.ds(0, 1)], in_sem.at[0, 1])
    start(velocity.at[:, pl.ds(0, 3)], wind.at[0, :, pl.ds(1, 3)], in_sem.at[0, 2])
    start(velocity.at[:, pl.ds(slabs - 3, 3)], wind.at[1, :, pl.ds(0, 3)], in_sem.at[1, 2])
    start(u_high.at[edge], wind.at[1, 0, pl.ds(3, 1)], in_sem.at[1, 1])
    if not last:
        packs[0][...] = packed[0][...]
        packs[1][...] = packed[1][...]

    def one(block, _):
        begin = block * (slabs - 2)
        arrived(q.at[block, :, :, inner] if last else natural.at[block], in_sem.at[block, 0])
        arrived(wind.at[0, 0, pl.ds(0, 1)], in_sem.at[block, 1])
        arrived(wind.at[0, :, pl.ds(0, 3)], in_sem.at[block, 2])

        def complete(slab, _):
            jobs = []
            for c in range(comps):
                dust = falling(deposit, begin + slab, tiles) if c == comps - 1 else None
                source = natural.at[block, c, slab]
                jobs.append(functools.partial(field_job, q, block, c, slab, source, dust, None, None, None))
            staged(jobs)
            return 0

        if not last:
            lax.fori_loop(0, 6, complete, 0)

        def edges(k, _):
            x = begin + k
            jobs = [
                functools.partial(field_job, q, block, c, k + 2, None, None, below, above, x) for c in range(comps)
            ]
            jobs.append(functools.partial(north_job, v, block, k, wind.at[block, 1, k + 1], v_below, v_above, x))
            jobs.append(functools.partial(plain_job, w, block, k, wind.at[block, 2, k + 1]))
            staged(jobs)
            return 0

        lax.fori_loop(0, 2, edges, 0)
        staged([functools.partial(plain_job, u, block, k, wind.at[block, 0, k]) for k in range(4)])
        f = Slabs(q, u, v, w, fx, lx, block, 0, 0)
        first_face(f)

        def step(k, _):
            def put(c, t, value):
                if last:
                    stage[block, c, k, pl.ds(t, 8, stride=tiles), :] = value
                else:
                    stage[block, c, k, t] = value

            slab_step(f, k, put)
            if not last:
                pack_edges(packs, lambda c: stage.at[block, c, k], comps, begin + k)
            return 0

        lax.fori_loop(0, 2, step, 0)
        return 0

    lax.fori_loop(0, 2, one, 0)
    copies = []
    for block in range(2):
        target = out.at[:, pl.ds(block * (slabs - 2), 2)] if last else ends[block]
        copies.append(pltpu.make_async_copy(stage.at[block], target, out_sem.at[block]))
    for copy in copies:
        copy.start()
    for copy in copies:
        copy.wait()


def boundary(fields, velocity, u_low, u_high, below, above, v_below, v_above, *, deposit=None, packed=None, out=None):
    last = out is not None
    _, slabs, rows, lanes = velocity.shape
    tiles, comps = rows // 8, fields[0].shape[0]
    operands = list(fields) + [velocity, u_low, u_high, below, above, v_below, v_above]
    specs = [ANY] * (len(fields) + 3) + [VMEM] * 4
    form = (rows, lanes) if last else (tiles, 8, lanes)
    scratch = [
        pltpu.VMEM((2, comps, 6, tiles + 4, 8, lanes), jnp.float32),
        pltpu.VMEM((2, 4, tiles, 8, lanes), jnp.float32),
        pltpu.VMEM((2, 2, tiles + 2, 8, lanes), jnp.float32),
        pltpu.VMEM((2, 2, tiles, 8, lanes), jnp.float32),
        pltpu.VMEM((tiles, comps, 8, lanes), jnp.float32),
        pltpu.VMEM((tiles, comps, 8, lanes), jnp.float32),
        pltpu.VMEM((2, 3, 4, rows, lanes), jnp.float32),
        pltpu.VMEM((2, comps, 2, *form), jnp.float32),
        pltpu.SemaphoreType.DMA((2, 3)),
        pltpu.SemaphoreType.DMA((2,)),
    ]
    if last:
        aliases = {len(operands): 0}
        operands.append(out)
        specs.append(ANY)
        out_shape = jax.ShapeDtypeStruct(out.shape, out.dtype)
        out_specs = ANY
    else:
        aliases = {}
        operands += [deposit, *packed]
        specs += [VMEM] * 3
        out_shape = (jax.ShapeDtypeStruct((comps, 2, *form), jnp.float32),) * 2
        out_shape += (jax.ShapeDtypeStruct((2 * comps, slabs, lanes), jnp.float32),) * 2
        out_specs = (ANY, ANY, VMEM, VMEM)
        scratch.append(pltpu.VMEM((2, comps, 6, rows, lanes), jnp.float32))
    cells = comps * 4 * rows * lanes
    return pl.pallas_call(
        functools.partial(boundary_kernel, last, slabs),
        out_shape=out_shape,
        in_specs=specs,
        out_specs=out_specs,
        scratch_shapes=scratch,
        input_output_aliases=aliases,
        compiler_params=params(),
        cost_estimate=cost(50 * cells, 4 * 6 * cells),
        name="boundary",
    )(*operands)


def x_copies(state, velocity, low, high, sems):
    comps, slabs = state.shape[0], state.shape[1]
    copies = []
    for n, (target, first, edge) in enumerate(((low, 0, 0), (high, slabs - 2, slabs - 1))):
        pairs = [(state.at[c, pl.ds(first, 2)], target.at[pl.ds(2 * c, 2)]) for c in range(comps)]
        pairs.append((velocity.at[0, pl.ds(edge, 1)], target.at[pl.ds(2 * comps, 1)]))
        copies += [pltpu.make_async_copy(*pair, sems.at[n, i]) for i, pair in enumerate(pairs)]
    return copies


def as_column(row):
    count = row.shape[1]
    shape = (count, count)
    same = lax.broadcasted_iota(jnp.int32, shape, 0) == lax.broadcasted_iota(jnp.int32, shape, 1)
    return jnp.sum(jnp.where(same, row, 0.0), axis=1, keepdims=True)


def survey_kernel(
    groups, low_in, high_in, v_low, v_high, wind, threshold_in, tile_owner_in, parcel_owner_in, count_in, share_in,
    state, velocity, low, high, payload, x_low, x_high,
    gathered, threshold, tile_owner, parcel_owner, count, share, sems, small_sems,
):
    small = [
        pltpu.make_async_copy(source, target, small_sems.at[n])
        for n, (source, target) in enumerate(
            (
                (threshold_in, threshold), (tile_owner_in, tile_owner), (parcel_owner_in, parcel_owner),
                (count_in, count), (share_in, share),
            )
        )
    ]
    step, steps = pl.program_id(0), pl.num_programs(0)

    @pl.when(step == 0)
    def _():
        for copy in small + x_copies(state, velocity, x_low, x_high, sems):
            copy.start()

    comps, part, rows, lanes = low_in.shape[0], wind.shape[1], wind.shape[2], wind.shape[3]
    slabs = share.shape[1]
    for x in range(part):
        for c in range(comps):
            for r in range(2):
                low[2 * c + r, x : x + 1, :] = low_in[c, x, r : r + 1, :]
                high[2 * c + r, x : x + 1, :] = high_in[c, x, 6 + r : 7 + r, :]
        low[2 * comps, x : x + 1, :] = v_low[0, x, 0:1, :]
        high[2 * comps, x : x + 1, :] = v_high[0, x, 7:8, :]
    lane = lax.broadcasted_iota(jnp.int32, (rows, lanes), 1)
    weight = jnp.zeros((rows, lanes), jnp.float32)
    for level, value in enumerate(profile_weights):
        weight = jnp.where(lane == level, value, weight)
    total = jnp.zeros((rows, lanes), jnp.float32)
    for x in range(part):
        east, north = wind[0, x], wind[1, x]
        friction = jnp.where(lane < LEVELS, weight * (east * east + north * north), 0.0)
        total = total + pltpu.roll(friction, LEVELS * x, 1) if x else friction

    @pl.when(step == 0)
    def _():
        gathered[...] = total

    @pl.when(step == steps // 2)
    def _():
        for copy in small:
            copy.wait()
        payload[slabs : slabs + 8] = jnp.zeros((8, lanes), jnp.float32)
        payload[slabs : slabs + 1] = threshold[...]
        payload[slabs + 1 : slabs + 2, 0:slabs] = tile_owner[...].astype(jnp.float32)
        owners = parcel_owner[...].astype(jnp.float32)
        shape = (groups, slabs)
        place = (owners == lax.broadcasted_iota(jnp.int32, shape, 0).astype(jnp.float32)).astype(jnp.float32)
        live = as_column(count[...].astype(jnp.float32))
        shape = (slabs, lanes)
        reach = lax.broadcasted_iota(jnp.int32, shape, 1).astype(jnp.float32) < live
        masses = jnp.where(reach, share[0], 0.0)
        payload[slabs + 8 : slabs + 8 + groups] = jnp.dot(
            place, masses, precision=HIGHEST, preferred_element_type=jnp.float32
        )

    @pl.when(step > 0)
    def _():
        gathered[...] += pltpu.roll(total, LEVELS * part * step, 1)

    @pl.when(step == steps - 1)
    def _():
        gathered[...] = gathered[...].T
        stress = gathered[pl.ds(0, slabs, stride=LEVELS), :]
        for level in range(1, LEVELS):
            stress = stress + gathered[pl.ds(level, slabs, stride=LEVELS), :]
        payload[0:slabs] = stress
        for copy in x_copies(state, velocity, x_low, x_high, sems):
            copy.wait()


def survey(groups, state, velocity, threshold, tile_owner, parcel_owner, count, share):
    comps, slabs, rows, lanes = state.shape
    part = 8
    last = rows // 8 - 1

    small = (threshold, tile_owner, parcel_owner, count, share)
    packed = jax.ShapeDtypeStruct((2 * comps + 1, slabs, lanes), jnp.float32)
    packed_spec = pl.BlockSpec((2 * comps + 1, part, lanes), lambda i: (0, i, 0))
    x_packed = jax.ShapeDtypeStruct((2 * comps + 1, rows, lanes), jnp.float32)
    height = slabs + 8 + groups
    return pl.pallas_call(
        functools.partial(survey_kernel, groups),
        grid=(slabs // part,),
        out_shape=(packed, packed, jax.ShapeDtypeStruct((height, lanes), jnp.float32), x_packed, x_packed),
        in_specs=[
            pl.BlockSpec((comps, part, 8, lanes), lambda i: (0, i, 0, 0)),
            pl.BlockSpec((comps, part, 8, lanes), lambda i: (0, i, last, 0)),
            pl.BlockSpec((1, part, 8, lanes), lambda i: (1, i, 0, 0)),
            pl.BlockSpec((1, part, 8, lanes), lambda i: (1, i, last, 0)),
            pl.BlockSpec((2, part, rows, lanes), lambda i: (0, i, 0, 0)),
            *[pl.BlockSpec(memory_space=pltpu.HBM)] * 7,
        ],
        out_specs=(packed_spec, packed_spec, pl.BlockSpec((height, lanes), lambda i: (0, 0)), ANY, ANY),
        scratch_shapes=[
            pltpu.VMEM((rows, lanes), jnp.float32),
            *[pltpu.VMEM(array.shape, array.dtype) for array in small],
            pltpu.SemaphoreType.DMA((2, comps + 1)),
            pltpu.SemaphoreType.DMA((len(small),)),
        ],
        compiler_params=params(),
        cost_estimate=cost(10 * slabs * rows * lanes, 10 * slabs * rows * lanes),
        name="survey",
    )(state, state, velocity, velocity, velocity, *small, state, velocity)


def deposit_kernel(slabs, me, gathered, low_in, high_in, flux_out, deposit, low, high, flux, dropped):
    groups, lanes = gathered.shape[0], gathered.shape[2]
    here = me[0]
    limits = jnp.concatenate([gathered[g, slabs : slabs + 1] for g in range(groups)], axis=0)
    total = jnp.zeros((groups, lanes), jnp.float32)
    shape = (groups, slabs)
    numbers = lax.broadcasted_iota(jnp.int32, shape, 0).astype(jnp.float32)
    for g in range(groups):
        owners = gathered[g, slabs + 1 : slabs + 2, 0:slabs]
        stress = gathered[g, 0:slabs]
        named = (owners == numbers).astype(jnp.float32)
        limit = lax.dot_general(
            named, limits, (((0,), (0,)), ((), ())), precision=HIGHEST, preferred_element_type=jnp.float32
        )
        lifting = jnp.maximum(stress - limit, 0.0)
        total = total + jnp.dot(named, lifting, precision=HIGHEST, preferred_element_type=jnp.float32)
    flux[...] = total / slabs
    flux_out[...] = flux[pl.ds(here, 1), :]
    dropped[...] = jnp.zeros_like(dropped)
    before, after = jnp.maximum(here - 1, 0), jnp.minimum(here + 1, groups - 1)
    has_before, has_after = here > 0, here < groups - 1
    base = slabs + 8
    for p in range(groups):
        x = p % slabs
        row = flux[p : p + 1, :]
        dropped[x + 2 : x + 3] += row * gathered[p, pl.ds(base + here, 1), :]
        if x >= slabs - 2:
            mass = row * gathered[p, pl.ds(base + before, 1), :]
            dropped[x - slabs + 2 : x - slabs + 3] += jnp.where(has_before, mass, 0.0)
        if x < 2:
            mass = row * gathered[p, pl.ds(base + after, 1), :]
            dropped[x + slabs + 2 : x + slabs + 3] += jnp.where(has_after, mass, 0.0)
    deposit[...] = dropped[...].T
    own = dropped[2 : 2 + slabs, :]
    lane = lax.broadcasted_iota(jnp.int32, (slabs, lanes), 1)
    rows = lanes
    dust = low.shape[0] - 3
    low[...] = low_in[...]
    high[...] = high_in[...]
    for r in range(2):
        low[dust + r] += jnp.where(lane == 0, own[:, r : r + 1], 0.0)
        high[dust + r] += jnp.where(lane == 0, own[:, rows - 2 + r : rows - 1 + r], 0.0)


def settle(me, gathered, low, high, slabs):
    groups, _, lanes = gathered.shape
    edge = jax.ShapeDtypeStruct(low.shape, jnp.float32)
    return pl.pallas_call(
        functools.partial(deposit_kernel, slabs),
        out_shape=(
            jax.ShapeDtypeStruct((1, lanes), jnp.float32),
            jax.ShapeDtypeStruct((lanes, lanes), jnp.float32),
            edge,
            edge,
        ),
        in_specs=[SMEM, VMEM, VMEM, VMEM],
        out_specs=(VMEM, VMEM, VMEM, VMEM),
        scratch_shapes=[
            pltpu.VMEM((groups, lanes), jnp.float32),
            pltpu.VMEM((lanes, lanes), jnp.float32),
        ],
        compiler_params=params(),
        cost_estimate=cost(10**6, 10**6),
        name="settle",
    )(me, gathered, low, high)


def exchange(low, high, axis):
    count = lax.axis_size(axis)
    forward = [(i, i + 1) for i in range(count - 1)]
    backward = [(target, source) for source, target in forward]
    return lax.ppermute(high, axis, forward), lax.ppermute(low, axis, backward)


def shards(state, velocity, threshold, tile_owner, parcel_owner, parcel_count, parcel_share):
    groups = lax.axis_size("gx")
    slabs = state.shape[1]
    me = lax.axis_index("gx").astype(jnp.int32).reshape(1)

    low, high, payload, x_low, x_high = survey(
        groups, state, velocity, threshold, tile_owner[:, :, 0], parcel_owner[:, :, 0], parcel_count, parcel_share
    )
    copies = jnp.broadcast_to(payload[None], (groups, *payload.shape))
    gathered = lax.all_to_all(copies, "gx", split_axis=0, concat_axis=0, tiled=True)
    flux, deposit, low, high = settle(me, gathered, low, high, slabs)
    below, above = exchange(low, high, "gy")
    x_low, x_high, _ = lax.optimization_barrier((x_low, x_high, gathered))
    x_low, x_high = exchange(x_low, x_high, "gx")
    middle, pack_low, pack_high = interior([state], velocity, below, above, below, above, deposit)
    end_low, end_high, y_low, y_high = boundary(
        [state, x_low, x_high], velocity, x_low, x_high, below, above, below, above,
        deposit=deposit, packed=(pack_low, pack_high),
    )
    x2_low, x2_high = exchange(end_low, end_high, "gx")
    below2, above2 = exchange(y_low, y_high, "gy")
    (inside,) = interior([middle, end_low, end_high], velocity, below2, above2, below, above)
    fields = boundary(
        [middle, end_low, end_high, x2_low, x2_high], velocity, x_low, x_high, below2, above2, below, above,
        out=inside,
    )
    return fields, flux


def solution(mesh):
    return jax.shard_map(
        shards,
        mesh=mesh,
        in_specs=(
            P(None, "gx", "gy", None),
            P(None, "gx", "gy", None),
            P("gx", "gy"),
            P("gy", "gx", None),
            P("gy", "gx", None),
            P("gy", "gx"),
            P("gy", "gx", None),
        ),
        out_specs=(P(None, "gx", "gy", None), P("gx", "gy")),
        check_vma=False,
    )
```

```python
import functools

import jax
import jax.numpy as jnp
from jax import lax
from jax.experimental import pallas as pl
from jax.experimental.pallas import tpu as pltpu
from jax.sharding import PartitionSpec as P

LEVELS = 4
profile_weights = (0.4, 0.3, 0.2, 0.1)
time_step = 0.1
FACTOR = 0.25 * time_step

VMEM_LIMIT = 48 * 1024 * 1024
PAIR = 2
GROUP = 8
CHUNK = 4
AHEAD = 3
HIGHEST = lax.Precision.HIGHEST
ANY = pl.BlockSpec(memory_space=pl.ANY)
VMEM = pl.BlockSpec(memory_space=pltpu.VMEM)
SMEM = pl.BlockSpec(memory_space=pltpu.SMEM)


def params():
    return pltpu.CompilerParams(vmem_limit_bytes=VMEM_LIMIT)


def cost(flops, moved):
    return pl.CostEstimate(flops=int(flops), bytes_accessed=int(moved), transcendentals=0)


def minmod(a, b):
    return jnp.maximum(jnp.minimum(a, b), jnp.minimum(jnp.maximum(a, b), 0.0))


def picked_minmod(a, b):
    smaller = jnp.where(jnp.abs(a) < jnp.abs(b), a, b)
    return jnp.where(a * b > 0, smaller, 0.0)


def tile_of(ref, t, tiles):
    return ref[pl.ds(t, 8, stride=tiles), :]


class Slabs:
    def __init__(self, q, u, v, w, fx, lx, block, u_at, v_at):
        self.q, self.u, self.v, self.w, self.fx, self.lx = q, u, v, w, fx, lx
        self.block, self.u_at, self.v_at = block, u_at, v_at
        self.comps, self.tiles, self.lanes = q.shape[1], w.shape[2], q.shape[-1]

    def field(self, c, slab, t):
        return self.q[self.block, c, slab, t + 2]

    def east(self, slab, t):
        return self.u[self.block, slab + self.u_at, t]

    def north(self, slab, t):
        return self.v[self.block, slab + self.v_at, t + 1]

    def up(self, slab, t):
        return self.w[self.block, slab + self.v_at, t]


def each(function, *lists):
    return [function(*items) for items in zip(*lists)]


def minmods(a, b):
    low, high = each(jnp.minimum, a, b), each(jnp.maximum, a, b)
    high = each(lambda x: jnp.minimum(x, 0.0), high)
    return each(jnp.maximum, low, high)


def difference(a, b):
    return each(lambda x, y: x - y, a, b)


def total_of(a, b):
    return each(lambda x, y: x + y, a, b)


def face_flux(speeds, masks, low_side, high_side):
    picked = each(jnp.where, masks, low_side, high_side)
    return each(lambda x, y: x * y, speeds, picked)


def staged(jobs):
    waiting = []
    for job in jobs:
        stores = job()
        for ref, index, value in waiting:
            ref[index] = value
        waiting = stores
    for ref, index, value in waiting:
        ref[index] = value


def first_face(f):
    def job(ts):
        spots = [(t, c) for t in ts for c in range(f.comps)]
        speeds = {t: FACTOR * (f.east(0, t) + f.east(1, t)) for t in ts}
        masks = {t: speeds[t] > 0 for t in ts}
        a, b, q0, q1 = [[f.field(c, slab, t) for t, c in spots] for slab in range(4)]
        middle = difference(q0, b)
        left = total_of(total_of(b, b), minmods(middle, difference(b, a)))
        slope = minmods(difference(q1, q0), middle)
        twice = total_of(q0, q0)
        flux = face_flux([speeds[t] for t, _ in spots], [masks[t] for t, _ in spots], left, difference(twice, slope))
        stores = [(f.fx, spot, x) for spot, x in zip(spots, flux)]
        return stores + [(f.lx, spot, x) for spot, x in zip(spots, total_of(twice, slope))]

    staged([functools.partial(job, range(t, t + PAIR)) for t in range(0, f.tiles, PAIR)])


def z_shifts(lanes):
    shape = (2 * lanes, 2 * lanes)
    row, column = (lax.broadcasted_iota(jnp.int32, shape, axis) for axis in range(2))
    row = jnp.where(row >= lanes, row - lanes, row)
    later = jnp.where(column >= lanes, 0, 1)
    column = jnp.where(column >= lanes, column - lanes, column)
    plus, minus = row == column + later, row == column + later - 1
    return (jnp.where(plus, 1.0, 0.0) - jnp.where(minus, 1.0, 0.0)).astype(jnp.bfloat16)


def slab_step(f, k, put, minmod=minmod, shifts=None):
    slab = k + 2
    lane = lax.broadcasted_iota(jnp.int32, (8, f.lanes), 1)
    top = f.lanes - 1
    is_first, is_last = lane == 0, lane == top
    carry = []
    north_here = f.north(k, 0)
    speed = FACTOR * (f.north(k, -1) + north_here)
    for c in range(f.comps):
        a, b, q0, q1 = [f.field(c, slab, t) for t in (-2, -1, 0, 1)]
        middle, ahead = q0 - b, q1 - q0
        left_state = (b + b) + minmod(middle, b - a)
        slope = minmod(ahead, middle)
        twice = q0 + q0
        flux = speed * jnp.where(speed > 0, left_state, twice - slope)
        carry.append((q0, q1, ahead, twice, twice + slope, flux))
    states = {}

    def vertical_by_product(ts):
        spots = [(t, c) for t in ts for c in range(f.comps)]
        tiles = [f.field(c, slab, t) for t, c in spots]
        here = jnp.concatenate(tiles, axis=0)
        high = here.astype(jnp.bfloat16)
        rest = (here - high.astype(jnp.float32)).astype(jnp.bfloat16)
        both = jnp.concatenate([high, rest], axis=1)
        change = jnp.dot(both, shifts, preferred_element_type=jnp.float32)
        for n, (spot, q0) in enumerate(zip(spots, tiles)):
            part = slice(8 * n, 8 * n + 8)
            slope = minmod(change[part, : f.lanes], change[part, f.lanes :])
            twice = q0 + q0
            states[spot] = (twice - slope, twice + slope)

    def vertical(t):
        if shifts is not None:
            if t % GROUP == 0:
                vertical_by_product(range(t, t + GROUP))
            return
        for c in range(f.comps):
            q0 = f.field(c, slab, t)
            over = jnp.where(is_last, 0.0, pltpu.roll(q0, top, 1))
            under = jnp.where(is_first, 0.0, pltpu.roll(q0, 1, 1))
            slope = minmod(over - q0, q0 - under)
            twice = q0 + q0
            states[t, c] = (twice - slope, twice + slope)

    held = []
    for t in range(GROUP):
        vertical(t)
    for begin in range(0, f.tiles, GROUP):
        group = range(begin, min(begin + GROUP, f.tiles))
        for t in range(begin + GROUP, min(begin + 2 * GROUP, f.tiles)):
            vertical(t)
        loaded = {}
        for t in group:
            loaded[t] = (f.east(k + 1, t), f.east(k + 2, t), f.north(k, t + 1), f.up(k, t))
            for c in range(f.comps):
                loaded[t, c] = (
                    f.field(c, slab, t + 2), f.field(c, slab + 1, t), f.field(c, slab + 2, t),
                    f.fx[t, c], f.lx[t, c],
                )
        for c, t, flux_x, left_x, value in held:
            f.fx[t, c], f.lx[t, c] = flux_x, left_x
            put(c, t, value)
        held = []
        for t in group:
            east_here, east_next, north_next, rise = loaded[t]
            speed_x = FACTOR * (east_here + east_next)
            speed_y = FACTOR * (north_here + north_next)
            north_here = north_next
            rise = FACTOR * rise
            speed_z = rise + pltpu.roll(rise, top, 1)
            fall = jnp.where(is_first, jnp.minimum(rise, 0.0), pltpu.roll(speed_z, 1, 1))
            speed_z = jnp.where(is_last, jnp.maximum(rise, 0.0), speed_z)
            go_x, go_y, go_z, go_fall = speed_x > 0, speed_y > 0, speed_z > 0, fall > 0
            for c in range(f.comps):
                y2, x1, x2, flux_w, left_w = loaded[t, c]
                q0, y1, ahead, twice, left_y, flux_y = carry[c]
                beyond = y2 - y1
                slope = minmod(beyond, ahead)
                twice_y = y1 + y1
                flux_next = speed_y * jnp.where(go_y, left_y, twice_y - slope)
                total = flux_next - flux_y
                carry[c] = (y1, y2, beyond, twice_y, twice_y + slope, flux_next)
                slope = minmod(x2 - x1, x1 - q0)
                twice_x = x1 + x1
                flux_x = speed_x * jnp.where(go_x, left_w, twice_x - slope)
                left_x = twice_x + slope
                total = total + (flux_x - flux_w)
                lower, upper = states[t, c]
                flux_z = speed_z * jnp.where(go_z, upper, pltpu.roll(lower, top, 1))
                flux_below = fall * jnp.where(go_fall, pltpu.roll(upper, 1, 1), lower)
                total = total + (flux_z - flux_below)
                held.append((c, t, flux_x, left_x, q0 - total))
    for c, t, flux_x, left_x, value in held:
        f.fx[t, c], f.lx[t, c] = flux_x, left_x
        put(c, t, value)


def rotated_edges(tiles, lows, highs):
    row = lax.broadcasted_iota(jnp.int32, tiles[0].shape, 0)
    ahead = [pltpu.roll(tile, 1, 0) for tile in tiles[-len(lows) :]]
    after = [pltpu.roll(tile, 7, 0) for tile in tiles[: len(highs)]]
    ahead = [jnp.where(row == 0, low, tile) for low, tile in zip(lows, ahead)]
    after = [jnp.where(row == 7, high, tile) for high, tile in zip(highs, after)]
    return ahead, after


def field_job(q, block, c, slab, source, dust, below, above, x):
    count = q.shape[3] - 4
    spots = range(count) if source is not None else (0, 1, count - 2, count - 1)
    if source is None:
        tiles = [q[block, c, slab, 2 + t] for t in spots]
    else:
        tiles = [tile_of(source, t, count) for t in spots]
    if below is not None:
        x = pl.ds(x, 1)
        lows = [below[2 * c + r, x, :] for r in range(2)]
        highs = [above[2 * c + r, x, :] for r in range(2)]
    if dust is not None:
        tiles = total_of(tiles, dust(spots))
    stores = []
    if source is not None:
        stores += [(q, (block, c, slab, t + 2), tile) for t, tile in zip(spots, tiles)]
    if below is not None:
        ahead, after = rotated_edges(tiles, lows, highs)
        stores += [(q, (block, c, slab, r), tile) for r, tile in enumerate(ahead)]
        stores += [(q, (block, c, slab, count + 2 + r), tile) for r, tile in enumerate(after)]
    return stores


def north_job(v, block, slab, source, below, above, x):
    count = v.shape[2] - 2
    tiles = [tile_of(source, t, count) for t in range(count)]
    x = pl.ds(x, 1)
    ahead, after = rotated_edges(tiles, [below[8, x, :]], [above[8, x, :]])
    return [(v, (block, slab, t), tile) for t, tile in enumerate(ahead + tiles + after)]


def plain_job(target, block, slab, source):
    count = target.shape[2]
    return [(target, (block, slab, t), tile_of(source, t, count)) for t in range(count)]


def falling(deposit, column, tiles):
    lanes = deposit.shape[-1]

    def dust(spots):
        parts = [pltpu.roll(tile_of(deposit, t, tiles), lanes - column, 1) for t in spots]
        lane = lax.broadcasted_iota(jnp.int32, parts[0].shape, 1)
        return [jnp.where(lane == 0, part, 0.0) for part in parts]

    return dust


def pack_edges(packs, stage_slab, comps, x):
    x = pl.ds(x, 1)
    stores = []
    for c in range(comps):
        tiles = stage_slab(c)
        count = tiles.shape[0]
        for r in range(2):
            stores.append((packs[0], (2 * c + r, x), tiles[r, 0:1, :]))
            stores.append((packs[1], (2 * c + r, x), tiles[count - 2 + r, 7:8, :]))
    staged([lambda: stores])


def start(source, target, sem):
    pltpu.make_async_copy(source, target, sem).start()


def arrived(spot, sem):
    pltpu.make_async_copy(spot, spot, sem).wait()


def interior_kernel(last, count, *refs):
    refs = list(refs)
    fields, velocity = refs[:count], refs[count]
    below, above, v_below, v_above = refs[count + 1 : count + 5]
    del refs[: count + 5]
    deposit = None if last else refs.pop(0)
    out = refs.pop(0)
    packs = None if last else (refs.pop(0), refs.pop(0))
    q, u, v, w, fx, lx, wind, stage, in_sem, out_sem = refs[:10]
    natural = None if last else refs[10]
    if last:
        shifts = refs[10]
        shifts[...] = z_shifts(q.shape[-1])
    comps, slabs, tiles = q.shape[1], q.shape[2], w.shape[2]
    chunks = slabs // CHUNK
    inner = pl.ds(2, tiles)

    def fetch(j, first, final):
        begin, size = j * CHUNK, CHUNK
        span = pl.ds(begin, CHUNK)
        if last:
            middle, low, high = fields
            if first:
                begin, size = begin + 2, size - 2
                start(low, q.at[0, :, pl.ds(0, 2), inner], in_sem.at[j, 0])
            if final:
                size -= 2
                start(high, q.at[0, :, pl.ds(slabs - 2, 2), inner], in_sem.at[j, 0])
            part = pl.ds(begin, size)
            start(middle.at[:, part], q.at[0, :, part, inner], in_sem.at[j, 0])
        else:
            start(fields[0].at[:, span], natural.at[:, span], in_sem.at[j, 0])
        start(velocity.at[:, span], wind.at[:, span], in_sem.at[j, 1])

    for j in range(AHEAD):
        fetch(j, j == 0, False)

    def arrive(j):
        span = pl.ds(j * CHUNK, CHUNK)
        arrived(q.at[0, :, span, inner] if last else natural.at[:, span], in_sem.at[j, 0])
        arrived(wind.at[:, span], in_sem.at[j, 1])
        later = j + AHEAD

        @pl.when(later < chunks - 1)
        def _():
            fetch(later, False, False)

        @pl.when(later == chunks - 1)
        def _():
            fetch(chunks - 1, False, True)

        def complete(x, _):
            jobs = []
            for c in range(comps):
                dust = falling(deposit, x + 2, tiles) if not last and c == comps - 1 else None
                source = None if last else natural.at[c, x]
                jobs.append(functools.partial(field_job, q, 0, c, x, source, dust, below, above, x))
            jobs.append(functools.partial(plain_job, u, 0, x, wind.at[0, x]))
            jobs.append(functools.partial(north_job, v, 0, x, wind.at[1, x], v_below, v_above, x))
            jobs.append(functools.partial(plain_job, w, 0, x, wind.at[2, x]))
            staged(jobs)
            return 0

        lax.fori_loop(j * CHUNK, (j + 1) * CHUNK, complete, 0)

    f = Slabs(q, u, v, w, fx, lx, 0, 1, 2)
    arrive(jnp.int32(0))
    first_face(f)

    def step(k, _):
        @pl.when(k % CHUNK == 0)
        def _():
            arrive(k // CHUNK + 1)

        def put(c, t, value):
            if last:
                stage[c, k, pl.ds(t, 8, stride=tiles), :] = value
            else:
                stage[c, k, t] = value

        slab_step(f, k, put, minmod if last else picked_minmod, shifts[...] if last else None)
        start(stage.at[:, k], out.at[:, k + 2], out_sem)
        if not last:
            pack_edges(packs, lambda c: stage.at[c, k], comps, k + 2)
        return 0

    if not last:
        for pack in packs:
            pack[...] = jnp.zeros_like(pack)
    lax.fori_loop(0, slabs - 4, step, 0)
    pltpu.make_async_copy(stage, out.at[:, pl.ds(2, slabs - 4)], out_sem).wait()


def interior(fields, velocity, below, above, v_below, v_above, deposit=None):
    last = deposit is None
    _, slabs, rows, lanes = velocity.shape
    tiles, comps = rows // 8, fields[0].shape[0]
    operands = list(fields) + [velocity, below, above, v_below, v_above]
    specs = [ANY] * (len(fields) + 1) + [VMEM] * 4
    form = (rows, lanes) if last else (tiles, 8, lanes)
    out_shape = [jax.ShapeDtypeStruct((comps, slabs, *form), jnp.float32)]
    out_specs = [ANY]
    scratch = [
        pltpu.VMEM((1, comps, slabs, tiles + 4, 8, lanes), jnp.float32),
        pltpu.VMEM((1, slabs, tiles, 8, lanes), jnp.float32),
        pltpu.VMEM((1, slabs, tiles + 2, 8, lanes), jnp.float32),
        pltpu.VMEM((1, slabs, tiles, 8, lanes), jnp.float32),
        pltpu.VMEM((tiles, comps, 8, lanes), jnp.float32),
        pltpu.VMEM((tiles, comps, 8, lanes), jnp.float32),
        pltpu.VMEM(velocity.shape, jnp.float32),
        pltpu.VMEM((comps, slabs - 4, *form), jnp.float32),
        pltpu.SemaphoreType.DMA((slabs // CHUNK, 2)),
        pltpu.SemaphoreType.DMA,
    ]
    if last:
        scratch.append(pltpu.VMEM((2 * lanes, 2 * lanes), jnp.bfloat16))
    else:
        out_shape += [jax.ShapeDtypeStruct((2 * comps, slabs, lanes), jnp.float32)] * 2
        out_specs += [VMEM] * 2
        operands.append(deposit)
        specs.append(VMEM)
        scratch.append(pltpu.VMEM((comps, slabs, rows, lanes), jnp.float32))
    cells = comps * (slabs - 4) * rows * lanes
    return pl.pallas_call(
        functools.partial(interior_kernel, last, len(fields)),
        out_shape=tuple(out_shape),
        in_specs=specs,
        out_specs=tuple(out_specs),
        scratch_shapes=scratch,
        compiler_params=params(),
        cost_estimate=cost(45 * cells, 4 * (2 * cells + 3 * slabs * rows * lanes)),
        name="interior",
    )(*operands)


def boundary_kernel(last, slabs, *refs):
    refs = list(refs)
    count = 5 if last else 3
    fields, velocity, u_low, u_high = refs[:count], refs[count], refs[count + 1], refs[count + 2]
    below, above, v_below, v_above = refs[count + 3 : count + 7]
    del refs[: count + 7]
    if last:
        out = refs[1]
        del refs[:2]
    else:
        deposit, packed, ends, packs = refs[0], refs[1:3], refs[3:5], refs[5:7]
        del refs[:7]
    q, u, v, w, fx, lx, wind, stage, in_sem, out_sem = refs[:10]
    natural = None if last else refs[10]
    comps, tiles = q.shape[1], w.shape[2]
    inner = pl.ds(2, tiles)

    if last:
        middle, end_low, end_high, x_low, x_high = fields
        for block, at, source in (
            (0, 0, x_low), (0, 2, end_low), (0, 4, middle.at[:, pl.ds(2, 2)]),
            (1, 0, middle.at[:, pl.ds(slabs - 4, 2)]), (1, 2, end_high), (1, 4, x_high),
        ):
            start(source, q.at[block, :, pl.ds(at, 2), inner], in_sem.at[block, 0])
    else:
        state, x_low, x_high = fields
        start(state.at[:, pl.ds(0, 4)], natural.at[0, :, pl.ds(2, 4)], in_sem.at[0, 0])
        start(state.at[:, pl.ds(slabs - 4, 4)], natural.at[1, :, pl.ds(0, 4)], in_sem.at[1, 0])
        for c in range(comps):
            pair = pl.ds(2 * c, 2)
            start(x_low.at[pair], natural.at[0, c, pl.ds(0, 2)], in_sem.at[0, 0])
            start(x_high.at[pair], natural.at[1, c, pl.ds(4, 2)], in_sem.at[1, 0])
    edge = pl.ds(2 * comps, 1)
    start(u_low.at[edge], wind.at[0, 0, pl.ds(0, 1)], in_sem.at[0, 1])
    start(velocity.at[:, pl.ds(0, 3)], wind.at[0, :, pl.ds(1, 3)], in_sem.at[0, 2])
    start(velocity.at[:, pl.ds(slabs - 3, 3)], wind.at[1, :, pl.ds(0, 3)], in_sem.at[1, 2])
    start(u_high.at[edge], wind.at[1, 0, pl.ds(3, 1)], in_sem.at[1, 1])
    if not last:
        packs[0][...] = packed[0][...]
        packs[1][...] = packed[1][...]

    def one(block, _):
        begin = block * (slabs - 2)
        arrived(q.at[block, :, :, inner] if last else natural.at[block], in_sem.at[block, 0])
        arrived(wind.at[0, 0, pl.ds(0, 1)], in_sem.at[block, 1])
        arrived(wind.at[0, :, pl.ds(0, 3)], in_sem.at[block, 2])

        def complete(slab, _):
            jobs = []
            for c in range(comps):
                dust = falling(deposit, begin + slab, tiles) if c == comps - 1 else None
                source = natural.at[block, c, slab]
                jobs.append(functools.partial(field_job, q, block, c, slab, source, dust, None, None, None))
            staged(jobs)
            return 0

        if not last:
            lax.fori_loop(0, 6, complete, 0)

        def edges(k, _):
            x = begin + k
            jobs = [
                functools.partial(field_job, q, block, c, k + 2, None, None, below, above, x) for c in range(comps)
            ]
            jobs.append(functools.partial(north_job, v, block, k, wind.at[block, 1, k + 1], v_below, v_above, x))
            jobs.append(functools.partial(plain_job, w, block, k, wind.at[block, 2, k + 1]))
            staged(jobs)
            return 0

        lax.fori_loop(0, 2, edges, 0)
        staged([functools.partial(plain_job, u, block, k, wind.at[block, 0, k]) for k in range(4)])
        f = Slabs(q, u, v, w, fx, lx, block, 0, 0)
        first_face(f)

        def step(k, _):
            def put(c, t, value):
                if last:
                    stage[block, c, k, pl.ds(t, 8, stride=tiles), :] = value
                else:
                    stage[block, c, k, t] = value

            slab_step(f, k, put)
            if not last:
                pack_edges(packs, lambda c: stage.at[block, c, k], comps, begin + k)
            return 0

        lax.fori_loop(0, 2, step, 0)
        return 0

    lax.fori_loop(0, 2, one, 0)
    copies = []
    for block in range(2):
        target = out.at[:, pl.ds(block * (slabs - 2), 2)] if last else ends[block]
        copies.append(pltpu.make_async_copy(stage.at[block], target, out_sem.at[block]))
    for copy in copies:
        copy.start()
    for copy in copies:
        copy.wait()


def boundary(fields, velocity, u_low, u_high, below, above, v_below, v_above, *, deposit=None, packed=None, out=None):
    last = out is not None
    _, slabs, rows, lanes = velocity.shape
    tiles, comps = rows // 8, fields[0].shape[0]
    operands = list(fields) + [velocity, u_low, u_high, below, above, v_below, v_above]
    specs = [ANY] * (len(fields) + 3) + [VMEM] * 4
    form = (rows, lanes) if last else (tiles, 8, lanes)
    scratch = [
        pltpu.VMEM((2, comps, 6, tiles + 4, 8, lanes), jnp.float32),
        pltpu.VMEM((2, 4, tiles, 8, lanes), jnp.float32),
        pltpu.VMEM((2, 2, tiles + 2, 8, lanes), jnp.float32),
        pltpu.VMEM((2, 2, tiles, 8, lanes), jnp.float32),
        pltpu.VMEM((tiles, comps, 8, lanes), jnp.float32),
        pltpu.VMEM((tiles, comps, 8, lanes), jnp.float32),
        pltpu.VMEM((2, 3, 4, rows, lanes), jnp.float32),
        pltpu.VMEM((2, comps, 2, *form), jnp.float32),
        pltpu.SemaphoreType.DMA((2, 3)),
        pltpu.SemaphoreType.DMA((2,)),
    ]
    if last:
        aliases = {len(operands): 0}
        operands.append(out)
        specs.append(ANY)
        out_shape = jax.ShapeDtypeStruct(out.shape, out.dtype)
        out_specs = ANY
    else:
        aliases = {}
        operands += [deposit, *packed]
        specs += [VMEM] * 3
        out_shape = (jax.ShapeDtypeStruct((comps, 2, *form), jnp.float32),) * 2
        out_shape += (jax.ShapeDtypeStruct((2 * comps, slabs, lanes), jnp.float32),) * 2
        out_specs = (ANY, ANY, VMEM, VMEM)
        scratch.append(pltpu.VMEM((2, comps, 6, rows, lanes), jnp.float32))
    cells = comps * 4 * rows * lanes
    return pl.pallas_call(
        functools.partial(boundary_kernel, last, slabs),
        out_shape=out_shape,
        in_specs=specs,
        out_specs=out_specs,
        scratch_shapes=scratch,
        input_output_aliases=aliases,
        compiler_params=params(),
        cost_estimate=cost(50 * cells, 4 * 6 * cells),
        name="boundary",
    )(*operands)


def x_copies(state, velocity, low, high, sems):
    comps, slabs = state.shape[0], state.shape[1]
    copies = []
    for n, (target, first, edge) in enumerate(((low, 0, 0), (high, slabs - 2, slabs - 1))):
        pairs = [(state.at[c, pl.ds(first, 2)], target.at[pl.ds(2 * c, 2)]) for c in range(comps)]
        pairs.append((velocity.at[0, pl.ds(edge, 1)], target.at[pl.ds(2 * comps, 1)]))
        copies += [pltpu.make_async_copy(*pair, sems.at[n, i]) for i, pair in enumerate(pairs)]
    return copies


def as_column(row):
    count = row.shape[1]
    shape = (count, count)
    same = lax.broadcasted_iota(jnp.int32, shape, 0) == lax.broadcasted_iota(jnp.int32, shape, 1)
    return jnp.sum(jnp.where(same, row, 0.0), axis=1, keepdims=True)


def survey_kernel(
    groups, low_in, high_in, v_low, v_high, wind, threshold_in, tile_owner_in, parcel_owner_in, count_in, share_in,
    state, velocity, low, high, payload, x_low, x_high,
    gathered, threshold, tile_owner, parcel_owner, count, share, sems, small_sems,
):
    small = [
        pltpu.make_async_copy(source, target, small_sems.at[n])
        for n, (source, target) in enumerate(
            (
                (threshold_in, threshold), (tile_owner_in, tile_owner), (parcel_owner_in, parcel_owner),
                (count_in, count), (share_in, share),
            )
        )
    ]
    step, steps = pl.program_id(0), pl.num_programs(0)

    @pl.when(step == 0)
    def _():
        for copy in small + x_copies(state, velocity, x_low, x_high, sems):
            copy.start()

    comps, part, rows, lanes = low_in.shape[0], wind.shape[1], wind.shape[2], wind.shape[3]
    slabs = share.shape[1]
    for x in range(part):
        for c in range(comps):
            for r in range(2):
                low[2 * c + r, x : x + 1, :] = low_in[c, x, r : r + 1, :]
                high[2 * c + r, x : x + 1, :] = high_in[c, x, 6 + r : 7 + r, :]
        low[2 * comps, x : x + 1, :] = v_low[0, x, 0:1, :]
        high[2 * comps, x : x + 1, :] = v_high[0, x, 7:8, :]
    lane = lax.broadcasted_iota(jnp.int32, (rows, lanes), 1)
    weight = jnp.zeros((rows, lanes), jnp.float32)
    for level, value in enumerate(profile_weights):
        weight = jnp.where(lane == level, value, weight)
    total = jnp.zeros((rows, lanes), jnp.float32)
    for x in range(part):
        east, north = wind[0, x], wind[1, x]
        friction = jnp.where(lane < LEVELS, weight * (east * east + north * north), 0.0)
        total = total + pltpu.roll(friction, LEVELS * x, 1) if x else friction

    @pl.when(step == 0)
    def _():
        gathered[...] = total

    @pl.when(step == steps // 2)
    def _():
        for copy in small:
            copy.wait()
        payload[slabs : slabs + 8] = jnp.zeros((8, lanes), jnp.float32)
        payload[slabs : slabs + 1] = threshold[...]
        payload[slabs + 1 : slabs + 2, 0:slabs] = tile_owner[...].astype(jnp.float32)
        owners = parcel_owner[...].astype(jnp.float32)
        shape = (groups, slabs)
        place = (owners == lax.broadcasted_iota(jnp.int32, shape, 0).astype(jnp.float32)).astype(jnp.float32)
        live = as_column(count[...].astype(jnp.float32))
        shape = (slabs, lanes)
        reach = lax.broadcasted_iota(jnp.int32, shape, 1).astype(jnp.float32) < live
        masses = jnp.where(reach, share[0], 0.0)
        payload[slabs + 8 : slabs + 8 + groups] = jnp.dot(
            place, masses, precision=HIGHEST, preferred_element_type=jnp.float32
        )

    @pl.when(step > 0)
    def _():
        gathered[...] += pltpu.roll(total, LEVELS * part * step, 1)

    @pl.when(step == steps - 1)
    def _():
        gathered[...] = gathered[...].T
        stress = gathered[pl.ds(0, slabs, stride=LEVELS), :]
        for level in range(1, LEVELS):
            stress = stress + gathered[pl.ds(level, slabs, stride=LEVELS), :]
        payload[0:slabs] = stress
        for copy in x_copies(state, velocity, x_low, x_high, sems):
            copy.wait()


def survey(groups, state, velocity, threshold, tile_owner, parcel_owner, count, share):
    comps, slabs, rows, lanes = state.shape
    part = 8
    last = rows // 8 - 1

    small = (threshold, tile_owner, parcel_owner, count, share)
    packed = jax.ShapeDtypeStruct((2 * comps + 1, slabs, lanes), jnp.float32)
    packed_spec = pl.BlockSpec((2 * comps + 1, part, lanes), lambda i: (0, i, 0))
    x_packed = jax.ShapeDtypeStruct((2 * comps + 1, rows, lanes), jnp.float32)
    height = slabs + 8 + groups
    return pl.pallas_call(
        functools.partial(survey_kernel, groups),
        grid=(slabs // part,),
        out_shape=(packed, packed, jax.ShapeDtypeStruct((height, lanes), jnp.float32), x_packed, x_packed),
        in_specs=[
            pl.BlockSpec((comps, part, 8, lanes), lambda i: (0, i, 0, 0)),
            pl.BlockSpec((comps, part, 8, lanes), lambda i: (0, i, last, 0)),
            pl.BlockSpec((1, part, 8, lanes), lambda i: (1, i, 0, 0)),
            pl.BlockSpec((1, part, 8, lanes), lambda i: (1, i, last, 0)),
            pl.BlockSpec((2, part, rows, lanes), lambda i: (0, i, 0, 0)),
            *[pl.BlockSpec(memory_space=pltpu.HBM)] * 7,
        ],
        out_specs=(packed_spec, packed_spec, pl.BlockSpec((height, lanes), lambda i: (0, 0)), ANY, ANY),
        scratch_shapes=[
            pltpu.VMEM((rows, lanes), jnp.float32),
            *[pltpu.VMEM(array.shape, array.dtype) for array in small],
            pltpu.SemaphoreType.DMA((2, comps + 1)),
            pltpu.SemaphoreType.DMA((len(small),)),
        ],
        compiler_params=params(),
        cost_estimate=cost(10 * slabs * rows * lanes, 10 * slabs * rows * lanes),
        name="survey",
    )(state, state, velocity, velocity, velocity, *small, state, velocity)


def deposit_kernel(slabs, me, gathered, low_in, high_in, flux_out, deposit, low, high, flux, dropped):
    groups, lanes = gathered.shape[0], gathered.shape[2]
    here = me[0]
    limits = jnp.concatenate([gathered[g, slabs : slabs + 1] for g in range(groups)], axis=0)
    total = jnp.zeros((groups, lanes), jnp.float32)
    shape = (groups, slabs)
    numbers = lax.broadcasted_iota(jnp.int32, shape, 0).astype(jnp.float32)
    for g in range(groups):
        owners = gathered[g, slabs + 1 : slabs + 2, 0:slabs]
        stress = gathered[g, 0:slabs]
        named = (owners == numbers).astype(jnp.float32)
        limit = lax.dot_general(
            named, limits, (((0,), (0,)), ((), ())), precision=HIGHEST, preferred_element_type=jnp.float32
        )
        lifting = jnp.maximum(stress - limit, 0.0)
        total = total + jnp.dot(named, lifting, precision=HIGHEST, preferred_element_type=jnp.float32)
    flux[...] = total / slabs
    flux_out[...] = flux[pl.ds(here, 1), :]
    dropped[...] = jnp.zeros_like(dropped)
    before, after = jnp.maximum(here - 1, 0), jnp.minimum(here + 1, groups - 1)
    has_before, has_after = here > 0, here < groups - 1
    base = slabs + 8
    for p in range(groups):
        x = p % slabs
        row = flux[p : p + 1, :]
        dropped[x + 2 : x + 3] += row * gathered[p, pl.ds(base + here, 1), :]
        if x >= slabs - 2:
            mass = row * gathered[p, pl.ds(base + before, 1), :]
            dropped[x - slabs + 2 : x - slabs + 3] += jnp.where(has_before, mass, 0.0)
        if x < 2:
            mass = row * gathered[p, pl.ds(base + after, 1), :]
            dropped[x + slabs + 2 : x + slabs + 3] += jnp.where(has_after, mass, 0.0)
    deposit[...] = dropped[...].T
    own = dropped[2 : 2 + slabs, :]
    lane = lax.broadcasted_iota(jnp.int32, (slabs, lanes), 1)
    rows = lanes
    dust = low.shape[0] - 3
    low[...] = low_in[...]
    high[...] = high_in[...]
    for r in range(2):
        low[dust + r] += jnp.where(lane == 0, own[:, r : r + 1], 0.0)
        high[dust + r] += jnp.where(lane == 0, own[:, rows - 2 + r : rows - 1 + r], 0.0)


def settle(me, gathered, low, high, slabs):
    groups, _, lanes = gathered.shape
    edge = jax.ShapeDtypeStruct(low.shape, jnp.float32)
    return pl.pallas_call(
        functools.partial(deposit_kernel, slabs),
        out_shape=(
            jax.ShapeDtypeStruct((1, lanes), jnp.float32),
            jax.ShapeDtypeStruct((lanes, lanes), jnp.float32),
            edge,
            edge,
        ),
        in_specs=[SMEM, VMEM, VMEM, VMEM],
        out_specs=(VMEM, VMEM, VMEM, VMEM),
        scratch_shapes=[
            pltpu.VMEM((groups, lanes), jnp.float32),
            pltpu.VMEM((lanes, lanes), jnp.float32),
        ],
        compiler_params=params(),
        cost_estimate=cost(10**6, 10**6),
        name="settle",
    )(me, gathered, low, high)


def exchange(low, high, axis):
    count = lax.axis_size(axis)
    forward = [(i, i + 1) for i in range(count - 1)]
    backward = [(target, source) for source, target in forward]
    return lax.ppermute(high, axis, forward), lax.ppermute(low, axis, backward)


def shards(state, velocity, threshold, tile_owner, parcel_owner, parcel_count, parcel_share):
    groups = lax.axis_size("gx")
    slabs = state.shape[1]
    me = lax.axis_index("gx").astype(jnp.int32).reshape(1)

    low, high, payload, x_low, x_high = survey(
        groups, state, velocity, threshold, tile_owner[:, :, 0], parcel_owner[:, :, 0], parcel_count, parcel_share
    )
    copies = jnp.broadcast_to(payload[None], (groups, *payload.shape))
    gathered = lax.all_to_all(copies, "gx", split_axis=0, concat_axis=0, tiled=True)
    flux, deposit, low, high = settle(me, gathered, low, high, slabs)
    below, above = exchange(low, high, "gy")
    x_low, x_high, _ = lax.optimization_barrier((x_low, x_high, gathered))
    x_low, x_high = exchange(x_low, x_high, "gx")
    middle, pack_low, pack_high = interior([state], velocity, below, above, below, above, deposit)
    end_low, end_high, y_low, y_high = boundary(
        [state, x_low, x_high], velocity, x_low, x_high, below, above, below, above,
        deposit=deposit, packed=(pack_low, pack_high),
    )
    x2_low, x2_high = exchange(end_low, end_high, "gx")
    below2, above2 = exchange(y_low, y_high, "gy")
    (inside,) = interior([middle, end_low, end_high], velocity, below2, above2, below, above)
    fields = boundary(
        [middle, end_low, end_high, x2_low, x2_high], velocity, x_low, x_high, below2, above2, below, above,
        out=inside,
    )
    return fields, flux


def solution(mesh):
    return jax.shard_map(
        shards,
        mesh=mesh,
        in_specs=(
            P(None, "gx", "gy", None),
            P(None, "gx", "gy", None),
            P("gx", "gy"),
            P("gy", "gx", None),
            P("gy", "gx", None),
            P("gy", "gx"),
            P("gy", "gx", None),
        ),
        out_specs=(P(None, "gx", "gy", None), P("gx", "gy")),
        check_vma=False,
    )
```

```python
import functools

import jax
import jax.numpy as jnp
from jax import lax
from jax.experimental import pallas as pl
from jax.experimental.pallas import tpu as pltpu
from jax.sharding import PartitionSpec as P

LEVELS = 4
profile_weights = (0.4, 0.3, 0.2, 0.1)
time_step = 0.1
FACTOR = 0.25 * time_step

VMEM_LIMIT = 48 * 1024 * 1024
PAIR = 2
GROUP = 8
CHUNK = 4
AHEAD = 3
HIGHEST = lax.Precision.HIGHEST
ANY = pl.BlockSpec(memory_space=pl.ANY)
VMEM = pl.BlockSpec(memory_space=pltpu.VMEM)
SMEM = pl.BlockSpec(memory_space=pltpu.SMEM)


def params():
    return pltpu.CompilerParams(vmem_limit_bytes=VMEM_LIMIT)


def cost(flops, moved):
    return pl.CostEstimate(flops=int(flops), bytes_accessed=int(moved), transcendentals=0)


def minmod(a, b):
    return jnp.maximum(jnp.minimum(a, b), jnp.minimum(jnp.maximum(a, b), 0.0))


def tile_of(ref, t, tiles):
    return ref[pl.ds(t, 8, stride=tiles), :]


class Slabs:
    def __init__(self, q, sx, sy, sz, fall, fx, lx, block, x_at, at, kept=None):
        self.q, self.sx, self.sy, self.sz, self.falls, self.fx, self.lx = q, sx, sy, sz, fall, fx, lx
        self.block, self.x_at, self.at, self.kept = block, x_at, at, kept
        self.comps, self.tiles, self.lanes = q.shape[1], sz.shape[2], q.shape[-1]

    def field(self, c, slab, t):
        return self.q[self.block, c, slab, t + 2]

    def east(self, k, t):
        return self.sx[self.block, k + self.x_at, t]

    def north(self, k, t):
        return self.sy[self.block, k + self.at, t + 1]

    def up(self, k, t):
        return self.sz[self.block, k + self.at, t]

    def down(self, k, t):
        return self.falls[self.block, k + self.at, t]


def each(function, *lists):
    return [function(*items) for items in zip(*lists)]


def minmods(a, b):
    low, high = each(jnp.minimum, a, b), each(jnp.maximum, a, b)
    high = each(lambda x: jnp.minimum(x, 0.0), high)
    return each(jnp.maximum, low, high)


def difference(a, b):
    return each(lambda x, y: x - y, a, b)


def total_of(a, b):
    return each(lambda x, y: x + y, a, b)


def face_flux(speeds, masks, low_side, high_side):
    picked = each(jnp.where, masks, low_side, high_side)
    return each(lambda x, y: x * y, speeds, picked)


def staged(jobs):
    waiting = []
    for job in jobs:
        stores = job()
        for ref, index, value in waiting:
            ref[index] = value
        waiting = stores
    for ref, index, value in waiting:
        ref[index] = value


def first_face(f):
    def job(ts):
        spots = [(t, c) for t in ts for c in range(f.comps)]
        speeds = {t: f.east(-1, t) for t in ts}
        masks = {t: speeds[t] > 0 for t in ts}
        a, b, q0, q1 = [[f.field(c, slab, t) for t, c in spots] for slab in range(4)]
        middle = difference(q0, b)
        left = total_of(total_of(b, b), minmods(middle, difference(b, a)))
        slope = minmods(difference(q1, q0), middle)
        twice = total_of(q0, q0)
        flux = face_flux([speeds[t] for t, _ in spots], [masks[t] for t, _ in spots], left, difference(twice, slope))
        stores = [(f.fx, spot, x) for spot, x in zip(spots, flux)]
        if f.kept is not None:
            stores += [(f.kept[0], spot, x) for spot, x in zip(spots, twice)]
            stores += [(f.kept[1], spot, x) for spot, x in zip(spots, difference(q1, q0))]
        return stores + [(f.lx, spot, x) for spot, x in zip(spots, total_of(twice, slope))]

    staged([functools.partial(job, range(t, t + PAIR)) for t in range(0, f.tiles, PAIR)])


def slab_step(f, k, put):
    slab = k + 2
    lane = lax.broadcasted_iota(jnp.int32, (8, f.lanes), 1)
    top = f.lanes - 1
    is_first, is_last = lane == 0, lane == top
    carry = []
    speed = f.north(k, -1)
    for c in range(f.comps):
        a, b, q0, q1 = [f.field(c, slab, t) for t in (-2, -1, 0, 1)]
        middle, ahead = q0 - b, q1 - q0
        left_state = (b + b) + minmod(middle, b - a)
        slope = minmod(ahead, middle)
        twice = q0 + q0
        flux = speed * jnp.where(speed > 0, left_state, twice - slope)
        carry.append((q0, q1, ahead, twice, twice + slope, flux))
    states, doubles = {}, {}

    def vertical(t):
        for c in range(f.comps):
            q0 = f.field(c, slab, t)
            over = jnp.where(is_last, 0.0, pltpu.roll(q0, top, 1))
            under = jnp.where(is_first, 0.0, pltpu.roll(q0, 1, 1))
            slope = minmod(over - q0, q0 - under)
            if f.kept is not None:
                doubles[c, t] = f.kept[0][t, c]
            twice = double(c, t, q0)
            states[t, c] = (twice - slope, twice + slope)

    def flush(held):
        for c, t, flux_x, left_x, twice_x, step_x, value in held:
            f.fx[t, c], f.lx[t, c] = flux_x, left_x
            if f.kept is not None:
                f.kept[0][t, c], f.kept[1][t, c] = twice_x, step_x
            put(c, t, value)

    def double(c, t, tile):
        if f.kept is None or not 0 <= t < f.tiles:
            return tile + tile
        return doubles[c, t]

    held = []
    for t in range(GROUP):
        vertical(t)
    for begin in range(0, f.tiles, GROUP):
        group = range(begin, min(begin + GROUP, f.tiles))
        for t in range(begin + GROUP, min(begin + 2 * GROUP, f.tiles)):
            vertical(t)
        loaded = {}
        for t in group:
            loaded[t] = (f.east(k, t), f.north(k, t), f.up(k, t), f.down(k, t))
            for c in range(f.comps):
                loaded[t, c] = (
                    f.field(c, slab, t + 2), f.field(c, slab + 1, t), f.field(c, slab + 2, t),
                    f.fx[t, c], f.lx[t, c], f.kept[1][t, c] if f.kept is not None else None,
                )
        flush(held)
        held = []
        for t in group:
            speed_x, speed_y, speed_z, fall = loaded[t]
            go_x, go_y, go_z, go_fall = speed_x > 0, speed_y > 0, speed_z > 0, fall > 0
            for c in range(f.comps):
                y2, x1, x2, flux_w, left_w, step_w = loaded[t, c]
                q0, y1, ahead, twice, left_y, flux_y = carry[c]
                beyond = y2 - y1
                slope = minmod(beyond, ahead)
                twice_y = double(c, t + 1, y1)
                flux_next = speed_y * jnp.where(go_y, left_y, twice_y - slope)
                total = flux_next - flux_y
                carry[c] = (y1, y2, beyond, twice_y, twice_y + slope, flux_next)
                step_x = x2 - x1
                slope = minmod(step_x, x1 - q0 if step_w is None else step_w)
                twice_x = x1 + x1
                flux_x = speed_x * jnp.where(go_x, left_w, twice_x - slope)
                left_x = twice_x + slope
                total = total + (flux_x - flux_w)
                lower, upper = states[t, c]
                flux_z = speed_z * jnp.where(go_z, upper, pltpu.roll(lower, top, 1))
                flux_below = fall * jnp.where(go_fall, pltpu.roll(upper, 1, 1), lower)
                total = total + (flux_z - flux_below)
                held.append((c, t, flux_x, left_x, twice_x, step_x, q0 - total))
    flush(held)


def rotated_edges(tiles, lows, highs):
    row = lax.broadcasted_iota(jnp.int32, tiles[0].shape, 0)
    ahead = [pltpu.roll(tile, 1, 0) for tile in tiles[-len(lows) :]]
    after = [pltpu.roll(tile, 7, 0) for tile in tiles[: len(highs)]]
    ahead = [jnp.where(row == 0, low, tile) for low, tile in zip(lows, ahead)]
    after = [jnp.where(row == 7, high, tile) for high, tile in zip(highs, after)]
    return ahead, after


def field_job(q, block, c, slab, dust, below, above, x):
    count = q.shape[3] - 4
    spots = range(count) if dust is not None else (0, 1, count - 2, count - 1)
    tiles = [q[block, c, slab, 2 + t] for t in spots]
    stores = []
    if below is not None:
        x = pl.ds(x, 1)
        lows = [below[2 * c + r, x, :] for r in range(2)]
        highs = [above[2 * c + r, x, :] for r in range(2)]
    if dust is not None:
        tiles = total_of(tiles, dust(spots))
        stores += [(q, (block, c, slab, t + 2), tile) for t, tile in zip(spots, tiles)]
    if below is not None:
        ahead, after = rotated_edges(tiles, lows, highs)
        stores += [(q, (block, c, slab, r), tile) for r, tile in enumerate(ahead)]
        stores += [(q, (block, c, slab, count + 2 + r), tile) for r, tile in enumerate(after)]
    return stores


def north_job(sy, block, slab, below, above, x):
    count = sy.shape[2] - 1
    x = pl.ds(x, 1)
    row = lax.broadcasted_iota(jnp.int32, sy.shape[-2:], 0)
    first, final = sy[block, slab, 0], sy[block, slab, count]
    first = first + jnp.where(row == 0, FACTOR * below[8, x, :], 0.0)
    final = final + jnp.where(row == 7, FACTOR * above[8, x, :], 0.0)
    return [(sy, (block, slab, 0), first), (sy, (block, slab, count), final)]


def falling(deposit, column, tiles):
    lanes = deposit.shape[-1]

    def dust(spots):
        parts = [pltpu.roll(tile_of(deposit, t, tiles), lanes - column, 1) for t in spots]
        lane = lax.broadcasted_iota(jnp.int32, parts[0].shape, 1)
        return [jnp.where(lane == 0, part, 0.0) for part in parts]

    return dust


def pack_edges(packs, stage_slab, comps, x):
    x = pl.ds(x, 1)
    stores = []
    for c in range(comps):
        tiles = stage_slab(c)
        count = tiles.shape[0]
        for r in range(2):
            stores.append((packs[0], (2 * c + r, x), tiles[r, 0:1, :]))
            stores.append((packs[1], (2 * c + r, x), tiles[count - 2 + r, 7:8, :]))
    staged([lambda: stores])


def start(source, target, sem):
    pltpu.make_async_copy(source, target, sem).start()


def start_sets(pairs, sem):
    for source, target in pairs:
        for number in range(8):
            start(source(number), target(number), sem)


def arrived(spot, sem):
    pltpu.make_async_copy(spot, spot, sem).wait()


def interior_kernel(last, count, *refs):
    refs = list(refs)
    fields, speeds = refs[:count], refs[count : count + 4]
    below, above, v_below, v_above = refs[count + 4 : count + 8]
    del refs[: count + 8]
    deposit = None if last else refs.pop(0)
    out = refs.pop(0)
    packs = None if last else (refs.pop(0), refs.pop(0))
    q, sx, sy, sz, fall, fx, lx, stage, in_sem, out_sem = refs[:10]
    kept = refs[10:12]
    comps, slabs, tiles = q.shape[1], q.shape[2], sz.shape[2]
    chunks = slabs // CHUNK
    inner = pl.ds(2, tiles)

    def fetch(j, first, final):
        begin, size = j * CHUNK, CHUNK
        span = pl.ds(begin, CHUNK)
        if last:
            middle, low, high = fields
            if first:
                begin, size = begin + 2, size - 2
                start(low, q.at[0, :, pl.ds(0, 2), inner], in_sem.at[j, 0])
            if final:
                size -= 2
                start(high, q.at[0, :, pl.ds(slabs - 2, 2), inner], in_sem.at[j, 0])
            part = pl.ds(begin, size)
            start(middle.at[:, part], q.at[0, :, part, inner], in_sem.at[j, 0])
        else:
            pair = (lambda n: fields[0].at[:, span, n], lambda n: q.at[0, :, span, inner, n])
            start_sets([pair], in_sem.at[j, 0])
        for n, (source, target) in enumerate(zip(speeds, (sx, sy, sz, fall))):
            start(source.at[span], target.at[0, span], in_sem.at[j, n + 1])

    for j in range(AHEAD):
        fetch(j, j == 0, False)

    def arrive(j):
        span = pl.ds(j * CHUNK, CHUNK)
        arrived(q.at[0, :, span, inner], in_sem.at[j, 0])
        for n, target in enumerate((sx, sy, sz, fall)):
            arrived(target.at[0, span], in_sem.at[j, n + 1])
        later = j + AHEAD

        @pl.when(later < chunks - 1)
        def _():
            fetch(later, False, False)

        @pl.when(later == chunks - 1)
        def _():
            fetch(chunks - 1, False, True)

        def complete(x, _):
            jobs = []
            for c in range(comps):
                dust = falling(deposit, x + 2, tiles) if not last and c == comps - 1 else None
                jobs.append(functools.partial(field_job, q, 0, c, x, dust, below, above, x))
            jobs.append(functools.partial(north_job, sy, 0, x, v_below, v_above, x))
            staged(jobs)
            return 0

        lax.fori_loop(j * CHUNK, (j + 1) * CHUNK, complete, 0)

    f = Slabs(q, sx, sy, sz, fall, fx, lx, 0, 2, 2, kept)
    arrive(jnp.int32(0))
    first_face(f)

    def step(k, _):
        @pl.when(k % CHUNK == 0)
        def _():
            arrive(k // CHUNK + 1)

        def put(c, t, value):
            stage[c, k, t] = value

        slab_step(f, k, put)
        if last:
            start_sets([(lambda n: stage.at[:, k, :, n], lambda n: out.at[:, k + 2, n])], out_sem)
        else:
            start(stage.at[:, k], out.at[:, k + 2], out_sem)
        if not last:
            pack_edges(packs, lambda c: stage.at[c, k], comps, k + 2)
        return 0

    if not last:
        for pack in packs:
            pack[...] = jnp.zeros_like(pack)
    lax.fori_loop(0, slabs - 4, step, 0)
    arrived(stage, out_sem)


def interior(fields, speeds, below, above, v_below, v_above, deposit=None):
    last = deposit is None
    slabs, tiles, _, lanes = speeds[0].shape
    rows, comps = 8 * tiles, fields[0].shape[0]
    operands = list(fields) + [*speeds, below, above, v_below, v_above]
    specs = [ANY] * (len(fields) + 4) + [VMEM] * 4
    form = (8, tiles, lanes) if last else (tiles, 8, lanes)
    out_shape = [jax.ShapeDtypeStruct((comps, slabs, *form), jnp.float32)]
    out_specs = [ANY]
    scratch = [
        pltpu.VMEM((1, comps, slabs, tiles + 4, 8, lanes), jnp.float32),
        *[pltpu.VMEM((1, *speed.shape), jnp.float32) for speed in speeds],
        pltpu.VMEM((tiles, comps, 8, lanes), jnp.float32),
        pltpu.VMEM((tiles, comps, 8, lanes), jnp.float32),
        pltpu.VMEM((comps, slabs - 4, tiles, 8, lanes), jnp.float32),
        pltpu.SemaphoreType.DMA((slabs // CHUNK, 5)),
        pltpu.SemaphoreType.DMA,
    ]
    scratch += [pltpu.VMEM((tiles, comps, 8, lanes), jnp.float32)] * 2
    if not last:
        out_shape += [jax.ShapeDtypeStruct((2 * comps, slabs, lanes), jnp.float32)] * 2
        out_specs += [VMEM] * 2
        operands.append(deposit)
        specs.append(VMEM)
    cells = comps * (slabs - 4) * rows * lanes
    return pl.pallas_call(
        functools.partial(interior_kernel, last, len(fields)),
        out_shape=tuple(out_shape),
        in_specs=specs,
        out_specs=tuple(out_specs),
        scratch_shapes=scratch,
        compiler_params=params(),
        cost_estimate=cost(40 * cells, 4 * (2 * cells + 4 * slabs * rows * lanes)),
        name="interior",
    )(*operands)


def boundary_kernel(last, slabs, *refs):
    refs = list(refs)
    count = 5 if last else 3
    fields, speeds = refs[:count], refs[count : count + 4]
    u_outer, u_inner = refs[count + 4 : count + 6], refs[count + 6 : count + 8]
    below, above, v_below, v_above = refs[count + 8 : count + 12]
    del refs[: count + 12]
    if last:
        out = refs[1]
        del refs[:2]
    else:
        deposit, packed, ends, packs = refs[0], refs[1:3], refs[3:5], refs[5:7]
        del refs[:7]
    q, sx, sy, sz, fall, fx, lx, u, stage, in_sem, out_sem = refs
    comps, tiles = q.shape[1], sz.shape[2]
    inner = pl.ds(2, tiles)

    if last:
        middle, end_low, end_high, x_low, x_high = fields
        for block, at, source in (
            (0, 0, x_low), (0, 2, end_low), (0, 4, middle.at[:, pl.ds(2, 2)]),
            (1, 0, middle.at[:, pl.ds(slabs - 4, 2)]), (1, 2, end_high), (1, 4, x_high),
        ):
            start(source, q.at[block, :, pl.ds(at, 2), inner], in_sem.at[block, 0])
    else:
        state, x_low, x_high = fields
        for block, at, first in ((0, 2, 0), (1, 0, slabs - 4)):
            pair = (
                lambda n: state.at[:, pl.ds(first, 4), n], lambda n: q.at[block, :, pl.ds(at, 4), inner, n]
            )
            start_sets([pair], in_sem.at[block, 0])
        for block, at, halo in ((0, 0, x_low), (1, 4, x_high)):
            pairs = [
                (lambda n, c=c: halo.at[pl.ds(2 * c, 2), n], lambda n, c=c: q.at[block, c, pl.ds(at, 2), inner, n])
                for c in range(comps)
            ]
            start_sets(pairs, in_sem.at[block, 0])
    edge = pl.ds(2 * comps, 1)
    for block in range(2):
        pairs = [
            (lambda n, r=ref: r.at[edge, n], lambda n, i=i: u.at[block, pl.ds(i, 1), :, n])
            for i, ref in enumerate((u_outer[block], u_inner[block]))
        ]
        start_sets(pairs, in_sem.at[block, 1])
    start(speeds[0].at[pl.ds(0, 2)], sx.at[0, pl.ds(1, 2)], in_sem.at[0, 2])
    start(speeds[0].at[pl.ds(slabs - 3, 2)], sx.at[1, pl.ds(0, 2)], in_sem.at[1, 2])
    for block in range(2):
        span = pl.ds(block * (slabs - 2), 2)
        for n, target in enumerate((sy, sz, fall)):
            start(speeds[n + 1].at[span], target.at[block], in_sem.at[block, n + 3])
    if not last:
        packs[0][...] = packed[0][...]
        packs[1][...] = packed[1][...]

    def one(block, _):
        begin = block * (slabs - 2)
        arrived(q.at[block, :, :, inner], in_sem.at[block, 0])
        arrived(u.at[block], in_sem.at[block, 1])
        arrived(sx.at[block, pl.ds(0, 2)], in_sem.at[block, 2])
        for n, target in enumerate((sy, sz, fall)):
            arrived(target.at[block], in_sem.at[block, n + 3])

        def complete(slab, _):
            dust = falling(deposit, begin + slab, tiles)
            staged([functools.partial(field_job, q, block, comps - 1, slab, dust, None, None, None)])
            return 0

        if not last:
            lax.fori_loop(0, 6, complete, 0)

        def edges(k, _):
            x = begin + k
            jobs = [
                functools.partial(field_job, q, block, c, k + 2, None, below, above, x) for c in range(comps)
            ]
            jobs.append(functools.partial(north_job, sy, block, k, v_below, v_above, x))
            staged(jobs)
            return 0

        lax.fori_loop(0, 2, edges, 0)
        faces = total_of([u[block, 0, t] for t in range(tiles)], [u[block, 1, t] for t in range(tiles)])
        for t, x in enumerate(faces):
            sx[block, 2 * block, t] = FACTOR * x
        f = Slabs(q, sx, sy, sz, fall, fx, lx, block, 1, 0)
        first_face(f)

        def step(k, _):
            def put(c, t, value):
                stage[block, c, k, t] = value

            slab_step(f, k, put)
            if not last:
                pack_edges(packs, lambda c: stage.at[block, c, k], comps, begin + k)
            return 0

        lax.fori_loop(0, 2, step, 0)
        return 0

    lax.fori_loop(0, 2, one, 0)
    for block in range(2):
        if last:
            span = pl.ds(block * (slabs - 2), 2)
            pair = (lambda n: stage.at[block, :, :, :, n], lambda n: out.at[:, span, n])
            start_sets([pair], out_sem.at[block])
        else:
            start(stage.at[block], ends[block], out_sem.at[block])
    for block in range(2):
        arrived(stage.at[block], out_sem.at[block])


def boundary(fields, speeds, u_outer, u_inner, below, above, v_below, v_above, *, deposit=None, packed=None, out=None):
    last = out is not None
    slabs, tiles, _, lanes = speeds[0].shape
    rows, comps = 8 * tiles, fields[0].shape[0]
    operands = list(fields) + [*speeds, *u_outer, *u_inner, below, above, v_below, v_above]
    specs = [ANY] * (len(fields) + 8) + [VMEM] * 4
    form = (tiles, 8, lanes)
    scratch = [
        pltpu.VMEM((2, comps, 6, tiles + 4, 8, lanes), jnp.float32),
        pltpu.VMEM((2, 3, tiles, 8, lanes), jnp.float32),
        pltpu.VMEM((2, 2, tiles + 1, 8, lanes), jnp.float32),
        pltpu.VMEM((2, 2, tiles, 8, lanes), jnp.float32),
        pltpu.VMEM((2, 2, tiles, 8, lanes), jnp.float32),
        pltpu.VMEM((tiles, comps, 8, lanes), jnp.float32),
        pltpu.VMEM((tiles, comps, 8, lanes), jnp.float32),
        pltpu.VMEM((2, 2, tiles, 8, lanes), jnp.float32),
        pltpu.VMEM((2, comps, 2, *form), jnp.float32),
        pltpu.SemaphoreType.DMA((2, 6)),
        pltpu.SemaphoreType.DMA((2,)),
    ]
    if last:
        aliases = {len(operands): 0}
        operands.append(out)
        specs.append(ANY)
        out_shape = jax.ShapeDtypeStruct(out.shape, out.dtype)
        out_specs = ANY
    else:
        aliases = {}
        operands += [deposit, *packed]
        specs += [VMEM] * 3
        out_shape = (jax.ShapeDtypeStruct((comps, 2, *form), jnp.float32),) * 2
        out_shape += (jax.ShapeDtypeStruct((2 * comps, slabs, lanes), jnp.float32),) * 2
        out_specs = (ANY, ANY, VMEM, VMEM)
    cells = comps * 4 * rows * lanes
    return pl.pallas_call(
        functools.partial(boundary_kernel, last, slabs),
        out_shape=out_shape,
        in_specs=specs,
        out_specs=out_specs,
        scratch_shapes=scratch,
        input_output_aliases=aliases,
        compiler_params=params(),
        cost_estimate=cost(50 * cells, 4 * 6 * cells),
        name="boundary",
    )(*operands)


def speeds_kernel(velocity, sx, sy, sz, fall, wind, sems):
    step, steps = pl.program_id(0), pl.num_programs(0)
    part, count, lanes = sx.shape[0], wind.shape[2], wind.shape[4]
    shape = (8, lanes)
    row, lane = (lax.broadcasted_iota(jnp.int32, shape, axis) for axis in range(2))
    is_first, is_last = lane == 0, lane == lanes - 1

    @pl.when(step == 0)
    def _():
        for j in range(wind.shape[1] // part):
            span = pl.ds(j * part, part)
            start_sets([(lambda n: velocity.at[:, span, n], lambda n: wind.at[:, span, :, n])], sems.at[j])
        arrived(wind.at[:, pl.ds(0, part)], sems.at[0])

    @pl.when(step < steps - 1)
    def _():
        arrived(wind.at[:, pl.ds((step + 1) * part, part)], sems.at[step + 1])

    def one(x, _):
        at = step * part + x
        after = jnp.minimum(at + 1, wind.shape[1] - 1)

        def job_x():
            here = [wind[0, at, t] for t in range(count)]
            nearer = [wind[0, after, t] for t in range(count)]
            return [(sx, (x, t), FACTOR * tile) for t, tile in enumerate(total_of(here, nearer))]

        def job_y():
            here = [FACTOR * wind[1, at, t] for t in range(count)]
            inner = total_of(here[:-1], here[1:])
            final = here[-1] + jnp.where(row == 7, 0.0, pltpu.roll(here[0], 7, 0))
            first = here[0] + jnp.where(row == 0, 0.0, pltpu.roll(here[-1], 1, 0))
            return [(sy, (x, t), tile) for t, tile in enumerate([first, *inner, final])]

        def job_z():
            here = [FACTOR * wind[2, at, t] for t in range(count)]
            over = [pltpu.roll(tile, lanes - 1, 1) for tile in here]
            under = [pltpu.roll(tile, 1, 1) for tile in here]
            upper = [jnp.where(is_last, jnp.maximum(a, 0.0), a + b) for a, b in zip(here, over)]
            lower = [jnp.where(is_first, jnp.minimum(a, 0.0), a + b) for a, b in zip(here, under)]
            stores = [(sz, (x, t), tile) for t, tile in enumerate(upper)]
            return stores + [(fall, (x, t), tile) for t, tile in enumerate(lower)]

        staged([job_x, job_y, job_z])
        return 0

    lax.fori_loop(0, part, one, 0)


def face_speeds(velocity):
    _, slabs, _, tiles, lanes = velocity.shape
    part = 8
    counts = (tiles, tiles + 1, tiles, tiles)
    return pl.pallas_call(
        speeds_kernel,
        grid=(slabs // part,),
        out_shape=tuple(jax.ShapeDtypeStruct((slabs, n, 8, lanes), jnp.float32) for n in counts),
        in_specs=[ANY],
        out_specs=tuple(pl.BlockSpec((part, n, 8, lanes), lambda i: (i, 0, 0, 0)) for n in counts),
        scratch_shapes=[
            pltpu.VMEM((3, slabs, tiles, 8, lanes), jnp.float32),
            pltpu.SemaphoreType.DMA((slabs // part,)),
        ],
        compiler_params=params(),
        cost_estimate=cost(16 * slabs * 8 * tiles * lanes, 28 * slabs * 8 * tiles * lanes),
        name="face_speeds",
    )(velocity)


def x_copies(state, velocity, low, high, sems):
    comps, slabs = state.shape[0], state.shape[1]
    copies = []
    for n, (target, first, edge) in enumerate(((low, 0, 0), (high, slabs - 2, slabs - 1))):
        pairs = [(state.at[c, pl.ds(first, 2)], target.at[pl.ds(2 * c, 2)]) for c in range(comps)]
        pairs.append((velocity.at[0, pl.ds(edge, 1)], target.at[pl.ds(2 * comps, 1)]))
        copies += [pltpu.make_async_copy(*pair, sems.at[n, i]) for i, pair in enumerate(pairs)]
    return copies


def as_column(row):
    count = row.shape[1]
    shape = (count, count)
    same = lax.broadcasted_iota(jnp.int32, shape, 0) == lax.broadcasted_iota(jnp.int32, shape, 1)
    return jnp.sum(jnp.where(same, row, 0.0), axis=1, keepdims=True)


def survey_kernel(
    groups, low_in, high_in, v_low, v_high, wind, threshold_in, tile_owner_in, parcel_owner_in, count_in, share_in,
    state, velocity, low, high, payload, x_low, x_high,
    gathered, threshold, tile_owner, parcel_owner, count, share, sems, small_sems,
):
    small = [
        pltpu.make_async_copy(source, target, small_sems.at[n])
        for n, (source, target) in enumerate(
            (
                (threshold_in, threshold), (tile_owner_in, tile_owner), (parcel_owner_in, parcel_owner),
                (count_in, count), (share_in, share),
            )
        )
    ]
    step, steps = pl.program_id(0), pl.num_programs(0)

    @pl.when(step == 0)
    def _():
        for copy in small + x_copies(state, velocity, x_low, x_high, sems):
            copy.start()

    comps, part, rows, lanes = low_in.shape[0], wind.shape[1], wind.shape[2], wind.shape[3]
    slabs = share.shape[1]
    for x in range(part):
        for c in range(comps):
            for r in range(2):
                low[2 * c + r, x : x + 1, :] = low_in[c, x, r : r + 1, :]
                high[2 * c + r, x : x + 1, :] = high_in[c, x, 6 + r : 7 + r, :]
        low[2 * comps, x : x + 1, :] = v_low[0, x, 0:1, :]
        high[2 * comps, x : x + 1, :] = v_high[0, x, 7:8, :]
    lane = lax.broadcasted_iota(jnp.int32, (rows, lanes), 1)
    weight = jnp.zeros((rows, lanes), jnp.float32)
    for level, value in enumerate(profile_weights):
        weight = jnp.where(lane == level, value, weight)
    total = jnp.zeros((rows, lanes), jnp.float32)
    for x in range(part):
        east, north = wind[0, x], wind[1, x]
        friction = jnp.where(lane < LEVELS, weight * (east * east + north * north), 0.0)
        total = total + pltpu.roll(friction, LEVELS * x, 1) if x else friction

    @pl.when(step == 0)
    def _():
        gathered[...] = total

    @pl.when(step == steps // 2)
    def _():
        for copy in small:
            copy.wait()
        payload[slabs : slabs + 8] = jnp.zeros((8, lanes), jnp.float32)
        payload[slabs : slabs + 1] = threshold[...]
        payload[slabs + 1 : slabs + 2, 0:slabs] = tile_owner[...].astype(jnp.float32)
        owners = parcel_owner[...].astype(jnp.float32)
        shape = (groups, slabs)
        place = (owners == lax.broadcasted_iota(jnp.int32, shape, 0).astype(jnp.float32)).astype(jnp.float32)
        live = as_column(count[...].astype(jnp.float32))
        shape = (slabs, lanes)
        reach = lax.broadcasted_iota(jnp.int32, shape, 1).astype(jnp.float32) < live
        masses = jnp.where(reach, share[0], 0.0)
        payload[slabs + 8 : slabs + 8 + groups] = jnp.dot(
            place, masses, precision=HIGHEST, preferred_element_type=jnp.float32
        )

    @pl.when(step > 0)
    def _():
        gathered[...] += pltpu.roll(total, LEVELS * part * step, 1)

    @pl.when(step == steps - 1)
    def _():
        gathered[...] = gathered[...].T
        stress = gathered[pl.ds(0, slabs, stride=LEVELS), :]
        for level in range(1, LEVELS):
            stress = stress + gathered[pl.ds(level, slabs, stride=LEVELS), :]
        payload[0:slabs] = stress
        for copy in x_copies(state, velocity, x_low, x_high, sems):
            copy.wait()


def survey(groups, state, velocity, threshold, tile_owner, parcel_owner, count, share):
    comps, slabs, rows, lanes = state.shape
    part = 8
    last = rows // 8 - 1

    small = (threshold, tile_owner, parcel_owner, count, share)
    packed = jax.ShapeDtypeStruct((2 * comps + 1, slabs, lanes), jnp.float32)
    packed_spec = pl.BlockSpec((2 * comps + 1, part, lanes), lambda i: (0, i, 0))
    x_packed = jax.ShapeDtypeStruct((2 * comps + 1, rows, lanes), jnp.float32)
    height = slabs + 8 + groups
    return pl.pallas_call(
        functools.partial(survey_kernel, groups),
        grid=(slabs // part,),
        out_shape=(packed, packed, jax.ShapeDtypeStruct((height, lanes), jnp.float32), x_packed, x_packed),
        in_specs=[
            pl.BlockSpec((comps, part, 8, lanes), lambda i: (0, i, 0, 0)),
            pl.BlockSpec((comps, part, 8, lanes), lambda i: (0, i, last, 0)),
            pl.BlockSpec((1, part, 8, lanes), lambda i: (1, i, 0, 0)),
            pl.BlockSpec((1, part, 8, lanes), lambda i: (1, i, last, 0)),
            pl.BlockSpec((2, part, rows, lanes), lambda i: (0, i, 0, 0)),
            *[pl.BlockSpec(memory_space=pltpu.HBM)] * 7,
        ],
        out_specs=(packed_spec, packed_spec, pl.BlockSpec((height, lanes), lambda i: (0, 0)), ANY, ANY),
        scratch_shapes=[
            pltpu.VMEM((rows, lanes), jnp.float32),
            *[pltpu.VMEM(array.shape, array.dtype) for array in small],
            pltpu.SemaphoreType.DMA((2, comps + 1)),
            pltpu.SemaphoreType.DMA((len(small),)),
        ],
        compiler_params=params(),
        cost_estimate=cost(10 * slabs * rows * lanes, 10 * slabs * rows * lanes),
        name="survey",
    )(state, state, velocity, velocity, velocity, *small, state, velocity)


def deposit_kernel(slabs, me, gathered, low_in, high_in, flux_out, deposit, low, high, flux, dropped):
    groups, lanes = gathered.shape[0], gathered.shape[2]
    here = me[0]
    limits = jnp.concatenate([gathered[g, slabs : slabs + 1] for g in range(groups)], axis=0)
    total = jnp.zeros((groups, lanes), jnp.float32)
    shape = (groups, slabs)
    numbers = lax.broadcasted_iota(jnp.int32, shape, 0).astype(jnp.float32)
    for g in range(groups):
        owners = gathered[g, slabs + 1 : slabs + 2, 0:slabs]
        stress = gathered[g, 0:slabs]
        named = (owners == numbers).astype(jnp.float32)
        limit = lax.dot_general(
            named, limits, (((0,), (0,)), ((), ())), precision=HIGHEST, preferred_element_type=jnp.float32
        )
        lifting = jnp.maximum(stress - limit, 0.0)
        total = total + jnp.dot(named, lifting, precision=HIGHEST, preferred_element_type=jnp.float32)
    flux[...] = total / slabs
    flux_out[...] = flux[pl.ds(here, 1), :]
    dropped[...] = jnp.zeros_like(dropped)
    before, after = jnp.maximum(here - 1, 0), jnp.minimum(here + 1, groups - 1)
    has_before, has_after = here > 0, here < groups - 1
    base = slabs + 8
    for p in range(groups):
        x = p % slabs
        row = flux[p : p + 1, :]
        dropped[x + 2 : x + 3] += row * gathered[p, pl.ds(base + here, 1), :]
        if x >= slabs - 2:
            mass = row * gathered[p, pl.ds(base + before, 1), :]
            dropped[x - slabs + 2 : x - slabs + 3] += jnp.where(has_before, mass, 0.0)
        if x < 2:
            mass = row * gathered[p, pl.ds(base + after, 1), :]
            dropped[x + slabs + 2 : x + slabs + 3] += jnp.where(has_after, mass, 0.0)
    deposit[...] = dropped[...].T
    own = dropped[2 : 2 + slabs, :]
    lane = lax.broadcasted_iota(jnp.int32, (slabs, lanes), 1)
    rows = lanes
    dust = low.shape[0] - 3
    low[...] = low_in[...]
    high[...] = high_in[...]
    for r in range(2):
        low[dust + r] += jnp.where(lane == 0, own[:, r : r + 1], 0.0)
        high[dust + r] += jnp.where(lane == 0, own[:, rows - 2 + r : rows - 1 + r], 0.0)


def settle(me, gathered, low, high, slabs):
    groups, _, lanes = gathered.shape
    edge = jax.ShapeDtypeStruct(low.shape, jnp.float32)
    return pl.pallas_call(
        functools.partial(deposit_kernel, slabs),
        out_shape=(
            jax.ShapeDtypeStruct((1, lanes), jnp.float32),
            jax.ShapeDtypeStruct((lanes, lanes), jnp.float32),
            edge,
            edge,
        ),
        in_specs=[SMEM, VMEM, VMEM, VMEM],
        out_specs=(VMEM, VMEM, VMEM, VMEM),
        scratch_shapes=[
            pltpu.VMEM((groups, lanes), jnp.float32),
            pltpu.VMEM((lanes, lanes), jnp.float32),
        ],
        compiler_params=params(),
        cost_estimate=cost(10**6, 10**6),
        name="settle",
    )(me, gathered, low, high)


def exchange(low, high, axis):
    count = lax.axis_size(axis)
    forward = [(i, i + 1) for i in range(count - 1)]
    backward = [(target, source) for source, target in forward]
    return lax.ppermute(high, axis, forward), lax.ppermute(low, axis, backward)


def shards(state, velocity, threshold, tile_owner, parcel_owner, parcel_count, parcel_share):
    groups = lax.axis_size("gx")
    slabs = state.shape[1]
    me = lax.axis_index("gx").astype(jnp.int32).reshape(1)

    low, high, payload, own_low, own_high = survey(
        groups, state, velocity, threshold, tile_owner[:, :, 0], parcel_owner[:, :, 0], parcel_count, parcel_share
    )
    rows, lanes = state.shape[2:]

    def sets(array):
        return array.reshape(*array.shape[:-2], 8, rows // 8, lanes)

    speeds = face_speeds(sets(velocity))
    copies = jnp.broadcast_to(payload[None], (groups, *payload.shape))
    gathered = lax.all_to_all(copies, "gx", split_axis=0, concat_axis=0, tiled=True)
    flux, deposit, low, high = settle(me, gathered, low, high, slabs)
    below, above = exchange(low, high, "gy")
    own_low, own_high, _ = lax.optimization_barrier((own_low, own_high, gathered))
    x_low, x_high = exchange(own_low, own_high, "gx")
    x_low, x_high = sets(x_low), sets(x_high)
    u_edges = ((x_low, x_high), (sets(own_low), sets(own_high)))
    middle, pack_low, pack_high = interior([sets(state)], speeds, below, above, below, above, deposit)
    end_low, end_high, y_low, y_high = boundary(
        [sets(state), x_low, x_high], speeds, *u_edges, below, above, below, above,
        deposit=deposit, packed=(pack_low, pack_high),
    )
    x2_low, x2_high = exchange(end_low, end_high, "gx")
    below2, above2 = exchange(y_low, y_high, "gy")
    (inside,) = interior([middle, end_low, end_high], speeds, below2, above2, below, above)
    fields = boundary(
        [middle, end_low, end_high, x2_low, x2_high], speeds, *u_edges, below2, above2, below, above,
        out=inside,
    )
    return fields.reshape(state.shape), flux


def solution(mesh):
    return jax.shard_map(
        shards,
        mesh=mesh,
        in_specs=(
            P(None, "gx", "gy", None),
            P(None, "gx", "gy", None),
            P("gx", "gy"),
            P("gy", "gx", None),
            P("gy", "gx", None),
            P("gy", "gx"),
            P("gy", "gx", None),
        ),
        out_specs=(P(None, "gx", "gy", None), P("gx", "gy")),
        check_vma=False,
    )
```

```python
import functools

import jax
import jax.numpy as jnp
from jax import lax
from jax.experimental import pallas as pl
from jax.experimental.pallas import tpu as pltpu
from jax.sharding import PartitionSpec as P

LEVELS = 4
profile_weights = (0.4, 0.3, 0.2, 0.1)
time_step = 0.1
FACTOR = 0.25 * time_step

VMEM_LIMIT = 48 * 1024 * 1024
PAIR = 2
GROUP = 8
HIGHEST = lax.Precision.HIGHEST
ANY = pl.BlockSpec(memory_space=pl.ANY)
VMEM = pl.BlockSpec(memory_space=pltpu.VMEM)
SMEM = pl.BlockSpec(memory_space=pltpu.SMEM)


def params():
    return pltpu.CompilerParams(vmem_limit_bytes=VMEM_LIMIT)


def cost(flops, moved):
    return pl.CostEstimate(flops=int(flops), bytes_accessed=int(moved), transcendentals=0)


def minmod(a, b):
    return jnp.maximum(jnp.minimum(a, b), jnp.minimum(jnp.maximum(a, b), 0.0))


def tile_of(ref, t, tiles):
    return ref[pl.ds(t, 8, stride=tiles), :]


class Slabs:
    def __init__(self, q, u, v, sz, fall, fx, lx, block, x_at, at, halo, x, kept=None):
        self.q, self.u, self.v, self.sz, self.falls, self.fx, self.lx = q, u, v, sz, fall, fx, lx
        self.block, self.x_at, self.at, self.kept = block, x_at, at, kept
        self.halo, self.x = halo, x
        self.comps, self.tiles, self.lanes = q.shape[1], sz.shape[2], q.shape[-1]

    def field(self, c, slab, t):
        return self.q[self.block, c, slab, t]

    def row(self, k, which, number):
        return self.halo[which][number, pl.ds(self.x + k, 1), :]

    def centre(self, c, k, t):
        slab = k + 2
        if 0 <= t < self.tiles:
            return self.field(c, slab, t)
        row = lax.broadcasted_iota(jnp.int32, (8, self.lanes), 0)
        if t < 0:
            moved = pltpu.roll(self.field(c, slab, t + self.tiles), 1, 0)
            return jnp.where(row == 0, self.row(k, 0, 2 * c + t + 2), moved)
        t -= self.tiles
        return jnp.where(row == 7, self.row(k, 1, 2 * c + t), pltpu.roll(self.field(c, slab, t), 7, 0))

    def east(self, k, t):
        here = k + self.x_at
        return FACTOR * (self.u[self.block, here, t] + self.u[self.block, here + 1, t])

    def wind(self, k, t):
        inner = self.v[self.block, k + self.at, t % self.tiles]
        if 0 <= t < self.tiles:
            return inner
        row = lax.broadcasted_iota(jnp.int32, (8, self.lanes), 0)
        end, turn, which = (0, 1, 2) if t < 0 else (7, 7, 3)
        return jnp.where(row == end, self.row(k, which, 2 * self.comps), pltpu.roll(inner, turn, 0))

    def north(self, k, t):
        return FACTOR * (self.wind(k, t) + self.wind(k, t + 1))

    def up(self, k, t):
        return self.sz[self.block, k + self.at, t]

    def down(self, k, t):
        return self.falls[self.block, k + self.at, t]


def each(function, *lists):
    return [function(*items) for items in zip(*lists)]


def minmods(a, b):
    low, high = each(jnp.minimum, a, b), each(jnp.maximum, a, b)
    high = each(lambda x: jnp.minimum(x, 0.0), high)
    return each(jnp.maximum, low, high)


def difference(a, b):
    return each(lambda x, y: x - y, a, b)


def total_of(a, b):
    return each(lambda x, y: x + y, a, b)


def face_flux(speeds, masks, low_side, high_side):
    picked = each(jnp.where, masks, low_side, high_side)
    return each(lambda x, y: x * y, speeds, picked)


def staged(jobs):
    waiting = []
    for job in jobs:
        stores = job()
        for ref, index, value in waiting:
            ref[index] = value
        waiting = stores
    for ref, index, value in waiting:
        ref[index] = value


def first_face(f):
    def job(ts):
        spots = [(t, c) for t in ts for c in range(f.comps)]
        speeds = {t: f.east(-1, t) for t in ts}
        masks = {t: speeds[t] > 0 for t in ts}
        a, b, q0, q1 = [[f.field(c, slab, t) for t, c in spots] for slab in range(4)]
        middle = difference(q0, b)
        left = total_of(total_of(b, b), minmods(middle, difference(b, a)))
        slope = minmods(difference(q1, q0), middle)
        twice = total_of(q0, q0)
        flux = face_flux([speeds[t] for t, _ in spots], [masks[t] for t, _ in spots], left, difference(twice, slope))
        stores = [(f.fx, spot, x) for spot, x in zip(spots, flux)]
        if f.kept is not None:
            stores += [(f.kept[0], spot, x) for spot, x in zip(spots, twice)]
            stores += [(f.kept[1], spot, x) for spot, x in zip(spots, difference(q1, q0))]
        return stores + [(f.lx, spot, x) for spot, x in zip(spots, total_of(twice, slope))]

    staged([functools.partial(job, range(t, t + PAIR)) for t in range(0, f.tiles, PAIR)])


def slab_step(f, k, put):
    slab = k + 2
    lane = lax.broadcasted_iota(jnp.int32, (8, f.lanes), 1)
    top = f.lanes - 1
    is_first, is_last = lane == 0, lane == top
    carry = []
    speed = f.north(k, -1)
    for c in range(f.comps):
        a, b, q0, q1 = [f.centre(c, k, t) for t in (-2, -1, 0, 1)]
        middle, ahead = q0 - b, q1 - q0
        left_state = (b + b) + minmod(middle, b - a)
        slope = minmod(ahead, middle)
        twice = q0 + q0
        flux = speed * jnp.where(speed > 0, left_state, twice - slope)
        carry.append((q0, q1, ahead, twice, twice + slope, flux))
    states, doubles = {}, {}

    def vertical(t):
        for c in range(f.comps):
            q0 = f.field(c, slab, t)
            over = jnp.where(is_last, 0.0, pltpu.roll(q0, top, 1))
            under = jnp.where(is_first, 0.0, pltpu.roll(q0, 1, 1))
            slope = minmod(over - q0, q0 - under)
            if f.kept is not None:
                doubles[c, t] = f.kept[0][t, c]
            twice = double(c, t, q0)
            states[t, c] = (twice - slope, twice + slope)

    def flush(held):
        for c, t, flux_x, left_x, twice_x, step_x, value in held:
            f.fx[t, c], f.lx[t, c] = flux_x, left_x
            if f.kept is not None:
                f.kept[0][t, c], f.kept[1][t, c] = twice_x, step_x
            put(c, t, value)

    def double(c, t, tile):
        if f.kept is None or not 0 <= t < f.tiles:
            return tile + tile
        return doubles[c, t]

    held = []
    for t in range(GROUP):
        vertical(t)
    for begin in range(0, f.tiles, GROUP):
        group = range(begin, min(begin + GROUP, f.tiles))
        for t in range(begin + GROUP, min(begin + 2 * GROUP, f.tiles)):
            vertical(t)
        loaded = {}
        for t in group:
            loaded[t] = (f.east(k, t), f.north(k, t), f.up(k, t), f.down(k, t))
            for c in range(f.comps):
                loaded[t, c] = (
                    f.centre(c, k, t + 2), f.field(c, slab + 1, t), f.field(c, slab + 2, t),
                    f.fx[t, c], f.lx[t, c], f.kept[1][t, c] if f.kept is not None else None,
                )
        flush(held)
        held = []
        for t in group:
            speed_x, speed_y, speed_z, fall = loaded[t]
            go_x, go_y, go_z, go_fall = speed_x > 0, speed_y > 0, speed_z > 0, fall > 0
            for c in range(f.comps):
                y2, x1, x2, flux_w, left_w, step_w = loaded[t, c]
                q0, y1, ahead, twice, left_y, flux_y = carry[c]
                beyond = y2 - y1
                slope = minmod(beyond, ahead)
                twice_y = double(c, t + 1, y1)
                flux_next = speed_y * jnp.where(go_y, left_y, twice_y - slope)
                total = flux_next - flux_y
                carry[c] = (y1, y2, beyond, twice_y, twice_y + slope, flux_next)
                step_x = x2 - x1
                slope = minmod(step_x, x1 - q0 if step_w is None else step_w)
                twice_x = x1 + x1
                flux_x = speed_x * jnp.where(go_x, left_w, twice_x - slope)
                left_x = twice_x + slope
                total = total + (flux_x - flux_w)
                lower, upper = states[t, c]
                flux_z = speed_z * jnp.where(go_z, upper, pltpu.roll(lower, top, 1))
                flux_below = fall * jnp.where(go_fall, pltpu.roll(upper, 1, 1), lower)
                total = total + (flux_z - flux_below)
                held.append((c, t, flux_x, left_x, twice_x, step_x, q0 - total))
    flush(held)


def dust_job(q, block, slab, dust):
    c, spots = q.shape[1] - 1, range(q.shape[3])
    tiles = total_of([q[block, c, slab, t] for t in spots], dust(spots))
    return [(q, (block, c, slab, t), tile) for t, tile in zip(spots, tiles)]


def falling(deposit, column):
    lanes = deposit.shape[-1]

    def dust(spots):
        parts = [pltpu.roll(deposit[t], lanes - column, 1) for t in spots]
        lane = lax.broadcasted_iota(jnp.int32, parts[0].shape, 1)
        return [jnp.where(lane == 0, part, 0.0) for part in parts]

    return dust


def pack_edges(packs, stage_slab, comps, x):
    x = pl.ds(x, 1)
    stores = []
    for c in range(comps):
        tiles = stage_slab(c)
        count = tiles.shape[0]
        for r in range(2):
            stores.append((packs[0], (2 * c + r, x), tiles[r, 0:1, :]))
            stores.append((packs[1], (2 * c + r, x), tiles[count - 2 + r, 7:8, :]))
    staged([lambda: stores])


def start(source, target, sem):
    pltpu.make_async_copy(source, target, sem).start()


def start_sets(pairs, sem):
    for source, target in pairs:
        for number in range(8):
            start(source(number), target(number), sem)


def arrived(spot, sem):
    pltpu.make_async_copy(spot, spot, sem).wait()


def interior_kernel(last, groups, count, *refs):
    refs = list(refs)
    fields, velocity, speeds = refs[:count], refs[count], refs[count + 1 : count + 3]
    below, above, v_below, v_above = refs[count + 3 : count + 7]
    del refs[: count + 7]
    deposit = None if last else refs.pop(0)
    out = refs.pop(0)
    packs = None if last else (refs.pop(0), refs.pop(0))
    q, u, v, sz, fall, fx, lx, stage, in_sem, out_sem = refs[:10]
    kept = refs[10:12]
    comps, slabs, tiles = q.shape[1], q.shape[2], sz.shape[2]
    chunk, flight = (8, 3) if last else (4, 6)
    chunks = slabs // chunk

    def fetch(j, first, final):
        span = pl.ds(j * chunk, chunk)
        if last:
            middle, low, high = fields
            begin, size = j * chunk, chunk
            if first:
                begin, size = begin + 2, size - 2
                start(low, q.at[0, :, pl.ds(0, 2)], in_sem.at[j, 0])
            if final:
                size -= 2
                start(high, q.at[0, :, pl.ds(slabs - 2, 2)], in_sem.at[j, 0])
            part = pl.ds(begin, size)
            start(middle.at[:, part], q.at[0, :, part], in_sem.at[j, 0])
        else:
            pair = (lambda n: fields[0].at[:, span, n], lambda n: q.at[0, :, span, :, n])
            start_sets([pair], in_sem.at[j, 0])
        for c, target in enumerate((u, v)):
            pair = (lambda n: velocity.at[c, span, n], lambda n: target.at[0, span, :, n])
            start_sets([pair], in_sem.at[j, c + 1])
        for n, (source, target) in enumerate(zip(speeds, (sz, fall))):
            start(source.at[span], target.at[0, span], in_sem.at[j, n + 3])

    for j in range(flight):
        fetch(j, j == 0, False)

    def arrive(j):
        span = pl.ds(j * chunk, chunk)
        arrived(q.at[0, :, span], in_sem.at[j, 0])
        for n, target in enumerate((u, v, sz, fall)):
            arrived(target.at[0, span], in_sem.at[j, n + 1])
        later = j + flight

        @pl.when(later < chunks - 1)
        def _():
            fetch(later, False, False)

        @pl.when(later == chunks - 1)
        def _():
            fetch(chunks - 1, False, True)

        def complete(x, _):
            staged([functools.partial(dust_job, q, 0, x, falling(deposit, x + 2))])
            return 0

        if not last:
            lax.fori_loop(j * chunk, jnp.minimum((j + 1) * chunk, groups), complete, 0)

    f = Slabs(q, u, v, sz, fall, fx, lx, 0, 2, 2, (below, above, v_below, v_above), 2, kept)
    arrive(jnp.int32(0))
    first_face(f)

    def step(k, _):
        @pl.when((k + 4) % chunk == 0)
        def _():
            arrive((k + 4) // chunk)

        def put(c, t, value):
            stage[c, k, t] = value

        slab_step(f, k, put)
        if last:
            start_sets([(lambda n: stage.at[:, k, :, n], lambda n: out.at[:, k + 2, n])], out_sem)
        else:
            start(stage.at[:, k], out.at[:, k + 2], out_sem)
        if not last:
            pack_edges(packs, lambda c: stage.at[c, k], comps, k + 2)
        return 0

    if not last:
        for pack in packs:
            pack[...] = jnp.zeros_like(pack)
    lax.fori_loop(0, slabs - 4, step, 0)
    arrived(stage, out_sem)


def interior(groups, fields, velocity, speeds, below, above, v_below, v_above, deposit=None):
    last = deposit is None
    slabs, tiles, _, lanes = speeds[0].shape
    rows, comps = 8 * tiles, fields[0].shape[0]
    operands = list(fields) + [velocity, *speeds, below, above, v_below, v_above]
    specs = [ANY] * (len(fields) + 3) + [VMEM] * 4
    form = (8, tiles, lanes) if last else (tiles, 8, lanes)
    out_shape = [jax.ShapeDtypeStruct((comps, slabs, *form), jnp.float32)]
    out_specs = [ANY]
    scratch = [
        pltpu.VMEM((1, comps, slabs, tiles, 8, lanes), jnp.float32),
        *[pltpu.VMEM((1, slabs, tiles, 8, lanes), jnp.float32)] * 4,
        pltpu.VMEM((tiles, comps, 8, lanes), jnp.float32),
        pltpu.VMEM((tiles, comps, 8, lanes), jnp.float32),
        pltpu.VMEM((comps, slabs - 4, tiles, 8, lanes), jnp.float32),
        pltpu.SemaphoreType.DMA((slabs // 4, 5)),
        pltpu.SemaphoreType.DMA,
    ]
    scratch += [pltpu.VMEM((tiles, comps, 8, lanes), jnp.float32)] * 2
    if not last:
        out_shape += [jax.ShapeDtypeStruct((2 * comps, slabs, lanes), jnp.float32)] * 2
        out_specs += [VMEM] * 2
        operands.append(deposit)
        specs.append(VMEM)
    cells = comps * (slabs - 4) * rows * lanes
    return pl.pallas_call(
        functools.partial(interior_kernel, last, groups, len(fields)),
        out_shape=tuple(out_shape),
        in_specs=specs,
        out_specs=tuple(out_specs),
        scratch_shapes=scratch,
        compiler_params=params(),
        cost_estimate=cost(40 * cells, 4 * (2 * cells + 4 * slabs * rows * lanes)),
        name="interior",
    )(*operands)


def boundary_kernel(last, groups, slabs, *refs):
    refs = list(refs)
    count = 5 if last else 3
    fields, velocity, speeds = refs[:count], refs[count], refs[count + 1 : count + 3]
    u_outer = refs[count + 3 : count + 5]
    below, above, v_below, v_above = refs[count + 5 : count + 9]
    del refs[: count + 9]
    if last:
        out = refs[1]
        del refs[:2]
    else:
        deposit, packed, ends, packs = refs[0], refs[1:3], refs[3:5], refs[5:7]
        del refs[:7]
    q, u, v, sz, fall, fx, lx, stage, in_sem, out_sem = refs
    comps, tiles = q.shape[1], sz.shape[2]

    if last:
        middle, end_low, end_high, x_low, x_high = fields
        for block, at, source in (
            (0, 0, x_low), (0, 2, end_low), (0, 4, middle.at[:, pl.ds(2, 2)]),
            (1, 0, middle.at[:, pl.ds(slabs - 4, 2)]), (1, 2, end_high), (1, 4, x_high),
        ):
            start(source, q.at[block, :, pl.ds(at, 2)], in_sem.at[block, 0])
    else:
        state, x_low, x_high = fields
        for block, at, first in ((0, 2, 0), (1, 0, slabs - 4)):
            pair = (
                lambda n: state.at[:, pl.ds(first, 4), n], lambda n: q.at[block, :, pl.ds(at, 4), :, n]
            )
            start_sets([pair], in_sem.at[block, 0])
        for block, at, halo in ((0, 0, x_low), (1, 4, x_high)):
            pairs = [
                (lambda n, c=c: halo.at[pl.ds(2 * c, 2), n], lambda n, c=c: q.at[block, c, pl.ds(at, 2), :, n])
                for c in range(comps)
            ]
            start_sets(pairs, in_sem.at[block, 0])
    edge = pl.ds(2 * comps, 1)
    for block in range(2):
        outer, first, at = 3 * block, block * (slabs - 3), 1 - block
        pairs = [
            (lambda n: u_outer[block].at[edge, n], lambda n: u.at[block, pl.ds(outer, 1), :, n]),
            (lambda n: velocity.at[0, pl.ds(first, 3), n], lambda n: u.at[block, pl.ds(at, 3), :, n]),
        ]
        start_sets(pairs, in_sem.at[block, 1])
        span = pl.ds(block * (slabs - 2), 2)
        start_sets([(lambda n: velocity.at[1, span, n], lambda n: v.at[block, :, :, n])], in_sem.at[block, 2])
        for n, target in enumerate((sz, fall)):
            start(speeds[n].at[span], target.at[block], in_sem.at[block, n + 3])
    if not last:
        packs[0][...] = packed[0][...]
        packs[1][...] = packed[1][...]

    def one(block, _):
        begin = block * (slabs - 2)
        arrived(q.at[block], in_sem.at[block, 0])
        for n, target in enumerate((u, v, sz, fall)):
            arrived(target.at[block], in_sem.at[block, n + 1])

        def complete(slab, _):
            x = begin + slab - 2
            lands = (x >= slabs) | ((x >= 0) & (x < groups)) | (x + slabs < groups)

            @pl.when(lands)
            def _():
                staged([functools.partial(dust_job, q, block, slab, falling(deposit, x + 2))])

            return 0

        if not last:
            lax.fori_loop(0, 6, complete, 0)
        f = Slabs(q, u, v, sz, fall, fx, lx, block, 1, 0, (below, above, v_below, v_above), begin)
        first_face(f)

        def step(k, _):
            def put(c, t, value):
                stage[block, c, k, t] = value

            slab_step(f, k, put)
            if not last:
                pack_edges(packs, lambda c: stage.at[block, c, k], comps, begin + k)
            return 0

        lax.fori_loop(0, 2, step, 0)
        if last:
            span = pl.ds(begin, 2)
            pair = (lambda n: stage.at[block, :, :, :, n], lambda n: out.at[:, span, n])
            start_sets([pair], out_sem.at[block])
        else:
            for number in range(2):

                @pl.when(block == number)
                def _():
                    start(stage.at[number], ends[number], out_sem.at[number])

        return 0

    lax.fori_loop(0, 2, one, 0)
    for block in range(2):
        arrived(stage.at[block], out_sem.at[block])


def boundary(groups, fields, velocity, speeds, u_outer, below, above, v_below, v_above, *, deposit=None, packed=None, out=None):
    last = out is not None
    slabs, tiles, _, lanes = speeds[0].shape
    rows, comps = 8 * tiles, fields[0].shape[0]
    operands = list(fields) + [velocity, *speeds, *u_outer, below, above, v_below, v_above]
    specs = [ANY] * (len(fields) + 5) + [VMEM] * 4
    form = (tiles, 8, lanes)
    scratch = [
        pltpu.VMEM((2, comps, 6, tiles, 8, lanes), jnp.float32),
        pltpu.VMEM((2, 4, tiles, 8, lanes), jnp.float32),
        *[pltpu.VMEM((2, 2, tiles, 8, lanes), jnp.float32)] * 3,
        pltpu.VMEM((tiles, comps, 8, lanes), jnp.float32),
        pltpu.VMEM((tiles, comps, 8, lanes), jnp.float32),
        pltpu.VMEM((2, comps, 2, *form), jnp.float32),
        pltpu.SemaphoreType.DMA((2, 5)),
        pltpu.SemaphoreType.DMA((2,)),
    ]
    if last:
        aliases = {len(operands): 0}
        operands.append(out)
        specs.append(ANY)
        out_shape = jax.ShapeDtypeStruct(out.shape, out.dtype)
        out_specs = ANY
    else:
        aliases = {}
        operands += [deposit, *packed]
        specs += [VMEM] * 3
        out_shape = (jax.ShapeDtypeStruct((comps, 2, *form), jnp.float32),) * 2
        out_shape += (jax.ShapeDtypeStruct((2 * comps, slabs, lanes), jnp.float32),) * 2
        out_specs = (ANY, ANY, VMEM, VMEM)
    cells = comps * 4 * rows * lanes
    return pl.pallas_call(
        functools.partial(boundary_kernel, last, groups, slabs),
        out_shape=out_shape,
        in_specs=specs,
        out_specs=out_specs,
        scratch_shapes=scratch,
        input_output_aliases=aliases,
        compiler_params=params(),
        cost_estimate=cost(50 * cells, 4 * 6 * cells),
        name="boundary",
    )(*operands)


def speeds_kernel(velocity, sz, fall, wind, sems):
    step = pl.program_id(0)
    part, count, lanes = sz.shape[0], wind.shape[1], wind.shape[3]
    lane = lax.broadcasted_iota(jnp.int32, (8, lanes), 1)
    is_first, is_last = lane == 0, lane == lanes - 1

    @pl.when(step == 0)
    def _():
        for j in range(wind.shape[0] // part):
            span = pl.ds(j * part, part)
            start_sets([(lambda n: velocity.at[2, span, n], lambda n: wind.at[span, :, n])], sems.at[j])

    arrived(wind.at[pl.ds(step * part, part)], sems.at[step])

    def one(x, _):
        here = [FACTOR * wind[step * part + x, t] for t in range(count)]
        over = [pltpu.roll(tile, lanes - 1, 1) for tile in here]
        under = [pltpu.roll(tile, 1, 1) for tile in here]
        upper = [jnp.where(is_last, jnp.maximum(a, 0.0), a + b) for a, b in zip(here, over)]
        lower = [jnp.where(is_first, jnp.minimum(a, 0.0), a + b) for a, b in zip(here, under)]
        for t in range(count):
            sz[x, t] = upper[t]
            fall[x, t] = lower[t]
        return 0

    lax.fori_loop(0, part, one, 0)


def face_speeds(velocity):
    _, slabs, _, tiles, lanes = velocity.shape
    part = 8
    return pl.pallas_call(
        speeds_kernel,
        grid=(slabs // part,),
        out_shape=(jax.ShapeDtypeStruct((slabs, tiles, 8, lanes), jnp.float32),) * 2,
        in_specs=[ANY],
        out_specs=(pl.BlockSpec((part, tiles, 8, lanes), lambda i: (i, 0, 0, 0)),) * 2,
        scratch_shapes=[
            pltpu.VMEM((slabs, tiles, 8, lanes), jnp.float32),
            pltpu.SemaphoreType.DMA((slabs // part,)),
        ],
        compiler_params=params(),
        cost_estimate=cost(8 * slabs * 8 * tiles * lanes, 12 * slabs * 8 * tiles * lanes),
        name="face_speeds",
    )(velocity)


def x_copies(state, velocity, low, high, sems):
    comps, slabs = state.shape[0], state.shape[1]
    copies = []
    for n, (target, first, edge) in enumerate(((low, 0, 0), (high, slabs - 2, slabs - 1))):
        pairs = [(state.at[c, pl.ds(first, 2)], target.at[pl.ds(2 * c, 2)]) for c in range(comps)]
        pairs.append((velocity.at[0, pl.ds(edge, 1)], target.at[pl.ds(2 * comps, 1)]))
        copies += [pltpu.make_async_copy(*pair, sems.at[n, i]) for i, pair in enumerate(pairs)]
    return copies


def as_column(row):
    count = row.shape[1]
    shape = (count, count)
    same = lax.broadcasted_iota(jnp.int32, shape, 0) == lax.broadcasted_iota(jnp.int32, shape, 1)
    return jnp.sum(jnp.where(same, row, 0.0), axis=1, keepdims=True)


def survey_kernel(
    low_in, high_in, v_low, v_high, wind, state, velocity, low, high, stress, x_low, x_high, gathered, sems,
):
    step, steps = pl.program_id(0), pl.num_programs(0)

    @pl.when(step == 0)
    def _():
        for copy in x_copies(state, velocity, x_low, x_high, sems):
            copy.start()

    comps, part, rows, lanes = low_in.shape[0], wind.shape[1], wind.shape[2], wind.shape[3]
    slabs = stress.shape[0]
    for x in range(part):
        for c in range(comps):
            for r in range(2):
                low[2 * c + r, x : x + 1, :] = low_in[c, x, r : r + 1, :]
                high[2 * c + r, x : x + 1, :] = high_in[c, x, 6 + r : 7 + r, :]
        low[2 * comps, x : x + 1, :] = v_low[0, x, 0:1, :]
        high[2 * comps, x : x + 1, :] = v_high[0, x, 7:8, :]
    lane = lax.broadcasted_iota(jnp.int32, (rows, lanes), 1)
    weight = jnp.zeros((rows, lanes), jnp.float32)
    for level, value in enumerate(profile_weights):
        weight = jnp.where(lane == level, value, weight)
    total = jnp.zeros((rows, lanes), jnp.float32)
    for x in range(part):
        east, north = wind[0, x], wind[1, x]
        friction = jnp.where(lane < LEVELS, weight * (east * east + north * north), 0.0)
        total = total + pltpu.roll(friction, LEVELS * x, 1) if x else friction

    @pl.when(step == 0)
    def _():
        gathered[...] = total

    @pl.when(step > 0)
    def _():
        gathered[...] += pltpu.roll(total, LEVELS * part * step, 1)

    @pl.when(step == steps - 1)
    def _():
        gathered[...] = gathered[...].T
        total = gathered[pl.ds(0, slabs, stride=LEVELS), :]
        for level in range(1, LEVELS):
            total = total + gathered[pl.ds(level, slabs, stride=LEVELS), :]
        stress[...] = total
        for copy in x_copies(state, velocity, x_low, x_high, sems):
            copy.wait()


def survey(state, velocity):
    comps, slabs, rows, lanes = state.shape
    part = 8
    last = rows // 8 - 1
    packed = jax.ShapeDtypeStruct((2 * comps + 1, slabs, lanes), jnp.float32)
    packed_spec = pl.BlockSpec((2 * comps + 1, part, lanes), lambda i: (0, i, 0))
    x_packed = jax.ShapeDtypeStruct((2 * comps + 1, rows, lanes), jnp.float32)
    return pl.pallas_call(
        survey_kernel,
        grid=(slabs // part,),
        out_shape=(packed, packed, jax.ShapeDtypeStruct((slabs, lanes), jnp.float32), x_packed, x_packed),
        in_specs=[
            pl.BlockSpec((comps, part, 8, lanes), lambda i: (0, i, 0, 0)),
            pl.BlockSpec((comps, part, 8, lanes), lambda i: (0, i, last, 0)),
            pl.BlockSpec((1, part, 8, lanes), lambda i: (1, i, 0, 0)),
            pl.BlockSpec((1, part, 8, lanes), lambda i: (1, i, last, 0)),
            pl.BlockSpec((2, part, rows, lanes), lambda i: (0, i, 0, 0)),
            ANY,
            ANY,
        ],
        out_specs=(packed_spec, packed_spec, pl.BlockSpec((slabs, lanes), lambda i: (0, 0)), ANY, ANY),
        scratch_shapes=[pltpu.VMEM((rows, lanes), jnp.float32), pltpu.SemaphoreType.DMA((2, comps + 1))],
        compiler_params=params(),
        cost_estimate=cost(10 * slabs * rows * lanes, 10 * slabs * rows * lanes),
        name="survey",
    )(state, state, velocity, velocity, velocity, state, velocity)


def census_kernel(stress, threshold, tile_owner, parcel_owner, count, share, copies):
    groups, height, lanes = copies.shape
    slabs = stress.shape[0]
    owners = parcel_owner[...].astype(jnp.float32)
    shape = (groups, slabs)
    place = (owners == lax.broadcasted_iota(jnp.int32, shape, 0).astype(jnp.float32)).astype(jnp.float32)
    live = as_column(count[...].astype(jnp.float32))
    shape = (slabs, lanes)
    reach = lax.broadcasted_iota(jnp.int32, shape, 1).astype(jnp.float32) < live
    masses = jnp.where(reach, share[0], 0.0)
    copies[0, 0:slabs] = stress[...]
    copies[0, slabs : slabs + 8] = jnp.zeros((8, lanes), jnp.float32)
    copies[0, slabs : slabs + 1] = threshold[...]
    copies[0, slabs + 1 : slabs + 2, 0:slabs] = tile_owner[...].astype(jnp.float32)
    copies[0, slabs + 8 : height] = jnp.dot(place, masses, precision=HIGHEST, preferred_element_type=jnp.float32)
    whole = copies[0]
    for g in range(1, groups):
        copies[g] = whole


def census(groups, stress, *small):
    slabs, lanes = stress.shape
    return pl.pallas_call(
        census_kernel,
        out_shape=jax.ShapeDtypeStruct((groups, slabs + 8 + groups, lanes), jnp.float32),
        in_specs=[VMEM] * 6,
        out_specs=VMEM,
        compiler_params=params(),
        cost_estimate=cost(10**6, 10**6),
        name="census",
    )(stress, *small)


def deposit_kernel(slabs, me, gathered, low_in, high_in, flux_out, deposit, low, high, flux, dropped):
    groups, lanes = gathered.shape[0], gathered.shape[2]
    here = me[0]
    limits = jnp.concatenate([gathered[g, slabs : slabs + 1] for g in range(groups)], axis=0)
    total = jnp.zeros((groups, lanes), jnp.float32)
    shape = (groups, slabs)
    numbers = lax.broadcasted_iota(jnp.int32, shape, 0).astype(jnp.float32)
    for g in range(groups):
        owners = gathered[g, slabs + 1 : slabs + 2, 0:slabs]
        stress = gathered[g, 0:slabs]
        named = (owners == numbers).astype(jnp.float32)
        limit = lax.dot_general(
            named, limits, (((0,), (0,)), ((), ())), precision=HIGHEST, preferred_element_type=jnp.float32
        )
        lifting = jnp.maximum(stress - limit, 0.0)
        total = total + jnp.dot(named, lifting, precision=HIGHEST, preferred_element_type=jnp.float32)
    flux[...] = total / slabs
    flux_out[...] = flux[pl.ds(here, 1), :]
    dropped[...] = jnp.zeros_like(dropped)
    before, after = jnp.maximum(here - 1, 0), jnp.minimum(here + 1, groups - 1)
    has_before, has_after = here > 0, here < groups - 1
    base = slabs + 8
    for p in range(groups):
        x = p % slabs
        row = flux[p : p + 1, :]
        dropped[x + 2 : x + 3] += row * gathered[p, pl.ds(base + here, 1), :]
        if x >= slabs - 2:
            mass = row * gathered[p, pl.ds(base + before, 1), :]
            dropped[x - slabs + 2 : x - slabs + 3] += jnp.where(has_before, mass, 0.0)
        if x < 2:
            mass = row * gathered[p, pl.ds(base + after, 1), :]
            dropped[x + slabs + 2 : x + slabs + 3] += jnp.where(has_after, mass, 0.0)
    own = dropped[2 : 2 + slabs, :]
    dropped[...] = dropped[...].T
    count = deposit.shape[0]
    tiles = [tile_of(dropped, t, count) for t in range(count)]
    for t, tile in enumerate(tiles):
        deposit[t] = tile
    lane = lax.broadcasted_iota(jnp.int32, (slabs, lanes), 1)
    rows = lanes
    dust = low.shape[0] - 3
    low[...] = low_in[...]
    high[...] = high_in[...]
    for r in range(2):
        low[dust + r] += jnp.where(lane == 0, own[:, r : r + 1], 0.0)
        high[dust + r] += jnp.where(lane == 0, own[:, rows - 2 + r : rows - 1 + r], 0.0)


def settle(me, gathered, low, high, slabs):
    groups, _, lanes = gathered.shape
    edge = jax.ShapeDtypeStruct(low.shape, jnp.float32)
    return pl.pallas_call(
        functools.partial(deposit_kernel, slabs),
        out_shape=(
            jax.ShapeDtypeStruct((1, lanes), jnp.float32),
            jax.ShapeDtypeStruct((lanes // 8, 8, lanes), jnp.float32),
            edge,
            edge,
        ),
        in_specs=[SMEM, VMEM, VMEM, VMEM],
        out_specs=(VMEM, VMEM, VMEM, VMEM),
        scratch_shapes=[
            pltpu.VMEM((groups, lanes), jnp.float32),
            pltpu.VMEM((lanes, lanes), jnp.float32),
        ],
        compiler_params=params(),
        cost_estimate=cost(10**6, 10**6),
        name="settle",
    )(me, gathered, low, high)


def exchange(low, high, axis):
    count = lax.axis_size(axis)
    forward = [(i, i + 1) for i in range(count - 1)]
    backward = [(target, source) for source, target in forward]
    return lax.ppermute(high, axis, forward), lax.ppermute(low, axis, backward)


def shards(state, velocity, threshold, tile_owner, parcel_owner, parcel_count, parcel_share):
    groups = lax.axis_size("gx")
    slabs = state.shape[1]
    me = lax.axis_index("gx").astype(jnp.int32).reshape(1)

    low, high, stress, own_low, own_high = survey(state, velocity)
    copies = census(
        groups, stress, threshold, tile_owner[:, :, 0], parcel_owner[:, :, 0], parcel_count, parcel_share
    )
    rows, lanes = state.shape[2:]

    def sets(array):
        return array.reshape(*array.shape[:-2], 8, rows // 8, lanes)

    velocity = sets(velocity)
    speeds = face_speeds(velocity)
    gathered = lax.all_to_all(copies, "gx", split_axis=0, concat_axis=0, tiled=True)
    flux, deposit, low, high = settle(me, gathered, low, high, slabs)
    below, above = exchange(low, high, "gy")
    own_low, own_high, _ = lax.optimization_barrier((own_low, own_high, gathered))
    x_low, x_high = exchange(own_low, own_high, "gx")
    x_low, x_high = sets(x_low), sets(x_high)
    u_edges = (x_low, x_high)
    middle, pack_low, pack_high = interior(groups, [sets(state)], velocity, speeds, below, above, below, above, deposit)
    end_low, end_high, y_low, y_high = boundary(
        groups, [sets(state), x_low, x_high], velocity, speeds, u_edges, below, above, below, above,
        deposit=deposit, packed=(pack_low, pack_high),
    )
    x2_low, x2_high = exchange(end_low, end_high, "gx")
    below2, above2 = exchange(y_low, y_high, "gy")
    (inside,) = interior(groups, [middle, end_low, end_high], velocity, speeds, below2, above2, below, above)
    fields = boundary(
        groups, [middle, end_low, end_high, x2_low, x2_high], velocity, speeds, u_edges, below2, above2, below, above,
        out=inside,
    )
    return fields.reshape(state.shape), flux


def solution(mesh):
    return jax.shard_map(
        shards,
        mesh=mesh,
        in_specs=(
            P(None, "gx", "gy", None),
            P(None, "gx", "gy", None),
            P("gx", "gy"),
            P("gy", "gx", None),
            P("gy", "gx", None),
            P("gy", "gx"),
            P("gy", "gx", None),
        ),
        out_specs=(P(None, "gx", "gy", None), P("gx", "gy")),
        check_vma=False,
    )
```

```python
import functools

import jax
import jax.numpy as jnp
from jax import lax
from jax.experimental import pallas as pl
from jax.experimental.pallas import tpu as pltpu
from jax.sharding import PartitionSpec as P

LEVELS = 4
profile_weights = (0.4, 0.3, 0.2, 0.1)
time_step = 0.1
FACTOR = 0.25 * time_step

VMEM_LIMIT = 48 * 1024 * 1024
PAIR = 2
GROUP = 8
GATHER = 4
HIGHEST = lax.Precision.HIGHEST
ANY = pl.BlockSpec(memory_space=pl.ANY)
VMEM = pl.BlockSpec(memory_space=pltpu.VMEM)
SMEM = pl.BlockSpec(memory_space=pltpu.SMEM)


def params():
    return pltpu.CompilerParams(vmem_limit_bytes=VMEM_LIMIT)


def cost(flops, moved):
    return pl.CostEstimate(flops=int(flops), bytes_accessed=int(moved), transcendentals=0)


def minmod(a, b):
    return jnp.maximum(jnp.minimum(a, b), jnp.minimum(jnp.maximum(a, b), 0.0))


def tile_of(ref, t, tiles):
    return ref[pl.ds(t, 8, stride=tiles), :]


class Slabs:
    def __init__(self, q, uv, sz, fall, fx, lx, block, x_at, at, halo, x, kept=None):
        self.q, self.uv, self.sz, self.falls, self.fx, self.lx = q, uv, sz, fall, fx, lx
        self.block, self.x_at, self.at, self.kept = block, x_at, at, kept
        self.halo, self.x = halo, x
        self.comps, self.tiles, self.lanes = q.shape[1], sz.shape[2], q.shape[-1]

    def field(self, c, slab, t):
        return self.q[self.block, c, slab, t]

    def row(self, k, which, number):
        return self.halo[which][number, pl.ds(self.x + k, 1), :]

    def centre(self, c, k, t):
        slab = k + 2
        if 0 <= t < self.tiles:
            return self.field(c, slab, t)
        row = lax.broadcasted_iota(jnp.int32, (8, self.lanes), 0)
        if t < 0:
            moved = pltpu.roll(self.field(c, slab, t + self.tiles), 1, 0)
            return jnp.where(row == 0, self.row(k, 0, 2 * c + t + 2), moved)
        t -= self.tiles
        return jnp.where(row == 7, self.row(k, 1, 2 * c + t), pltpu.roll(self.field(c, slab, t), 7, 0))

    def east(self, k, t):
        here = k + self.x_at
        return FACTOR * (self.uv[self.block, 0, here, t] + self.uv[self.block, 0, here + 1, t])

    def wind(self, k, t):
        inner = self.uv[self.block, 1, k + self.x_at, t % self.tiles]
        if 0 <= t < self.tiles:
            return inner
        row = lax.broadcasted_iota(jnp.int32, (8, self.lanes), 0)
        end, turn, which = (0, 1, 2) if t < 0 else (7, 7, 3)
        return jnp.where(row == end, self.row(k, which, 2 * self.comps), pltpu.roll(inner, turn, 0))

    def north(self, k, t):
        return FACTOR * (self.wind(k, t) + self.wind(k, t + 1))

    def up(self, k, t):
        return self.sz[self.block, k + self.at, t]

    def down(self, k, t):
        return self.falls[self.block, k + self.at, t]


def each(function, *lists):
    return [function(*items) for items in zip(*lists)]


def minmods(a, b):
    low, high = each(jnp.minimum, a, b), each(jnp.maximum, a, b)
    high = each(lambda x: jnp.minimum(x, 0.0), high)
    return each(jnp.maximum, low, high)


def difference(a, b):
    return each(lambda x, y: x - y, a, b)


def total_of(a, b):
    return each(lambda x, y: x + y, a, b)


def face_flux(speeds, masks, low_side, high_side):
    picked = each(jnp.where, masks, low_side, high_side)
    return each(lambda x, y: x * y, speeds, picked)


def staged(jobs):
    waiting = []
    for job in jobs:
        stores = job()
        for ref, index, value in waiting:
            ref[index] = value
        waiting = stores
    for ref, index, value in waiting:
        ref[index] = value


def first_face(f):
    def job(ts):
        spots = [(t, c) for t in ts for c in range(f.comps)]
        speeds = {t: f.east(-1, t) for t in ts}
        masks = {t: speeds[t] > 0 for t in ts}
        a, b, q0, q1 = [[f.field(c, slab, t) for t, c in spots] for slab in range(4)]
        middle = difference(q0, b)
        left = total_of(total_of(b, b), minmods(middle, difference(b, a)))
        slope = minmods(difference(q1, q0), middle)
        twice = total_of(q0, q0)
        flux = face_flux([speeds[t] for t, _ in spots], [masks[t] for t, _ in spots], left, difference(twice, slope))
        stores = [(f.fx, spot, x) for spot, x in zip(spots, flux)]
        if f.kept is not None:
            stores += [(f.kept[0], spot, x) for spot, x in zip(spots, twice)]
            stores += [(f.kept[1], spot, x) for spot, x in zip(spots, difference(q1, q0))]
        return stores + [(f.lx, spot, x) for spot, x in zip(spots, total_of(twice, slope))]

    staged([functools.partial(job, range(t, t + PAIR)) for t in range(0, f.tiles, PAIR)])


def slab_step(f, k, put):
    slab = k + 2
    lane = lax.broadcasted_iota(jnp.int32, (8, f.lanes), 1)
    top = f.lanes - 1
    is_first, is_last = lane == 0, lane == top
    carry = []
    speed = f.north(k, -1)
    for c in range(f.comps):
        a, b, q0, q1 = [f.centre(c, k, t) for t in (-2, -1, 0, 1)]
        middle, ahead = q0 - b, q1 - q0
        left_state = (b + b) + minmod(middle, b - a)
        slope = minmod(ahead, middle)
        twice = q0 + q0
        flux = speed * jnp.where(speed > 0, left_state, twice - slope)
        carry.append((q0, q1, ahead, twice, twice + slope, flux))
    states, doubles = {}, {}

    def vertical(t):
        for c in range(f.comps):
            q0 = f.field(c, slab, t)
            over = jnp.where(is_last, 0.0, pltpu.roll(q0, top, 1))
            under = jnp.where(is_first, 0.0, pltpu.roll(q0, 1, 1))
            slope = minmod(over - q0, q0 - under)
            if f.kept is not None:
                doubles[c, t] = f.kept[0][t, c]
            twice = double(c, t, q0)
            states[t, c] = (twice - slope, twice + slope)

    def flush(held):
        for c, t, flux_x, left_x, twice_x, step_x, value in held:
            f.fx[t, c], f.lx[t, c] = flux_x, left_x
            if f.kept is not None:
                f.kept[0][t, c], f.kept[1][t, c] = twice_x, step_x
            put(c, t, value)

    def double(c, t, tile):
        if f.kept is None or not 0 <= t < f.tiles:
            return tile + tile
        return doubles[c, t]

    held = []
    for t in range(GROUP):
        vertical(t)
    for begin in range(0, f.tiles, GROUP):
        group = range(begin, min(begin + GROUP, f.tiles))
        for t in range(begin + GROUP, min(begin + 2 * GROUP, f.tiles)):
            vertical(t)
        loaded = {}
        for t in group:
            loaded[t] = (f.east(k, t), f.north(k, t), f.up(k, t), f.down(k, t))
            for c in range(f.comps):
                loaded[t, c] = (
                    f.centre(c, k, t + 2), f.field(c, slab + 1, t), f.field(c, slab + 2, t),
                    f.fx[t, c], f.lx[t, c], f.kept[1][t, c] if f.kept is not None else None,
                )
        flush(held)
        held = []
        for t in group:
            speed_x, speed_y, speed_z, fall = loaded[t]
            go_x, go_y, go_z, go_fall = speed_x > 0, speed_y > 0, speed_z > 0, fall > 0
            for c in range(f.comps):
                y2, x1, x2, flux_w, left_w, step_w = loaded[t, c]
                q0, y1, ahead, twice, left_y, flux_y = carry[c]
                beyond = y2 - y1
                slope = minmod(beyond, ahead)
                twice_y = double(c, t + 1, y1)
                flux_next = speed_y * jnp.where(go_y, left_y, twice_y - slope)
                total = flux_next - flux_y
                carry[c] = (y1, y2, beyond, twice_y, twice_y + slope, flux_next)
                step_x = x2 - x1
                slope = minmod(step_x, x1 - q0 if step_w is None else step_w)
                twice_x = x1 + x1
                flux_x = speed_x * jnp.where(go_x, left_w, twice_x - slope)
                left_x = twice_x + slope
                total = total + (flux_x - flux_w)
                lower, upper = states[t, c]
                flux_z = speed_z * jnp.where(go_z, upper, pltpu.roll(lower, top, 1))
                flux_below = fall * jnp.where(go_fall, pltpu.roll(upper, 1, 1), lower)
                total = total + (flux_z - flux_below)
                held.append((c, t, flux_x, left_x, twice_x, step_x, q0 - total))
    flush(held)


def dust_job(q, block, slab, dust):
    c, spots = q.shape[1] - 1, range(q.shape[3])
    tiles = total_of([q[block, c, slab, t] for t in spots], dust(spots))
    return [(q, (block, c, slab, t), tile) for t, tile in zip(spots, tiles)]


def falling(deposit, column):
    lanes = deposit.shape[-1]

    def dust(spots):
        parts = [pltpu.roll(deposit[t], lanes - column, 1) for t in spots]
        lane = lax.broadcasted_iota(jnp.int32, parts[0].shape, 1)
        return [jnp.where(lane == 0, part, 0.0) for part in parts]

    return dust


def pack_edges(packs, stage_slab, comps, x):
    x = pl.ds(x, 1)
    stores = []
    for c in range(comps):
        tiles = stage_slab(c)
        count = tiles.shape[0]
        for r in range(2):
            stores.append((packs[0], (2 * c + r, x), tiles[r, 0:1, :]))
            stores.append((packs[1], (2 * c + r, x), tiles[count - 2 + r, 7:8, :]))
    staged([lambda: stores])


def start(source, target, sem):
    pltpu.make_async_copy(source, target, sem).start()


def start_sets(pairs, sem):
    for source, target in pairs:
        for number in range(8):
            start(source(number), target(number), sem)


def arrived(spot, sem):
    pltpu.make_async_copy(spot, spot, sem).wait()


def interior_kernel(last, groups, count, *refs):
    refs = list(refs)
    fields, velocity, speeds = refs[:count], refs[count], refs[count + 1 : count + 3]
    below, above, v_below, v_above = refs[count + 3 : count + 7]
    del refs[: count + 7]
    deposit = None if last else refs.pop(0)
    out = refs.pop(0)
    packs = None if last else (refs.pop(0), refs.pop(0))
    q, uv, sz, fall, fx, lx, stage, in_sem, out_sem = refs[:9]
    kept = refs[9:11]
    comps, slabs, tiles = q.shape[1], q.shape[2], sz.shape[2]
    chunk, flight = 8, 3
    chunks = slabs // chunk

    def fetch(j, first, final):
        span = pl.ds(j * chunk, chunk)
        if last:
            middle, low, high = fields
            begin, size = j * chunk, chunk
            if first:
                begin, size = begin + 2, size - 2
                start(low, q.at[0, :, pl.ds(0, 2)], in_sem.at[j, 0])
            if final:
                size -= 2
                start(high, q.at[0, :, pl.ds(slabs - 2, 2)], in_sem.at[j, 0])
            part = pl.ds(begin, size)
            start(middle.at[:, part], q.at[0, :, part], in_sem.at[j, 0])
        else:
            pair = (lambda n: fields[0].at[:, span, n], lambda n: q.at[0, :, span, :, n])
            start_sets([pair], in_sem.at[j, 0])
        pair = (lambda n: velocity.at[pl.ds(0, 2), span, n], lambda n: uv.at[0, :, span, :, n])
        start_sets([pair], in_sem.at[j, 1])
        for n, (source, target) in enumerate(zip(speeds, (sz, fall))):
            start(source.at[span], target.at[0, span], in_sem.at[j, n + 2])

    for j in range(flight):
        fetch(j, j == 0, False)

    def arrive(j):
        span = pl.ds(j * chunk, chunk)
        arrived(q.at[0, :, span], in_sem.at[j, 0])
        for n, spot in enumerate((uv.at[0, :, span], sz.at[0, span], fall.at[0, span])):
            arrived(spot, in_sem.at[j, n + 1])
        later = j + flight

        @pl.when(later < chunks - 1)
        def _():
            fetch(later, False, False)

        @pl.when(later == chunks - 1)
        def _():
            fetch(chunks - 1, False, True)

        def complete(x, _):
            staged([functools.partial(dust_job, q, 0, x, falling(deposit, x + 2))])
            return 0

        if not last:
            lax.fori_loop(j * chunk, jnp.minimum((j + 1) * chunk, groups), complete, 0)

    f = Slabs(q, uv, sz, fall, fx, lx, 0, 2, 2, (below, above, v_below, v_above), 2, kept)
    arrive(jnp.int32(0))
    first_face(f)

    def step(k, _):
        @pl.when((k + 4) % chunk == 0)
        def _():
            arrive((k + 4) // chunk)

        def put(c, t, value):
            stage[c, k, t] = value

        slab_step(f, k, put)
        if last:

            @pl.when((k + 1) % GATHER == 0)
            def _():
                first = k + 1 - GATHER
                source, target = pl.ds(first, GATHER), pl.ds(first + 2, GATHER)
                start_sets([(lambda n: stage.at[:, source, :, n], lambda n: out.at[:, target, n])], out_sem)

        else:
            start(stage.at[:, k], out.at[:, k + 2], out_sem)
        if not last:
            pack_edges(packs, lambda c: stage.at[c, k], comps, k + 2)
        return 0

    if not last:
        for pack in packs:
            pack[...] = jnp.zeros_like(pack)
    lax.fori_loop(0, slabs - 4, step, 0)
    arrived(stage, out_sem)


def interior(groups, fields, velocity, speeds, below, above, v_below, v_above, deposit=None):
    last = deposit is None
    slabs, tiles, _, lanes = speeds[0].shape
    rows, comps = 8 * tiles, fields[0].shape[0]
    operands = list(fields) + [velocity, *speeds, below, above, v_below, v_above]
    specs = [ANY] * (len(fields) + 3) + [VMEM] * 4
    form = (8, tiles, lanes) if last else (tiles, 8, lanes)
    out_shape = [jax.ShapeDtypeStruct((comps, slabs, *form), jnp.float32)]
    out_specs = [ANY]
    scratch = [
        pltpu.VMEM((1, comps, slabs, tiles, 8, lanes), jnp.float32),
        pltpu.VMEM((1, 2, slabs, tiles, 8, lanes), jnp.float32),
        *[pltpu.VMEM((1, slabs, tiles, 8, lanes), jnp.float32)] * 2,
        pltpu.VMEM((tiles, comps, 8, lanes), jnp.float32),
        pltpu.VMEM((tiles, comps, 8, lanes), jnp.float32),
        pltpu.VMEM((comps, slabs - 4, tiles, 8, lanes), jnp.float32),
        pltpu.SemaphoreType.DMA((slabs // 4, 5)),
        pltpu.SemaphoreType.DMA,
    ]
    scratch += [pltpu.VMEM((tiles, comps, 8, lanes), jnp.float32)] * 2
    if not last:
        out_shape += [jax.ShapeDtypeStruct((2 * comps, slabs, lanes), jnp.float32)] * 2
        out_specs += [VMEM] * 2
        operands.append(deposit)
        specs.append(VMEM)
    cells = comps * (slabs - 4) * rows * lanes
    return pl.pallas_call(
        functools.partial(interior_kernel, last, groups, len(fields)),
        out_shape=tuple(out_shape),
        in_specs=specs,
        out_specs=tuple(out_specs),
        scratch_shapes=scratch,
        compiler_params=params(),
        cost_estimate=cost(40 * cells, 4 * (2 * cells + 4 * slabs * rows * lanes)),
        name="interior",
    )(*operands)


def boundary_kernel(last, groups, slabs, *refs):
    refs = list(refs)
    count = 5 if last else 3
    fields, velocity, speeds = refs[:count], refs[count], refs[count + 1 : count + 3]
    u_outer = refs[count + 3 : count + 5]
    below, above, v_below, v_above = refs[count + 5 : count + 9]
    del refs[: count + 9]
    if last:
        out = refs[1]
        del refs[:2]
    else:
        deposit, packed, ends, packs = refs[0], refs[1:3], refs[3:5], refs[5:7]
        del refs[:7]
    q, uv, sz, fall, fx, lx, stage, in_sem, out_sem = refs
    comps, tiles = q.shape[1], sz.shape[2]

    if last:
        middle, end_low, end_high, x_low, x_high = fields
        for block, at, source in (
            (0, 0, x_low), (0, 2, end_low), (0, 4, middle.at[:, pl.ds(2, 2)]),
            (1, 0, middle.at[:, pl.ds(slabs - 4, 2)]), (1, 2, end_high), (1, 4, x_high),
        ):
            start(source, q.at[block, :, pl.ds(at, 2)], in_sem.at[block, 0])
    else:
        state, x_low, x_high = fields
        for block, at, first in ((0, 2, 0), (1, 0, slabs - 4)):
            pair = (
                lambda n: state.at[:, pl.ds(first, 4), n], lambda n: q.at[block, :, pl.ds(at, 4), :, n]
            )
            start_sets([pair], in_sem.at[block, 0])
        for block, at, halo in ((0, 0, x_low), (1, 4, x_high)):
            pairs = [
                (lambda n, c=c: halo.at[pl.ds(2 * c, 2), n], lambda n, c=c: q.at[block, c, pl.ds(at, 2), :, n])
                for c in range(comps)
            ]
            start_sets(pairs, in_sem.at[block, 0])
    edge = pl.ds(2 * comps, 1)
    for block in range(2):
        outer, first, at = 3 * block, block * (slabs - 3), 1 - block
        pairs = [
            (lambda n: u_outer[block].at[edge, n], lambda n: uv.at[block, 0, pl.ds(outer, 1), :, n]),
            (
                lambda n: velocity.at[pl.ds(0, 2), pl.ds(first, 3), n],
                lambda n: uv.at[block, :, pl.ds(at, 3), :, n],
            ),
        ]
        for number, pair in enumerate(pairs):
            start_sets([pair], in_sem.at[block, number + 1])
        span = pl.ds(block * (slabs - 2), 2)
        for n, target in enumerate((sz, fall)):
            start(speeds[n].at[span], target.at[block], in_sem.at[block, n + 3])
    if not last:
        packs[0][...] = packed[0][...]
        packs[1][...] = packed[1][...]

    def one(block, _):
        begin = block * (slabs - 2)
        arrived(q.at[block], in_sem.at[block, 0])
        spots = (uv.at[block, 0, pl.ds(0, 1)], uv.at[block, :, pl.ds(0, 3)], sz.at[block], fall.at[block])
        for n, spot in enumerate(spots):
            arrived(spot, in_sem.at[block, n + 1])

        def complete(slab, _):
            x = begin + slab - 2
            lands = (x >= slabs) | ((x >= 0) & (x < groups)) | (x + slabs < groups)

            @pl.when(lands)
            def _():
                staged([functools.partial(dust_job, q, block, slab, falling(deposit, x + 2))])

            return 0

        if not last:
            lax.fori_loop(0, 6, complete, 0)
        f = Slabs(q, uv, sz, fall, fx, lx, block, 1, 0, (below, above, v_below, v_above), begin)
        first_face(f)

        def step(k, _):
            def put(c, t, value):
                stage[block, c, k, t] = value

            slab_step(f, k, put)
            if not last:
                pack_edges(packs, lambda c: stage.at[block, c, k], comps, begin + k)
            return 0

        lax.fori_loop(0, 2, step, 0)
        if last:
            span = pl.ds(begin, 2)
            pair = (lambda n: stage.at[block, :, :, :, n], lambda n: out.at[:, span, n])
            start_sets([pair], out_sem.at[block])
        else:
            for number in range(2):

                @pl.when(block == number)
                def _():
                    start(stage.at[number], ends[number], out_sem.at[number])

        return 0

    lax.fori_loop(0, 2, one, 0)
    for block in range(2):
        arrived(stage.at[block], out_sem.at[block])


def boundary(groups, fields, velocity, speeds, u_outer, below, above, v_below, v_above, *, deposit=None, packed=None, out=None):
    last = out is not None
    slabs, tiles, _, lanes = speeds[0].shape
    rows, comps = 8 * tiles, fields[0].shape[0]
    operands = list(fields) + [velocity, *speeds, *u_outer, below, above, v_below, v_above]
    specs = [ANY] * (len(fields) + 5) + [VMEM] * 4
    form = (tiles, 8, lanes)
    scratch = [
        pltpu.VMEM((2, comps, 6, tiles, 8, lanes), jnp.float32),
        pltpu.VMEM((2, 2, 4, tiles, 8, lanes), jnp.float32),
        *[pltpu.VMEM((2, 2, tiles, 8, lanes), jnp.float32)] * 2,
        pltpu.VMEM((tiles, comps, 8, lanes), jnp.float32),
        pltpu.VMEM((tiles, comps, 8, lanes), jnp.float32),
        pltpu.VMEM((2, comps, 2, *form), jnp.float32),
        pltpu.SemaphoreType.DMA((2, 5)),
        pltpu.SemaphoreType.DMA((2,)),
    ]
    if last:
        aliases = {len(operands): 0}
        operands.append(out)
        specs.append(ANY)
        out_shape = jax.ShapeDtypeStruct(out.shape, out.dtype)
        out_specs = ANY
    else:
        aliases = {}
        operands += [deposit, *packed]
        specs += [VMEM] * 3
        out_shape = (jax.ShapeDtypeStruct((comps, 2, *form), jnp.float32),) * 2
        out_shape += (jax.ShapeDtypeStruct((2 * comps, slabs, lanes), jnp.float32),) * 2
        out_specs = (ANY, ANY, VMEM, VMEM)
    cells = comps * 4 * rows * lanes
    return pl.pallas_call(
        functools.partial(boundary_kernel, last, groups, slabs),
        out_shape=out_shape,
        in_specs=specs,
        out_specs=out_specs,
        scratch_shapes=scratch,
        input_output_aliases=aliases,
        compiler_params=params(),
        cost_estimate=cost(50 * cells, 4 * 6 * cells),
        name="boundary",
    )(*operands)


def speeds_kernel(velocity, sz, fall, wind, sems):
    step = pl.program_id(0)
    part, count, lanes = sz.shape[0], wind.shape[1], wind.shape[3]
    lane = lax.broadcasted_iota(jnp.int32, (8, lanes), 1)
    is_first, is_last = lane == 0, lane == lanes - 1

    @pl.when(step == 0)
    def _():
        for j in range(wind.shape[0] // part):
            span = pl.ds(j * part, part)
            start_sets([(lambda n: velocity.at[2, span, n], lambda n: wind.at[span, :, n])], sems.at[j])

    arrived(wind.at[pl.ds(step * part, part)], sems.at[step])

    def one(x, _):
        here = [FACTOR * wind[step * part + x, t] for t in range(count)]
        over = [pltpu.roll(tile, lanes - 1, 1) for tile in here]
        under = [pltpu.roll(tile, 1, 1) for tile in here]
        upper = [jnp.where(is_last, jnp.maximum(a, 0.0), a + b) for a, b in zip(here, over)]
        lower = [jnp.where(is_first, jnp.minimum(a, 0.0), a + b) for a, b in zip(here, under)]
        for t in range(count):
            sz[x, t] = upper[t]
            fall[x, t] = lower[t]
        return 0

    lax.fori_loop(0, part, one, 0)


def face_speeds(velocity):
    _, slabs, _, tiles, lanes = velocity.shape
    part = 8
    return pl.pallas_call(
        speeds_kernel,
        grid=(slabs // part,),
        out_shape=(jax.ShapeDtypeStruct((slabs, tiles, 8, lanes), jnp.float32),) * 2,
        in_specs=[ANY],
        out_specs=(pl.BlockSpec((part, tiles, 8, lanes), lambda i: (i, 0, 0, 0)),) * 2,
        scratch_shapes=[
            pltpu.VMEM((slabs, tiles, 8, lanes), jnp.float32),
            pltpu.SemaphoreType.DMA((slabs // part,)),
        ],
        compiler_params=params(),
        cost_estimate=cost(8 * slabs * 8 * tiles * lanes, 12 * slabs * 8 * tiles * lanes),
        name="face_speeds",
    )(velocity)


def x_copies(state, velocity, low, high, sems):
    comps, slabs = state.shape[0], state.shape[1]
    copies = []
    for n, (target, first, edge) in enumerate(((low, 0, 0), (high, slabs - 2, slabs - 1))):
        pairs = [(state.at[c, pl.ds(first, 2)], target.at[pl.ds(2 * c, 2)]) for c in range(comps)]
        pairs.append((velocity.at[0, pl.ds(edge, 1)], target.at[pl.ds(2 * comps, 1)]))
        copies += [pltpu.make_async_copy(*pair, sems.at[n, i]) for i, pair in enumerate(pairs)]
    return copies


def as_column(row):
    count = row.shape[1]
    shape = (count, count)
    same = lax.broadcasted_iota(jnp.int32, shape, 0) == lax.broadcasted_iota(jnp.int32, shape, 1)
    return jnp.sum(jnp.where(same, row, 0.0), axis=1, keepdims=True)


def survey_kernel(
    low_in, high_in, v_low, v_high, wind, state, velocity, low, high, stress, x_low, x_high, gathered, sems,
):
    step, steps = pl.program_id(0), pl.num_programs(0)

    @pl.when(step == 0)
    def _():
        for copy in x_copies(state, velocity, x_low, x_high, sems):
            copy.start()

    comps, part, rows, lanes = low_in.shape[0], wind.shape[1], wind.shape[2], wind.shape[3]
    slabs = stress.shape[0]
    for x in range(part):
        for c in range(comps):
            for r in range(2):
                low[2 * c + r, x : x + 1, :] = low_in[c, x, r : r + 1, :]
                high[2 * c + r, x : x + 1, :] = high_in[c, x, 6 + r : 7 + r, :]
        low[2 * comps, x : x + 1, :] = v_low[0, x, 0:1, :]
        high[2 * comps, x : x + 1, :] = v_high[0, x, 7:8, :]
    lane = lax.broadcasted_iota(jnp.int32, (rows, lanes), 1)
    weight = jnp.zeros((rows, lanes), jnp.float32)
    for level, value in enumerate(profile_weights):
        weight = jnp.where(lane == level, value, weight)
    total = jnp.zeros((rows, lanes), jnp.float32)
    for x in range(part):
        east, north = wind[0, x], wind[1, x]
        friction = jnp.where(lane < LEVELS, weight * (east * east + north * north), 0.0)
        total = total + pltpu.roll(friction, LEVELS * x, 1) if x else friction

    @pl.when(step == 0)
    def _():
        gathered[...] = total

    @pl.when(step > 0)
    def _():
        gathered[...] += pltpu.roll(total, LEVELS * part * step, 1)

    @pl.when(step == steps - 1)
    def _():
        gathered[...] = gathered[...].T
        total = gathered[pl.ds(0, slabs, stride=LEVELS), :]
        for level in range(1, LEVELS):
            total = total + gathered[pl.ds(level, slabs, stride=LEVELS), :]
        stress[...] = total
        for copy in x_copies(state, velocity, x_low, x_high, sems):
            copy.wait()


def survey(state, velocity):
    comps, slabs, rows, lanes = state.shape
    part = 8
    last = rows // 8 - 1
    packed = jax.ShapeDtypeStruct((2 * comps + 1, slabs, lanes), jnp.float32)
    packed_spec = pl.BlockSpec((2 * comps + 1, part, lanes), lambda i: (0, i, 0))
    x_packed = jax.ShapeDtypeStruct((2 * comps + 1, rows, lanes), jnp.float32)
    return pl.pallas_call(
        survey_kernel,
        grid=(slabs // part,),
        out_shape=(packed, packed, jax.ShapeDtypeStruct((slabs, lanes), jnp.float32), x_packed, x_packed),
        in_specs=[
            pl.BlockSpec((comps, part, 8, lanes), lambda i: (0, i, 0, 0)),
            pl.BlockSpec((comps, part, 8, lanes), lambda i: (0, i, last, 0)),
            pl.BlockSpec((1, part, 8, lanes), lambda i: (1, i, 0, 0)),
            pl.BlockSpec((1, part, 8, lanes), lambda i: (1, i, last, 0)),
            pl.BlockSpec((2, part, rows, lanes), lambda i: (0, i, 0, 0)),
            ANY,
            ANY,
        ],
        out_specs=(packed_spec, packed_spec, pl.BlockSpec((slabs, lanes), lambda i: (0, 0)), ANY, ANY),
        scratch_shapes=[pltpu.VMEM((rows, lanes), jnp.float32), pltpu.SemaphoreType.DMA((2, comps + 1))],
        compiler_params=params(),
        cost_estimate=cost(10 * slabs * rows * lanes, 10 * slabs * rows * lanes),
        name="survey",
    )(state, state, velocity, velocity, velocity, state, velocity)


def census_kernel(stress, threshold, tile_owner, parcel_owner, count, share, copies):
    groups, height, lanes = copies.shape
    slabs = stress.shape[0]
    owners = parcel_owner[...].astype(jnp.float32)
    shape = (groups, slabs)
    place = (owners == lax.broadcasted_iota(jnp.int32, shape, 0).astype(jnp.float32)).astype(jnp.float32)
    live = as_column(count[...].astype(jnp.float32))
    shape = (slabs, lanes)
    reach = lax.broadcasted_iota(jnp.int32, shape, 1).astype(jnp.float32) < live
    masses = jnp.where(reach, share[0], 0.0)
    copies[0, 0:slabs] = stress[...]
    copies[0, slabs : slabs + 8] = jnp.zeros((8, lanes), jnp.float32)
    copies[0, slabs : slabs + 1] = threshold[...]
    copies[0, slabs + 1 : slabs + 2, 0:slabs] = tile_owner[...].astype(jnp.float32)
    copies[0, slabs + 8 : height] = jnp.dot(place, masses, precision=HIGHEST, preferred_element_type=jnp.float32)
    whole = copies[0]
    for g in range(1, groups):
        copies[g] = whole


def census(groups, stress, *small):
    slabs, lanes = stress.shape
    return pl.pallas_call(
        census_kernel,
        out_shape=jax.ShapeDtypeStruct((groups, slabs + 8 + groups, lanes), jnp.float32),
        in_specs=[VMEM] * 6,
        out_specs=VMEM,
        compiler_params=params(),
        cost_estimate=cost(10**6, 10**6),
        name="census",
    )(stress, *small)


def deposit_kernel(slabs, me, gathered, low_in, high_in, flux_out, deposit, low, high, flux, dropped):
    groups, lanes = gathered.shape[0], gathered.shape[2]
    here = me[0]
    limits = jnp.concatenate([gathered[g, slabs : slabs + 1] for g in range(groups)], axis=0)
    total = jnp.zeros((groups, lanes), jnp.float32)
    shape = (groups, slabs)
    numbers = lax.broadcasted_iota(jnp.int32, shape, 0).astype(jnp.float32)
    for g in range(groups):
        owners = gathered[g, slabs + 1 : slabs + 2, 0:slabs]
        stress = gathered[g, 0:slabs]
        named = (owners == numbers).astype(jnp.float32)
        limit = lax.dot_general(
            named, limits, (((0,), (0,)), ((), ())), precision=HIGHEST, preferred_element_type=jnp.float32
        )
        lifting = jnp.maximum(stress - limit, 0.0)
        total = total + jnp.dot(named, lifting, precision=HIGHEST, preferred_element_type=jnp.float32)
    flux[...] = total / slabs
    flux_out[...] = flux[pl.ds(here, 1), :]
    dropped[...] = jnp.zeros_like(dropped)
    before, after = jnp.maximum(here - 1, 0), jnp.minimum(here + 1, groups - 1)
    has_before, has_after = here > 0, here < groups - 1
    base = slabs + 8
    for p in range(groups):
        x = p % slabs
        row = flux[p : p + 1, :]
        dropped[x + 2 : x + 3] += row * gathered[p, pl.ds(base + here, 1), :]
        if x >= slabs - 2:
            mass = row * gathered[p, pl.ds(base + before, 1), :]
            dropped[x - slabs + 2 : x - slabs + 3] += jnp.where(has_before, mass, 0.0)
        if x < 2:
            mass = row * gathered[p, pl.ds(base + after, 1), :]
            dropped[x + slabs + 2 : x + slabs + 3] += jnp.where(has_after, mass, 0.0)
    own = dropped[2 : 2 + slabs, :]
    dropped[...] = dropped[...].T
    count = deposit.shape[0]
    tiles = [tile_of(dropped, t, count) for t in range(count)]
    for t, tile in enumerate(tiles):
        deposit[t] = tile
    lane = lax.broadcasted_iota(jnp.int32, (slabs, lanes), 1)
    rows = lanes
    dust = low.shape[0] - 3
    low[...] = low_in[...]
    high[...] = high_in[...]
    for r in range(2):
        low[dust + r] += jnp.where(lane == 0, own[:, r : r + 1], 0.0)
        high[dust + r] += jnp.where(lane == 0, own[:, rows - 2 + r : rows - 1 + r], 0.0)


def settle(me, gathered, low, high, slabs):
    groups, _, lanes = gathered.shape
    edge = jax.ShapeDtypeStruct(low.shape, jnp.float32)
    return pl.pallas_call(
        functools.partial(deposit_kernel, slabs),
        out_shape=(
            jax.ShapeDtypeStruct((1, lanes), jnp.float32),
            jax.ShapeDtypeStruct((lanes // 8, 8, lanes), jnp.float32),
            edge,
            edge,
        ),
        in_specs=[SMEM, VMEM, VMEM, VMEM],
        out_specs=(VMEM, VMEM, VMEM, VMEM),
        scratch_shapes=[
            pltpu.VMEM((groups, lanes), jnp.float32),
            pltpu.VMEM((lanes, lanes), jnp.float32),
        ],
        compiler_params=params(),
        cost_estimate=cost(10**6, 10**6),
        name="settle",
    )(me, gathered, low, high)


def exchange(low, high, axis):
    count = lax.axis_size(axis)
    forward = [(i, i + 1) for i in range(count - 1)]
    backward = [(target, source) for source, target in forward]
    return lax.ppermute(high, axis, forward), lax.ppermute(low, axis, backward)


def shards(state, velocity, threshold, tile_owner, parcel_owner, parcel_count, parcel_share):
    groups = lax.axis_size("gx")
    slabs = state.shape[1]
    me = lax.axis_index("gx").astype(jnp.int32).reshape(1)

    low, high, stress, own_low, own_high = survey(state, velocity)
    copies = census(
        groups, stress, threshold, tile_owner[:, :, 0], parcel_owner[:, :, 0], parcel_count, parcel_share
    )
    rows, lanes = state.shape[2:]

    def sets(array):
        return array.reshape(*array.shape[:-2], 8, rows // 8, lanes)

    velocity = sets(velocity)
    speeds = face_speeds(velocity)
    gathered = lax.all_to_all(copies, "gx", split_axis=0, concat_axis=0, tiled=True)
    flux, deposit, low, high = settle(me, gathered, low, high, slabs)
    below, above = exchange(low, high, "gy")
    own_low, own_high, _ = lax.optimization_barrier((own_low, own_high, gathered))
    x_low, x_high = exchange(own_low, own_high, "gx")
    x_low, x_high = sets(x_low), sets(x_high)
    u_edges = (x_low, x_high)
    middle, pack_low, pack_high = interior(groups, [sets(state)], velocity, speeds, below, above, below, above, deposit)
    end_low, end_high, y_low, y_high = boundary(
        groups, [sets(state), x_low, x_high], velocity, speeds, u_edges, below, above, below, above,
        deposit=deposit, packed=(pack_low, pack_high),
    )
    x2_low, x2_high = exchange(end_low, end_high, "gx")
    below2, above2 = exchange(y_low, y_high, "gy")
    (inside,) = interior(groups, [middle, end_low, end_high], velocity, speeds, below2, above2, below, above)
    fields = boundary(
        groups, [middle, end_low, end_high, x2_low, x2_high], velocity, speeds, u_edges, below2, above2, below, above,
        out=inside,
    )
    return fields.reshape(state.shape), flux


def solution(mesh):
    return jax.shard_map(
        shards,
        mesh=mesh,
        in_specs=(
            P(None, "gx", "gy", None),
            P(None, "gx", "gy", None),
            P("gx", "gy"),
            P("gy", "gx", None),
            P("gy", "gx", None),
            P("gy", "gx"),
            P("gy", "gx", None),
        ),
        out_specs=(P(None, "gx", "gy", None), P("gx", "gy")),
        check_vma=False,
    )
```

```python
import functools

import jax
import jax.numpy as jnp
from jax import lax
from jax.experimental import pallas as pl
from jax.experimental.pallas import tpu as pltpu
from jax.sharding import PartitionSpec as P

LEVELS = 4
profile_weights = (0.4, 0.3, 0.2, 0.1)
time_step = 0.1
FACTOR = 0.25 * time_step

VMEM_LIMIT = 48 * 1024 * 1024
PAIR = 2
HIGHEST = lax.Precision.HIGHEST
ANY = pl.BlockSpec(memory_space=pl.ANY)
VMEM = pl.BlockSpec(memory_space=pltpu.VMEM)
SMEM = pl.BlockSpec(memory_space=pltpu.SMEM)


def params():
    return pltpu.CompilerParams(vmem_limit_bytes=VMEM_LIMIT)


def cost(flops, moved):
    return pl.CostEstimate(flops=int(flops), bytes_accessed=int(moved), transcendentals=0)


def minmod(a, b):
    return jnp.maximum(jnp.minimum(a, b), jnp.minimum(jnp.maximum(a, b), 0.0))


def tile_of(ref, t, tiles):
    return ref[pl.ds(t, 8, stride=tiles), :]


class Slabs:
    def __init__(self, q, uv, sz, fall, fx, lx, block, x_at, at, halo, x, kept=None):
        self.q, self.uv, self.sz, self.falls, self.fx, self.lx = q, uv, sz, fall, fx, lx
        self.block, self.x_at, self.at, self.kept = block, x_at, at, kept
        self.halo, self.x = halo, x
        self.comps, self.tiles, self.lanes = q.shape[1], sz.shape[2], q.shape[-1]

    def field(self, c, slab, t):
        return self.q[self.block, c, slab, t]

    def row(self, k, which, number):
        return self.halo[which][number, pl.ds(self.x + k, 1), :]

    def centre(self, c, k, t):
        slab = k + 2
        if 0 <= t < self.tiles:
            return self.field(c, slab, t)
        row = lax.broadcasted_iota(jnp.int32, (8, self.lanes), 0)
        if t < 0:
            moved = pltpu.roll(self.field(c, slab, t + self.tiles), 1, 0)
            return jnp.where(row == 0, self.row(k, 0, 2 * c + t + 2), moved)
        t -= self.tiles
        return jnp.where(row == 7, self.row(k, 1, 2 * c + t), pltpu.roll(self.field(c, slab, t), 7, 0))

    def east(self, k, t):
        here = k + self.x_at
        return FACTOR * (self.uv[self.block, 0, here, t] + self.uv[self.block, 0, here + 1, t])

    def wind(self, k, t):
        inner = self.uv[self.block, 1, k + self.x_at, t % self.tiles]
        if 0 <= t < self.tiles:
            return inner
        row = lax.broadcasted_iota(jnp.int32, (8, self.lanes), 0)
        end, turn, which = (0, 1, 2) if t < 0 else (7, 7, 3)
        return jnp.where(row == end, self.row(k, which, 2 * self.comps), pltpu.roll(inner, turn, 0))

    def north(self, k, t):
        return FACTOR * (self.wind(k, t) + self.wind(k, t + 1))

    def up(self, k, t):
        return self.sz[self.block, k + self.at, t]

    def down(self, k, t):
        return self.falls[self.block, k + self.at, t]


def each(function, *lists):
    return [function(*items) for items in zip(*lists)]


def minmods(a, b):
    low, high = each(jnp.minimum, a, b), each(jnp.maximum, a, b)
    high = each(lambda x: jnp.minimum(x, 0.0), high)
    return each(jnp.maximum, low, high)


def difference(a, b):
    return each(lambda x, y: x - y, a, b)


def total_of(a, b):
    return each(lambda x, y: x + y, a, b)


def face_flux(speeds, masks, low_side, high_side):
    picked = each(jnp.where, masks, low_side, high_side)
    return each(lambda x, y: x * y, speeds, picked)


def staged(jobs):
    waiting = []
    for job in jobs:
        stores = job()
        for ref, index, value in waiting:
            ref[index] = value
        waiting = stores
    for ref, index, value in waiting:
        ref[index] = value


def first_face(f):
    def job(ts):
        spots = [(t, c) for t in ts for c in range(f.comps)]
        speeds = {t: f.east(-1, t) for t in ts}
        masks = {t: speeds[t] > 0 for t in ts}
        a, b, q0, q1 = [[f.field(c, slab, t) for t, c in spots] for slab in range(4)]
        middle = difference(q0, b)
        left = total_of(total_of(b, b), minmods(middle, difference(b, a)))
        slope = minmods(difference(q1, q0), middle)
        twice = total_of(q0, q0)
        flux = face_flux([speeds[t] for t, _ in spots], [masks[t] for t, _ in spots], left, difference(twice, slope))
        stores = [(f.fx, spot, x) for spot, x in zip(spots, flux)]
        if f.kept is not None:
            stores += [(f.kept[0], spot, x) for spot, x in zip(spots, twice)]
            stores += [(f.kept[1], spot, x) for spot, x in zip(spots, difference(q1, q0))]
        return stores + [(f.lx, spot, x) for spot, x in zip(spots, total_of(twice, slope))]

    staged([functools.partial(job, range(t, t + PAIR)) for t in range(0, f.tiles, PAIR)])


def slab_step(f, k, put, group_size=8):
    slab = k + 2
    lane = lax.broadcasted_iota(jnp.int32, (8, f.lanes), 1)
    top = f.lanes - 1
    is_first, is_last = lane == 0, lane == top
    carry = []
    speed = f.north(k, -1)
    for c in range(f.comps):
        a, b, q0, q1 = [f.centre(c, k, t) for t in (-2, -1, 0, 1)]
        middle, ahead = q0 - b, q1 - q0
        left_state = (b + b) + minmod(middle, b - a)
        slope = minmod(ahead, middle)
        twice = q0 + q0
        flux = speed * jnp.where(speed > 0, left_state, twice - slope)
        carry.append((q0, q1, ahead, twice, twice + slope, flux))
    states, doubles = {}, {}

    def vertical(t):
        for c in range(f.comps):
            q0 = f.field(c, slab, t)
            over = jnp.where(is_last, 0.0, pltpu.roll(q0, top, 1))
            under = jnp.where(is_first, 0.0, pltpu.roll(q0, 1, 1))
            slope = minmod(over - q0, q0 - under)
            if f.kept is not None:
                doubles[c, t] = f.kept[0][t, c]
            twice = double(c, t, q0)
            states[t, c] = (twice - slope, twice + slope)

    def flush(held):
        for c, t, flux_x, left_x, twice_x, step_x, value in held:
            f.fx[t, c], f.lx[t, c] = flux_x, left_x
            if f.kept is not None:
                f.kept[0][t, c], f.kept[1][t, c] = twice_x, step_x
            put(c, t, value)

    def double(c, t, tile):
        if f.kept is None or not 0 <= t < f.tiles:
            return tile + tile
        return doubles[c, t]

    held = []
    for t in range(group_size):
        vertical(t)
    for begin in range(0, f.tiles, group_size):
        group = range(begin, min(begin + group_size, f.tiles))
        for t in range(begin + group_size, min(begin + 2 * group_size, f.tiles)):
            vertical(t)
        loaded = {}
        for t in group:
            loaded[t] = (f.east(k, t), f.north(k, t), f.up(k, t), f.down(k, t))
            for c in range(f.comps):
                loaded[t, c] = (
                    f.centre(c, k, t + 2), f.field(c, slab + 1, t), f.field(c, slab + 2, t),
                    f.fx[t, c], f.lx[t, c], f.kept[1][t, c] if f.kept is not None else None,
                )
        flush(held)
        held = []
        for t in group:
            speed_x, speed_y, speed_z, fall = loaded[t]
            go_x, go_y, go_z, go_fall = speed_x > 0, speed_y > 0, speed_z > 0, fall > 0
            for c in range(f.comps):
                y2, x1, x2, flux_w, left_w, step_w = loaded[t, c]
                q0, y1, ahead, twice, left_y, flux_y = carry[c]
                beyond = y2 - y1
                slope = minmod(beyond, ahead)
                twice_y = double(c, t + 1, y1)
                flux_next = speed_y * jnp.where(go_y, left_y, twice_y - slope)
                total = flux_next - flux_y
                carry[c] = (y1, y2, beyond, twice_y, twice_y + slope, flux_next)
                step_x = x2 - x1
                slope = minmod(step_x, x1 - q0 if step_w is None else step_w)
                twice_x = x1 + x1
                flux_x = speed_x * jnp.where(go_x, left_w, twice_x - slope)
                left_x = twice_x + slope
                total = total + (flux_x - flux_w)
                lower, upper = states[t, c]
                flux_z = speed_z * jnp.where(go_z, upper, pltpu.roll(lower, top, 1))
                flux_below = fall * jnp.where(go_fall, pltpu.roll(upper, 1, 1), lower)
                total = total + (flux_z - flux_below)
                held.append((c, t, flux_x, left_x, twice_x, step_x, q0 - total))
    flush(held)


def dust_job(q, block, slab, dust):
    c, spots = q.shape[1] - 1, range(q.shape[3])
    tiles = total_of([q[block, c, slab, t] for t in spots], dust(spots))
    return [(q, (block, c, slab, t), tile) for t, tile in zip(spots, tiles)]


def falling(deposit, column):
    lanes = deposit.shape[-1]

    def dust(spots):
        parts = [pltpu.roll(deposit[t], lanes - column, 1) for t in spots]
        lane = lax.broadcasted_iota(jnp.int32, parts[0].shape, 1)
        return [jnp.where(lane == 0, part, 0.0) for part in parts]

    return dust


def pack_edges(packs, stage_slab, comps, x):
    x = pl.ds(x, 1)
    stores = []
    for c in range(comps):
        tiles = stage_slab(c)
        count = tiles.shape[0]
        for r in range(2):
            stores.append((packs[0], (2 * c + r, x), tiles[r, 0:1, :]))
            stores.append((packs[1], (2 * c + r, x), tiles[count - 2 + r, 7:8, :]))
    staged([lambda: stores])


def start(source, target, sem):
    pltpu.make_async_copy(source, target, sem).start()


def start_sets(pairs, sem):
    for source, target in pairs:
        for number in range(8):
            start(source(number), target(number), sem)


def arrived(spot, sem):
    pltpu.make_async_copy(spot, spot, sem).wait()


def interior_kernel(last, groups, count, *refs):
    refs = list(refs)
    fields, velocity, speeds = refs[:count], refs[count], refs[count + 1 : count + 3]
    below, above, v_below, v_above = refs[count + 3 : count + 7]
    del refs[: count + 7]
    deposit = None if last else refs.pop(0)
    out = refs.pop(0)
    packs = None if last else (refs.pop(0), refs.pop(0))
    q, uv, sz, fall, fx, lx, stage, in_sem, out_sem = refs[:9]
    kept = refs[9:11]
    comps, slabs, tiles = q.shape[1], q.shape[2], sz.shape[2]
    chunk, flight = (8, 3) if last else (4, 6)
    chunks = slabs // chunk

    def fetch(j, first, final):
        span = pl.ds(j * chunk, chunk)
        if last:
            middle, low, high = fields
            begin, size = j * chunk, chunk
            if first:
                begin, size = begin + 2, size - 2
                start(low, q.at[0, :, pl.ds(0, 2)], in_sem.at[j, 0])
            if final:
                size -= 2
                start(high, q.at[0, :, pl.ds(slabs - 2, 2)], in_sem.at[j, 0])
            part = pl.ds(begin, size)
            start(middle.at[:, part], q.at[0, :, part], in_sem.at[j, 0])
        else:
            pair = (lambda n: fields[0].at[:, span, n], lambda n: q.at[0, :, span, :, n])
            start_sets([pair], in_sem.at[j, 0])
        pair = (lambda n: velocity.at[pl.ds(0, 2), span, n], lambda n: uv.at[0, :, span, :, n])
        start_sets([pair], in_sem.at[j, 1])
        for n, (source, target) in enumerate(zip(speeds, (sz, fall))):
            start(source.at[span], target.at[0, span], in_sem.at[j, n + 2])

    for j in range(flight):
        fetch(j, j == 0, False)

    def arrive(j):
        span = pl.ds(j * chunk, chunk)
        arrived(q.at[0, :, span], in_sem.at[j, 0])
        for n, spot in enumerate((uv.at[0, :, span], sz.at[0, span], fall.at[0, span])):
            arrived(spot, in_sem.at[j, n + 1])
        later = j + flight

        @pl.when(later < chunks - 1)
        def _():
            fetch(later, False, False)

        @pl.when(later == chunks - 1)
        def _():
            fetch(chunks - 1, False, True)

        def complete(x, _):
            staged([functools.partial(dust_job, q, 0, x, falling(deposit, x + 2))])
            return 0

        if not last:
            lax.fori_loop(j * chunk, jnp.minimum((j + 1) * chunk, groups), complete, 0)

    f = Slabs(q, uv, sz, fall, fx, lx, 0, 2, 2, (below, above, v_below, v_above), 2, kept)
    arrive(jnp.int32(0))
    first_face(f)

    def step(k, _):
        @pl.when((k + 4) % chunk == 0)
        def _():
            arrive((k + 4) // chunk)

        def put(c, t, value):
            stage[c, k, t] = value

        slab_step(f, k, put, 16 if last else 4)
        if last:
            start_sets([(lambda n: stage.at[:, k, :, n], lambda n: out.at[:, k + 2, n])], out_sem)
        else:
            start(stage.at[:, k], out.at[:, k + 2], out_sem)
        if not last:
            pack_edges(packs, lambda c: stage.at[c, k], comps, k + 2)
        return 0

    if not last:
        for pack in packs:
            pack[...] = jnp.zeros_like(pack)
    lax.fori_loop(0, slabs - 4, step, 0)
    arrived(stage, out_sem)


def interior(groups, fields, velocity, speeds, below, above, v_below, v_above, deposit=None):
    last = deposit is None
    slabs, tiles, _, lanes = speeds[0].shape
    rows, comps = 8 * tiles, fields[0].shape[0]
    operands = list(fields) + [velocity, *speeds, below, above, v_below, v_above]
    specs = [ANY] * (len(fields) + 3) + [VMEM] * 4
    form = (8, tiles, lanes) if last else (tiles, 8, lanes)
    out_shape = [jax.ShapeDtypeStruct((comps, slabs, *form), jnp.float32)]
    out_specs = [ANY]
    scratch = [
        pltpu.VMEM((1, comps, slabs, tiles, 8, lanes), jnp.float32),
        pltpu.VMEM((1, 2, slabs, tiles, 8, lanes), jnp.float32),
        *[pltpu.VMEM((1, slabs, tiles, 8, lanes), jnp.float32)] * 2,
        pltpu.VMEM((tiles, comps, 8, lanes), jnp.float32),
        pltpu.VMEM((tiles, comps, 8, lanes), jnp.float32),
        pltpu.VMEM((comps, slabs - 4, tiles, 8, lanes), jnp.float32),
        pltpu.SemaphoreType.DMA((slabs // 4, 5)),
        pltpu.SemaphoreType.DMA,
    ]
    scratch += [pltpu.VMEM((tiles, comps, 8, lanes), jnp.float32)] * 2
    if not last:
        out_shape += [jax.ShapeDtypeStruct((2 * comps, slabs, lanes), jnp.float32)] * 2
        out_specs += [VMEM] * 2
        operands.append(deposit)
        specs.append(VMEM)
    cells = comps * (slabs - 4) * rows * lanes
    return pl.pallas_call(
        functools.partial(interior_kernel, last, groups, len(fields)),
        out_shape=tuple(out_shape),
        in_specs=specs,
        out_specs=tuple(out_specs),
        scratch_shapes=scratch,
        compiler_params=params(),
        cost_estimate=cost(40 * cells, 4 * (2 * cells + 4 * slabs * rows * lanes)),
        name="interior",
    )(*operands)


def boundary_kernel(last, groups, slabs, *refs):
    refs = list(refs)
    count = 5 if last else 3
    fields, velocity, speeds = refs[:count], refs[count], refs[count + 1 : count + 3]
    u_outer = refs[count + 3 : count + 5]
    below, above, v_below, v_above = refs[count + 5 : count + 9]
    del refs[: count + 9]
    if last:
        out = refs[1]
        del refs[:2]
    else:
        deposit, packed, ends, packs = refs[0], refs[1:3], refs[3:5], refs[5:7]
        del refs[:7]
    q, uv, sz, fall, fx, lx, stage, in_sem, out_sem = refs
    comps, tiles = q.shape[1], sz.shape[2]

    if last:
        middle, end_low, end_high, x_low, x_high = fields
        for block, at, source in (
            (0, 0, x_low), (0, 2, end_low), (0, 4, middle.at[:, pl.ds(2, 2)]),
            (1, 0, middle.at[:, pl.ds(slabs - 4, 2)]), (1, 2, end_high), (1, 4, x_high),
        ):
            start(source, q.at[block, :, pl.ds(at, 2)], in_sem.at[block, 0])
    else:
        state, x_low, x_high = fields
        for block, at, first in ((0, 2, 0), (1, 0, slabs - 4)):
            pair = (
                lambda n: state.at[:, pl.ds(first, 4), n], lambda n: q.at[block, :, pl.ds(at, 4), :, n]
            )
            start_sets([pair], in_sem.at[block, 0])
        for block, at, halo in ((0, 0, x_low), (1, 4, x_high)):
            pairs = [
                (lambda n, c=c: halo.at[pl.ds(2 * c, 2), n], lambda n, c=c: q.at[block, c, pl.ds(at, 2), :, n])
                for c in range(comps)
            ]
            start_sets(pairs, in_sem.at[block, 0])
    edge = pl.ds(2 * comps, 1)
    for block in range(2):
        outer, first, at = 3 * block, block * (slabs - 3), 1 - block
        pairs = [
            (lambda n: u_outer[block].at[edge, n], lambda n: uv.at[block, 0, pl.ds(outer, 1), :, n]),
            (
                lambda n: velocity.at[pl.ds(0, 2), pl.ds(first, 3), n],
                lambda n: uv.at[block, :, pl.ds(at, 3), :, n],
            ),
        ]
        for number, pair in enumerate(pairs):
            start_sets([pair], in_sem.at[block, number + 1])
        span = pl.ds(block * (slabs - 2), 2)
        for n, target in enumerate((sz, fall)):
            start(speeds[n].at[span], target.at[block], in_sem.at[block, n + 3])
    if not last:
        packs[0][...] = packed[0][...]
        packs[1][...] = packed[1][...]

    def one(block, _):
        begin = block * (slabs - 2)
        arrived(q.at[block], in_sem.at[block, 0])
        spots = (uv.at[block, 0, pl.ds(0, 1)], uv.at[block, :, pl.ds(0, 3)], sz.at[block], fall.at[block])
        for n, spot in enumerate(spots):
            arrived(spot, in_sem.at[block, n + 1])

        def complete(slab, _):
            x = begin + slab - 2
            lands = (x >= slabs) | ((x >= 0) & (x < groups)) | (x + slabs < groups)

            @pl.when(lands)
            def _():
                staged([functools.partial(dust_job, q, block, slab, falling(deposit, x + 2))])

            return 0

        if not last:
            lax.fori_loop(0, 6, complete, 0)
        f = Slabs(q, uv, sz, fall, fx, lx, block, 1, 0, (below, above, v_below, v_above), begin)
        first_face(f)

        def step(k, _):
            def put(c, t, value):
                stage[block, c, k, t] = value

            slab_step(f, k, put)
            if not last:
                pack_edges(packs, lambda c: stage.at[block, c, k], comps, begin + k)
            return 0

        lax.fori_loop(0, 2, step, 0)
        if last:
            span = pl.ds(begin, 2)
            pair = (lambda n: stage.at[block, :, :, :, n], lambda n: out.at[:, span, n])
            start_sets([pair], out_sem.at[block])
        else:
            for number in range(2):

                @pl.when(block == number)
                def _():
                    start(stage.at[number], ends[number], out_sem.at[number])

        return 0

    lax.fori_loop(0, 2, one, 0)
    for block in range(2):
        arrived(stage.at[block], out_sem.at[block])


def boundary(groups, fields, velocity, speeds, u_outer, below, above, v_below, v_above, *, deposit=None, packed=None, out=None):
    last = out is not None
    slabs, tiles, _, lanes = speeds[0].shape
    rows, comps = 8 * tiles, fields[0].shape[0]
    operands = list(fields) + [velocity, *speeds, *u_outer, below, above, v_below, v_above]
    specs = [ANY] * (len(fields) + 5) + [VMEM] * 4
    form = (tiles, 8, lanes)
    scratch = [
        pltpu.VMEM((2, comps, 6, tiles, 8, lanes), jnp.float32),
        pltpu.VMEM((2, 2, 4, tiles, 8, lanes), jnp.float32),
        *[pltpu.VMEM((2, 2, tiles, 8, lanes), jnp.float32)] * 2,
        pltpu.VMEM((tiles, comps, 8, lanes), jnp.float32),
        pltpu.VMEM((tiles, comps, 8, lanes), jnp.float32),
        pltpu.VMEM((2, comps, 2, *form), jnp.float32),
        pltpu.SemaphoreType.DMA((2, 5)),
        pltpu.SemaphoreType.DMA((2,)),
    ]
    if last:
        aliases = {len(operands): 0}
        operands.append(out)
        specs.append(ANY)
        out_shape = jax.ShapeDtypeStruct(out.shape, out.dtype)
        out_specs = ANY
    else:
        aliases = {}
        operands += [deposit, *packed]
        specs += [VMEM] * 3
        out_shape = (jax.ShapeDtypeStruct((comps, 2, *form), jnp.float32),) * 2
        out_shape += (jax.ShapeDtypeStruct((2 * comps, slabs, lanes), jnp.float32),) * 2
        out_specs = (ANY, ANY, VMEM, VMEM)
    cells = comps * 4 * rows * lanes
    return pl.pallas_call(
        functools.partial(boundary_kernel, last, groups, slabs),
        out_shape=out_shape,
        in_specs=specs,
        out_specs=out_specs,
        scratch_shapes=scratch,
        input_output_aliases=aliases,
        compiler_params=params(),
        cost_estimate=cost(50 * cells, 4 * 6 * cells),
        name="boundary",
    )(*operands)


def speeds_kernel(velocity, sz, fall, wind, sems):
    step = pl.program_id(0)
    part, count, lanes = sz.shape[0], wind.shape[1], wind.shape[3]
    lane = lax.broadcasted_iota(jnp.int32, (8, lanes), 1)
    is_first, is_last = lane == 0, lane == lanes - 1

    @pl.when(step == 0)
    def _():
        for j in range(wind.shape[0] // part):
            span = pl.ds(j * part, part)
            start_sets([(lambda n: velocity.at[2, span, n], lambda n: wind.at[span, :, n])], sems.at[j])

    arrived(wind.at[pl.ds(step * part, part)], sems.at[step])

    def one(x, _):
        here = [FACTOR * wind[step * part + x, t] for t in range(count)]
        over = [pltpu.roll(tile, lanes - 1, 1) for tile in here]
        under = [pltpu.roll(tile, 1, 1) for tile in here]
        upper = [jnp.where(is_last, jnp.maximum(a, 0.0), a + b) for a, b in zip(here, over)]
        lower = [jnp.where(is_first, jnp.minimum(a, 0.0), a + b) for a, b in zip(here, under)]
        for t in range(count):
            sz[x, t] = upper[t]
            fall[x, t] = lower[t]
        return 0

    lax.fori_loop(0, part, one, 0)


def face_speeds(velocity):
    _, slabs, _, tiles, lanes = velocity.shape
    part = 8
    return pl.pallas_call(
        speeds_kernel,
        grid=(slabs // part,),
        out_shape=(jax.ShapeDtypeStruct((slabs, tiles, 8, lanes), jnp.float32),) * 2,
        in_specs=[ANY],
        out_specs=(pl.BlockSpec((part, tiles, 8, lanes), lambda i: (i, 0, 0, 0)),) * 2,
        scratch_shapes=[
            pltpu.VMEM((slabs, tiles, 8, lanes), jnp.float32),
            pltpu.SemaphoreType.DMA((slabs // part,)),
        ],
        compiler_params=params(),
        cost_estimate=cost(8 * slabs * 8 * tiles * lanes, 12 * slabs * 8 * tiles * lanes),
        name="face_speeds",
    )(velocity)


def x_copies(state, velocity, low, high, sems):
    comps, slabs = state.shape[0], state.shape[1]
    copies = []
    for n, (target, first, edge) in enumerate(((low, 0, 0), (high, slabs - 2, slabs - 1))):
        pairs = [(state.at[c, pl.ds(first, 2)], target.at[pl.ds(2 * c, 2)]) for c in range(comps)]
        pairs.append((velocity.at[0, pl.ds(edge, 1)], target.at[pl.ds(2 * comps, 1)]))
        copies += [pltpu.make_async_copy(*pair, sems.at[n, i]) for i, pair in enumerate(pairs)]
    return copies


def as_column(row):
    count = row.shape[1]
    shape = (count, count)
    same = lax.broadcasted_iota(jnp.int32, shape, 0) == lax.broadcasted_iota(jnp.int32, shape, 1)
    return jnp.sum(jnp.where(same, row, 0.0), axis=1, keepdims=True)


def stress_kernel(wind, stress, gathered):
    step, steps = pl.program_id(0), pl.num_programs(0)
    part, rows, lanes = wind.shape[1:]
    slabs = stress.shape[0]
    lane = lax.broadcasted_iota(jnp.int32, (rows, lanes), 1)
    weight = jnp.zeros((rows, lanes), jnp.float32)
    for level, value in enumerate(profile_weights):
        weight = jnp.where(lane == level, value, weight)
    total = jnp.zeros((rows, lanes), jnp.float32)
    for x in range(part):
        east, north = wind[0, x], wind[1, x]
        friction = jnp.where(lane < LEVELS, weight * (east * east + north * north), 0.0)
        total = total + pltpu.roll(friction, LEVELS * x, 1) if x else friction

    @pl.when(step == 0)
    def _():
        gathered[...] = total

    @pl.when(step > 0)
    def _():
        gathered[...] += pltpu.roll(total, LEVELS * part * step, 1)

    @pl.when(step == steps - 1)
    def _():
        gathered[...] = gathered[...].T
        total = gathered[pl.ds(0, slabs, stride=LEVELS), :]
        for level in range(1, LEVELS):
            total = total + gathered[pl.ds(level, slabs, stride=LEVELS), :]
        stress[...] = total


def tile_stress(velocity):
    _, slabs, rows, lanes = velocity.shape
    part = 8
    return pl.pallas_call(
        stress_kernel,
        grid=(slabs // part,),
        out_shape=jax.ShapeDtypeStruct((slabs, lanes), jnp.float32),
        in_specs=[pl.BlockSpec((2, part, rows, lanes), lambda i: (0, i, 0, 0))],
        out_specs=pl.BlockSpec((slabs, lanes), lambda i: (0, 0)),
        scratch_shapes=[pltpu.VMEM((rows, lanes), jnp.float32)],
        compiler_params=params(),
        cost_estimate=cost(10 * slabs * rows * lanes, 8 * slabs * rows * lanes),
        name="tile_stress",
    )(velocity)


def pack_kernel(low_in, high_in, v_low, v_high, state, velocity, low, high, x_low, x_high, sems):
    step, steps = pl.program_id(0), pl.num_programs(0)
    comps, part = low_in.shape[:2]

    @pl.when(step == 0)
    def _():
        for copy in x_copies(state, velocity, x_low, x_high, sems):
            copy.start()

    for x in range(part):
        for c in range(comps):
            for r in range(2):
                low[2 * c + r, x : x + 1, :] = low_in[c, x, r : r + 1, :]
                high[2 * c + r, x : x + 1, :] = high_in[c, x, 6 + r : 7 + r, :]
        low[2 * comps, x : x + 1, :] = v_low[0, x, 0:1, :]
        high[2 * comps, x : x + 1, :] = v_high[0, x, 7:8, :]

    @pl.when(step == steps - 1)
    def _():
        for copy in x_copies(state, velocity, x_low, x_high, sems):
            copy.wait()


def pack(state, velocity):
    comps, slabs, rows, lanes = state.shape
    part = 8
    last = rows // 8 - 1
    packed = jax.ShapeDtypeStruct((2 * comps + 1, slabs, lanes), jnp.float32)
    packed_spec = pl.BlockSpec((2 * comps + 1, part, lanes), lambda i: (0, i, 0))
    x_packed = jax.ShapeDtypeStruct((2 * comps + 1, rows, lanes), jnp.float32)
    return pl.pallas_call(
        pack_kernel,
        grid=(slabs // part,),
        out_shape=(packed, packed, x_packed, x_packed),
        in_specs=[
            pl.BlockSpec((comps, part, 8, lanes), lambda i: (0, i, 0, 0)),
            pl.BlockSpec((comps, part, 8, lanes), lambda i: (0, i, last, 0)),
            pl.BlockSpec((1, part, 8, lanes), lambda i: (1, i, 0, 0)),
            pl.BlockSpec((1, part, 8, lanes), lambda i: (1, i, last, 0)),
            ANY,
            ANY,
        ],
        out_specs=(packed_spec, packed_spec, ANY, ANY),
        scratch_shapes=[pltpu.SemaphoreType.DMA((2, comps + 1))],
        compiler_params=params(),
        cost_estimate=cost(1, 12 * (2 * comps + 1) * rows * lanes),
        name="pack",
    )(state, state, velocity, velocity, state, velocity)


def census_kernel(stress, threshold, tile_owner, parcel_owner, count, share, copies):
    groups, height, lanes = copies.shape
    slabs = stress.shape[0]
    owners = parcel_owner[...].astype(jnp.float32)
    shape = (groups, slabs)
    place = (owners == lax.broadcasted_iota(jnp.int32, shape, 0).astype(jnp.float32)).astype(jnp.float32)
    live = as_column(count[...].astype(jnp.float32))
    shape = (slabs, lanes)
    reach = lax.broadcasted_iota(jnp.int32, shape, 1).astype(jnp.float32) < live
    masses = jnp.where(reach, share[0], 0.0)
    copies[0, 0:slabs] = stress[...]
    copies[0, slabs : slabs + 8] = jnp.zeros((8, lanes), jnp.float32)
    copies[0, slabs : slabs + 1] = threshold[...]
    copies[0, slabs + 1 : slabs + 2, 0:slabs] = tile_owner[...].astype(jnp.float32)
    copies[0, slabs + 8 : height] = jnp.dot(place, masses, precision=HIGHEST, preferred_element_type=jnp.float32)
    whole = copies[0]
    for g in range(1, groups):
        copies[g] = whole


def census(groups, stress, *small):
    slabs, lanes = stress.shape
    return pl.pallas_call(
        census_kernel,
        out_shape=jax.ShapeDtypeStruct((groups, slabs + 8 + groups, lanes), jnp.float32),
        in_specs=[VMEM] * 6,
        out_specs=VMEM,
        compiler_params=params(),
        cost_estimate=cost(10**6, 10**6),
        name="census",
    )(stress, *small)


def deposit_kernel(slabs, me, gathered, low_in, high_in, flux_out, deposit, low, high, flux, dropped):
    groups, lanes = gathered.shape[0], gathered.shape[2]
    here = me[0]
    limits = jnp.concatenate([gathered[g, slabs : slabs + 1] for g in range(groups)], axis=0)
    total = jnp.zeros((groups, lanes), jnp.float32)
    shape = (groups, slabs)
    numbers = lax.broadcasted_iota(jnp.int32, shape, 0).astype(jnp.float32)
    for g in range(groups):
        owners = gathered[g, slabs + 1 : slabs + 2, 0:slabs]
        stress = gathered[g, 0:slabs]
        named = (owners == numbers).astype(jnp.float32)
        limit = lax.dot_general(
            named, limits, (((0,), (0,)), ((), ())), precision=HIGHEST, preferred_element_type=jnp.float32
        )
        lifting = jnp.maximum(stress - limit, 0.0)
        total = total + jnp.dot(named, lifting, precision=HIGHEST, preferred_element_type=jnp.float32)
    flux[...] = total / slabs
    flux_out[...] = flux[pl.ds(here, 1), :]
    dropped[...] = jnp.zeros_like(dropped)
    before, after = jnp.maximum(here - 1, 0), jnp.minimum(here + 1, groups - 1)
    has_before, has_after = here > 0, here < groups - 1
    base = slabs + 8
    for p in range(groups):
        x = p % slabs
        row = flux[p : p + 1, :]
        dropped[x + 2 : x + 3] += row * gathered[p, pl.ds(base + here, 1), :]
        if x >= slabs - 2:
            mass = row * gathered[p, pl.ds(base + before, 1), :]
            dropped[x - slabs + 2 : x - slabs + 3] += jnp.where(has_before, mass, 0.0)
        if x < 2:
            mass = row * gathered[p, pl.ds(base + after, 1), :]
            dropped[x + slabs + 2 : x + slabs + 3] += jnp.where(has_after, mass, 0.0)
    own = dropped[2 : 2 + slabs, :]
    dropped[...] = dropped[...].T
    count = deposit.shape[0]
    tiles = [tile_of(dropped, t, count) for t in range(count)]
    for t, tile in enumerate(tiles):
        deposit[t] = tile
    lane = lax.broadcasted_iota(jnp.int32, (slabs, lanes), 1)
    rows = lanes
    dust = low.shape[0] - 3
    low[...] = low_in[...]
    high[...] = high_in[...]
    for r in range(2):
        low[dust + r] += jnp.where(lane == 0, own[:, r : r + 1], 0.0)
        high[dust + r] += jnp.where(lane == 0, own[:, rows - 2 + r : rows - 1 + r], 0.0)


def settle(me, gathered, low, high, slabs):
    groups, _, lanes = gathered.shape
    edge = jax.ShapeDtypeStruct(low.shape, jnp.float32)
    return pl.pallas_call(
        functools.partial(deposit_kernel, slabs),
        out_shape=(
            jax.ShapeDtypeStruct((1, lanes), jnp.float32),
            jax.ShapeDtypeStruct((lanes // 8, 8, lanes), jnp.float32),
            edge,
            edge,
        ),
        in_specs=[SMEM, VMEM, VMEM, VMEM],
        out_specs=(VMEM, VMEM, VMEM, VMEM),
        scratch_shapes=[
            pltpu.VMEM((groups, lanes), jnp.float32),
            pltpu.VMEM((lanes, lanes), jnp.float32),
        ],
        compiler_params=params(),
        cost_estimate=cost(10**6, 10**6),
        name="settle",
    )(me, gathered, low, high)


def exchange(low, high, axis):
    count = lax.axis_size(axis)
    forward = [(i, i + 1) for i in range(count - 1)]
    backward = [(target, source) for source, target in forward]
    return lax.ppermute(high, axis, forward), lax.ppermute(low, axis, backward)


def shards(state, velocity, threshold, tile_owner, parcel_owner, parcel_count, parcel_share):
    groups = lax.axis_size("gx")
    slabs = state.shape[1]
    me = lax.axis_index("gx").astype(jnp.int32).reshape(1)

    stress = tile_stress(velocity)
    low, high, own_low, own_high = pack(state, velocity)
    copies = census(
        groups, stress, threshold, tile_owner[:, :, 0], parcel_owner[:, :, 0], parcel_count, parcel_share
    )
    rows, lanes = state.shape[2:]

    def sets(array):
        return array.reshape(*array.shape[:-2], 8, rows // 8, lanes)

    velocity = sets(velocity)
    speeds = face_speeds(velocity)
    gathered = lax.all_to_all(copies, "gx", split_axis=0, concat_axis=0, tiled=True)
    flux, deposit, low, high = settle(me, gathered, low, high, slabs)
    below, above = exchange(low, high, "gy")
    own_low, own_high, _ = lax.optimization_barrier((own_low, own_high, gathered))
    x_low, x_high = exchange(own_low, own_high, "gx")
    x_low, x_high = sets(x_low), sets(x_high)
    u_edges = (x_low, x_high)
    middle, pack_low, pack_high = interior(groups, [sets(state)], velocity, speeds, below, above, below, above, deposit)
    end_low, end_high, y_low, y_high = boundary(
        groups, [sets(state), x_low, x_high], velocity, speeds, u_edges, below, above, below, above,
        deposit=deposit, packed=(pack_low, pack_high),
    )
    x2_low, x2_high = exchange(end_low, end_high, "gx")
    below2, above2 = exchange(y_low, y_high, "gy")
    (inside,) = interior(groups, [middle, end_low, end_high], velocity, speeds, below2, above2, below, above)
    fields = boundary(
        groups, [middle, end_low, end_high, x2_low, x2_high], velocity, speeds, u_edges, below2, above2, below, above,
        out=inside,
    )
    return fields.reshape(state.shape), flux


def solution(mesh):
    return jax.shard_map(
        shards,
        mesh=mesh,
        in_specs=(
            P(None, "gx", "gy", None),
            P(None, "gx", "gy", None),
            P("gx", "gy"),
            P("gy", "gx", None),
            P("gy", "gx", None),
            P("gy", "gx"),
            P("gy", "gx", None),
        ),
        out_specs=(P(None, "gx", "gy", None), P("gx", "gy")),
        check_vma=False,
    )
```

```python
import functools

import jax
import jax.numpy as jnp
from jax import lax
from jax.experimental import pallas as pl
from jax.experimental.pallas import tpu as pltpu
from jax.sharding import PartitionSpec as P

LEVELS = 4
profile_weights = (0.4, 0.3, 0.2, 0.1)
time_step = 0.1
FACTOR = 0.25 * time_step

VMEM_LIMIT = 48 * 1024 * 1024
PAIR = 2
HIGHEST = lax.Precision.HIGHEST
ANY = pl.BlockSpec(memory_space=pl.ANY)
VMEM = pl.BlockSpec(memory_space=pltpu.VMEM)
SMEM = pl.BlockSpec(memory_space=pltpu.SMEM)


def params():
    return pltpu.CompilerParams(vmem_limit_bytes=VMEM_LIMIT)


def cost(flops, moved):
    return pl.CostEstimate(flops=int(flops), bytes_accessed=int(moved), transcendentals=0)


def minmod(a, b):
    return jnp.maximum(jnp.minimum(a, b), jnp.minimum(jnp.maximum(a, b), 0.0))


def tile_of(ref, t, tiles):
    return ref[pl.ds(t, 8, stride=tiles), :]


class Slabs:
    def __init__(self, q, uv, sz, fall, fx, lx, block, x_at, at, halo, x, kept=None):
        self.q, self.uv, self.sz, self.falls, self.fx, self.lx = q, uv, sz, fall, fx, lx
        self.block, self.x_at, self.at, self.kept = block, x_at, at, kept
        self.halo, self.x = halo, x
        self.comps, self.tiles, self.lanes = q.shape[1], sz.shape[2], q.shape[-1]

    def field(self, c, slab, t):
        return self.q[self.block, c, slab, t]

    def row(self, k, which, number):
        return self.halo[which][number, pl.ds(self.x + k, 1), :]

    def centre(self, c, k, t):
        slab = k + 2
        if 0 <= t < self.tiles:
            return self.field(c, slab, t)
        row = lax.broadcasted_iota(jnp.int32, (8, self.lanes), 0)
        if t < 0:
            moved = pltpu.roll(self.field(c, slab, t + self.tiles), 1, 0)
            return jnp.where(row == 0, self.row(k, 0, 2 * c + t + 2), moved)
        t -= self.tiles
        return jnp.where(row == 7, self.row(k, 1, 2 * c + t), pltpu.roll(self.field(c, slab, t), 7, 0))

    def east(self, k, t):
        here = k + self.x_at
        return FACTOR * (self.uv[self.block, 0, here, t] + self.uv[self.block, 0, here + 1, t])

    def wind(self, k, t):
        inner = self.uv[self.block, 1, k + self.x_at, t % self.tiles]
        if 0 <= t < self.tiles:
            return inner
        row = lax.broadcasted_iota(jnp.int32, (8, self.lanes), 0)
        end, turn, which = (0, 1, 2) if t < 0 else (7, 7, 3)
        return jnp.where(row == end, self.row(k, which, 2 * self.comps), pltpu.roll(inner, turn, 0))

    def north(self, k, t):
        return FACTOR * (self.wind(k, t) + self.wind(k, t + 1))

    def up(self, k, t):
        return self.sz[self.block, k + self.at, t]

    def down(self, k, t):
        return self.falls[self.block, k + self.at, t]


def each(function, *lists):
    return [function(*items) for items in zip(*lists)]


def minmods(a, b):
    low, high = each(jnp.minimum, a, b), each(jnp.maximum, a, b)
    high = each(lambda x: jnp.minimum(x, 0.0), high)
    return each(jnp.maximum, low, high)


def difference(a, b):
    return each(lambda x, y: x - y, a, b)


def total_of(a, b):
    return each(lambda x, y: x + y, a, b)


def face_flux(speeds, masks, low_side, high_side):
    picked = each(jnp.where, masks, low_side, high_side)
    return each(lambda x, y: x * y, speeds, picked)


def staged(jobs):
    waiting = []
    for job in jobs:
        stores = job()
        for ref, index, value in waiting:
            ref[index] = value
        waiting = stores
    for ref, index, value in waiting:
        ref[index] = value


def first_face(f):
    def job(ts):
        spots = [(t, c) for t in ts for c in range(f.comps)]
        speeds = {t: f.east(-1, t) for t in ts}
        masks = {t: speeds[t] > 0 for t in ts}
        a, b, q0, q1 = [[f.field(c, slab, t) for t, c in spots] for slab in range(4)]
        middle = difference(q0, b)
        left = total_of(total_of(b, b), minmods(middle, difference(b, a)))
        slope = minmods(difference(q1, q0), middle)
        twice = total_of(q0, q0)
        flux = face_flux([speeds[t] for t, _ in spots], [masks[t] for t, _ in spots], left, difference(twice, slope))
        stores = [(f.fx, spot, x) for spot, x in zip(spots, flux)]
        if f.kept is not None:
            stores += [(f.kept[0], spot, x) for spot, x in zip(spots, twice)]
            stores += [(f.kept[1], spot, x) for spot, x in zip(spots, difference(q1, q0))]
        return stores + [(f.lx, spot, x) for spot, x in zip(spots, total_of(twice, slope))]

    staged([functools.partial(job, range(t, t + PAIR)) for t in range(0, f.tiles, PAIR)])


def slab_step(f, k, put, group_size=4):
    slab = k + 2
    lane = lax.broadcasted_iota(jnp.int32, (8, f.lanes), 1)
    top = f.lanes - 1
    is_first, is_last = lane == 0, lane == top
    carry = []
    speed = f.north(k, -1)
    for c in range(f.comps):
        a, b, q0, q1 = [f.centre(c, k, t) for t in (-2, -1, 0, 1)]
        middle, ahead = q0 - b, q1 - q0
        left_state = (b + b) + minmod(middle, b - a)
        slope = minmod(ahead, middle)
        twice = q0 + q0
        flux = speed * jnp.where(speed > 0, left_state, twice - slope)
        carry.append((q0, q1, ahead, twice, twice + slope, flux))
    states, doubles = {}, {}

    def vertical(t):
        for c in range(f.comps):
            q0 = f.field(c, slab, t)
            over = jnp.where(is_last, 0.0, pltpu.roll(q0, top, 1))
            under = jnp.where(is_first, 0.0, pltpu.roll(q0, 1, 1))
            slope = minmod(over - q0, q0 - under)
            if f.kept is not None:
                doubles[c, t] = f.kept[0][t, c]
            twice = double(c, t, q0)
            states[t, c] = (twice - slope, twice + slope)

    def flush(held):
        for c, t, flux_x, left_x, twice_x, step_x, value in held:
            f.fx[t, c], f.lx[t, c] = flux_x, left_x
            if f.kept is not None:
                f.kept[0][t, c], f.kept[1][t, c] = twice_x, step_x
            put(c, t, value)

    def double(c, t, tile):
        if f.kept is None or not 0 <= t < f.tiles:
            return tile + tile
        return doubles[c, t]

    held = []
    for t in range(group_size):
        vertical(t)
    for begin in range(0, f.tiles, group_size):
        group = range(begin, min(begin + group_size, f.tiles))
        for t in range(begin + group_size, min(begin + 2 * group_size, f.tiles)):
            vertical(t)
        loaded = {}
        for t in group:
            loaded[t] = (f.east(k, t), f.north(k, t), f.up(k, t), f.down(k, t))
            for c in range(f.comps):
                loaded[t, c] = (
                    f.centre(c, k, t + 2), f.field(c, slab + 1, t), f.field(c, slab + 2, t),
                    f.fx[t, c], f.lx[t, c], f.kept[1][t, c] if f.kept is not None else None,
                )
        flush(held)
        held = []
        for t in group:
            speed_x, speed_y, speed_z, fall = loaded[t]
            go_x, go_y, go_z, go_fall = speed_x > 0, speed_y > 0, speed_z > 0, fall > 0
            for c in range(f.comps):
                y2, x1, x2, flux_w, left_w, step_w = loaded[t, c]
                q0, y1, ahead, twice, left_y, flux_y = carry[c]
                beyond = y2 - y1
                slope = minmod(beyond, ahead)
                twice_y = double(c, t + 1, y1)
                flux_next = speed_y * jnp.where(go_y, left_y, twice_y - slope)
                total = flux_next - flux_y
                carry[c] = (y1, y2, beyond, twice_y, twice_y + slope, flux_next)
                step_x = x2 - x1
                slope = minmod(step_x, x1 - q0 if step_w is None else step_w)
                twice_x = x1 + x1
                flux_x = speed_x * jnp.where(go_x, left_w, twice_x - slope)
                left_x = twice_x + slope
                total = total + (flux_x - flux_w)
                lower, upper = states[t, c]
                flux_z = speed_z * jnp.where(go_z, upper, pltpu.roll(lower, top, 1))
                flux_below = fall * jnp.where(go_fall, pltpu.roll(upper, 1, 1), lower)
                total = total + (flux_z - flux_below)
                held.append((c, t, flux_x, left_x, twice_x, step_x, q0 - total))
    flush(held)


def dust_job(q, block, slab, dust):
    c, spots = q.shape[1] - 1, range(q.shape[3])
    tiles = total_of([q[block, c, slab, t] for t in spots], dust(spots))
    return [(q, (block, c, slab, t), tile) for t, tile in zip(spots, tiles)]


def falling(deposit, column):
    lanes = deposit.shape[-1]

    def dust(spots):
        parts = [pltpu.roll(deposit[t], lanes - column, 1) for t in spots]
        lane = lax.broadcasted_iota(jnp.int32, parts[0].shape, 1)
        return [jnp.where(lane == 0, part, 0.0) for part in parts]

    return dust


def pack_edges(packs, stage_slab, comps, x):
    x = pl.ds(x, 1)
    stores = []
    for c in range(comps):
        tiles = stage_slab(c)
        count = tiles.shape[0]
        for r in range(2):
            stores.append((packs[0], (2 * c + r, x), tiles[r, 0:1, :]))
            stores.append((packs[1], (2 * c + r, x), tiles[count - 2 + r, 7:8, :]))
    staged([lambda: stores])


def start(source, target, sem):
    pltpu.make_async_copy(source, target, sem).start()


def start_sets(pairs, sem):
    for source, target in pairs:
        for number in range(8):
            start(source(number), target(number), sem)


def arrived(spot, sem):
    pltpu.make_async_copy(spot, spot, sem).wait()


def interior_kernel(last, groups, count, *refs):
    refs = list(refs)
    fields, velocity, speeds = refs[:count], refs[count], refs[count + 1 : count + 3]
    below, above, v_below, v_above = refs[count + 3 : count + 7]
    del refs[: count + 7]
    deposit = None if last else refs.pop(0)
    out = refs.pop(0)
    packs = None if last else (refs.pop(0), refs.pop(0))
    q, uv, sz, fall, fx, lx, stage, in_sem, out_sem = refs[:9]
    kept = refs[9:11]
    comps, slabs, tiles = q.shape[1], q.shape[2], sz.shape[2]
    chunk, flight = (8, 3) if last else (4, 6)
    chunks = slabs // chunk

    def fetch(j, first, final):
        span = pl.ds(j * chunk, chunk)
        if last:
            middle, low, high = fields
            begin, size = j * chunk, chunk
            if first:
                begin, size = begin + 2, size - 2
                start(low, q.at[0, :, pl.ds(0, 2)], in_sem.at[j, 0])
            if final:
                size -= 2
                start(high, q.at[0, :, pl.ds(slabs - 2, 2)], in_sem.at[j, 0])
            part = pl.ds(begin, size)
            start(middle.at[:, part], q.at[0, :, part], in_sem.at[j, 0])
        else:
            pair = (lambda n: fields[0].at[:, span, n], lambda n: q.at[0, :, span, :, n])
            start_sets([pair], in_sem.at[j, 0])
        pair = (lambda n: velocity.at[pl.ds(0, 2), span, n], lambda n: uv.at[0, :, span, :, n])
        start_sets([pair], in_sem.at[j, 1])
        for n, (source, target) in enumerate(zip(speeds, (sz, fall))):
            start(source.at[span], target.at[0, span], in_sem.at[j, n + 2])

    for j in range(flight):
        fetch(j, j == 0, False)

    def arrive(j):
        span = pl.ds(j * chunk, chunk)
        arrived(q.at[0, :, span], in_sem.at[j, 0])
        for n, spot in enumerate((uv.at[0, :, span], sz.at[0, span], fall.at[0, span])):
            arrived(spot, in_sem.at[j, n + 1])
        later = j + flight

        @pl.when(later < chunks - 1)
        def _():
            fetch(later, False, False)

        @pl.when(later == chunks - 1)
        def _():
            fetch(chunks - 1, False, True)

        def complete(x, _):
            staged([functools.partial(dust_job, q, 0, x, falling(deposit, x + 2))])
            return 0

        if not last:
            lax.fori_loop(j * chunk, jnp.minimum((j + 1) * chunk, groups), complete, 0)

    f = Slabs(q, uv, sz, fall, fx, lx, 0, 2, 2, (below, above, v_below, v_above), 2, kept)
    arrive(jnp.int32(0))
    first_face(f)

    def step(k, _):
        @pl.when((k + 4) % chunk == 0)
        def _():
            arrive((k + 4) // chunk)

        def put(c, t, value):
            stage[c, k, t] = value

        slab_step(f, k, put, 4 if last else 2)
        if last:
            start_sets([(lambda n: stage.at[:, k, :, n], lambda n: out.at[:, k + 2, n])], out_sem)
        else:
            start(stage.at[:, k], out.at[:, k + 2], out_sem)
        if not last:
            pack_edges(packs, lambda c: stage.at[c, k], comps, k + 2)
        return 0

    if not last:
        for pack in packs:
            pack[...] = jnp.zeros_like(pack)
    lax.fori_loop(0, slabs - 4, step, 0)
    arrived(stage, out_sem)


def interior(groups, fields, velocity, speeds, below, above, v_below, v_above, deposit=None):
    last = deposit is None
    slabs, tiles, _, lanes = speeds[0].shape
    rows, comps = 8 * tiles, fields[0].shape[0]
    operands = list(fields) + [velocity, *speeds, below, above, v_below, v_above]
    specs = [ANY] * (len(fields) + 3) + [VMEM] * 4
    form = (8, tiles, lanes) if last else (tiles, 8, lanes)
    out_shape = [jax.ShapeDtypeStruct((comps, slabs, *form), jnp.float32)]
    out_specs = [ANY]
    scratch = [
        pltpu.VMEM((1, comps, slabs, tiles, 8, lanes), jnp.float32),
        pltpu.VMEM((1, 2, slabs, tiles, 8, lanes), jnp.float32),
        *[pltpu.VMEM((1, slabs, tiles, 8, lanes), jnp.float32)] * 2,
        pltpu.VMEM((tiles, comps, 8, lanes), jnp.float32),
        pltpu.VMEM((tiles, comps, 8, lanes), jnp.float32),
        pltpu.VMEM((comps, slabs - 4, tiles, 8, lanes), jnp.float32),
        pltpu.SemaphoreType.DMA((slabs // 4, 5)),
        pltpu.SemaphoreType.DMA,
    ]
    scratch += [pltpu.VMEM((tiles, comps, 8, lanes), jnp.float32)] * 2
    if not last:
        out_shape += [jax.ShapeDtypeStruct((2 * comps, slabs, lanes), jnp.float32)] * 2
        out_specs += [VMEM] * 2
        operands.append(deposit)
        specs.append(VMEM)
    cells = comps * (slabs - 4) * rows * lanes
    return pl.pallas_call(
        functools.partial(interior_kernel, last, groups, len(fields)),
        out_shape=tuple(out_shape),
        in_specs=specs,
        out_specs=tuple(out_specs),
        scratch_shapes=scratch,
        compiler_params=params(),
        cost_estimate=cost(40 * cells, 4 * (2 * cells + 4 * slabs * rows * lanes)),
        name="interior",
    )(*operands)


def boundary_kernel(last, groups, slabs, *refs):
    refs = list(refs)
    count = 5 if last else 3
    fields, velocity, speeds = refs[:count], refs[count], refs[count + 1 : count + 3]
    u_outer = refs[count + 3 : count + 5]
    below, above, v_below, v_above = refs[count + 5 : count + 9]
    del refs[: count + 9]
    if last:
        out = refs[1]
        del refs[:2]
    else:
        deposit, packed, ends, packs = refs[0], refs[1:3], refs[3:5], refs[5:7]
        del refs[:7]
    q, uv, sz, fall, fx, lx, stage, in_sem, out_sem = refs
    comps, tiles = q.shape[1], sz.shape[2]

    if last:
        middle, end_low, end_high, x_low, x_high = fields
        for block, at, source in (
            (0, 0, x_low), (0, 2, end_low), (0, 4, middle.at[:, pl.ds(2, 2)]),
            (1, 0, middle.at[:, pl.ds(slabs - 4, 2)]), (1, 2, end_high), (1, 4, x_high),
        ):
            start(source, q.at[block, :, pl.ds(at, 2)], in_sem.at[block, 0])
    else:
        state, x_low, x_high = fields
        for block, at, first in ((0, 2, 0), (1, 0, slabs - 4)):
            pair = (
                lambda n: state.at[:, pl.ds(first, 4), n], lambda n: q.at[block, :, pl.ds(at, 4), :, n]
            )
            start_sets([pair], in_sem.at[block, 0])
        for block, at, halo in ((0, 0, x_low), (1, 4, x_high)):
            pairs = [
                (lambda n, c=c: halo.at[pl.ds(2 * c, 2), n], lambda n, c=c: q.at[block, c, pl.ds(at, 2), :, n])
                for c in range(comps)
            ]
            start_sets(pairs, in_sem.at[block, 0])
    edge = pl.ds(2 * comps, 1)
    for block in range(2):
        outer, first, at = 3 * block, block * (slabs - 3), 1 - block
        pairs = [
            (lambda n: u_outer[block].at[edge, n], lambda n: uv.at[block, 0, pl.ds(outer, 1), :, n]),
            (
                lambda n: velocity.at[pl.ds(0, 2), pl.ds(first, 3), n],
                lambda n: uv.at[block, :, pl.ds(at, 3), :, n],
            ),
        ]
        for number, pair in enumerate(pairs):
            start_sets([pair], in_sem.at[block, number + 1])
        span = pl.ds(block * (slabs - 2), 2)
        for n, target in enumerate((sz, fall)):
            start(speeds[n].at[span], target.at[block], in_sem.at[block, n + 3])
    if not last:
        packs[0][...] = packed[0][...]
        packs[1][...] = packed[1][...]

    def one(block, _):
        begin = block * (slabs - 2)
        arrived(q.at[block], in_sem.at[block, 0])
        spots = (uv.at[block, 0, pl.ds(0, 1)], uv.at[block, :, pl.ds(0, 3)], sz.at[block], fall.at[block])
        for n, spot in enumerate(spots):
            arrived(spot, in_sem.at[block, n + 1])

        def complete(slab, _):
            x = begin + slab - 2
            lands = (x >= slabs) | ((x >= 0) & (x < groups)) | (x + slabs < groups)

            @pl.when(lands)
            def _():
                staged([functools.partial(dust_job, q, block, slab, falling(deposit, x + 2))])

            return 0

        if not last:
            lax.fori_loop(0, 6, complete, 0)
        f = Slabs(q, uv, sz, fall, fx, lx, block, 1, 0, (below, above, v_below, v_above), begin)
        first_face(f)

        def step(k, _):
            def put(c, t, value):
                stage[block, c, k, t] = value

            slab_step(f, k, put)
            if not last:
                pack_edges(packs, lambda c: stage.at[block, c, k], comps, begin + k)
            return 0

        lax.fori_loop(0, 2, step, 0)
        if last:
            span = pl.ds(begin, 2)
            pair = (lambda n: stage.at[block, :, :, :, n], lambda n: out.at[:, span, n])
            start_sets([pair], out_sem.at[block])
        else:
            for number in range(2):

                @pl.when(block == number)
                def _():
                    start(stage.at[number], ends[number], out_sem.at[number])

        return 0

    lax.fori_loop(0, 2, one, 0)
    for block in range(2):
        arrived(stage.at[block], out_sem.at[block])


def boundary(groups, fields, velocity, speeds, u_outer, below, above, v_below, v_above, *, deposit=None, packed=None, out=None):
    last = out is not None
    slabs, tiles, _, lanes = speeds[0].shape
    rows, comps = 8 * tiles, fields[0].shape[0]
    operands = list(fields) + [velocity, *speeds, *u_outer, below, above, v_below, v_above]
    specs = [ANY] * (len(fields) + 5) + [VMEM] * 4
    form = (tiles, 8, lanes)
    scratch = [
        pltpu.VMEM((2, comps, 6, tiles, 8, lanes), jnp.float32),
        pltpu.VMEM((2, 2, 4, tiles, 8, lanes), jnp.float32),
        *[pltpu.VMEM((2, 2, tiles, 8, lanes), jnp.float32)] * 2,
        pltpu.VMEM((tiles, comps, 8, lanes), jnp.float32),
        pltpu.VMEM((tiles, comps, 8, lanes), jnp.float32),
        pltpu.VMEM((2, comps, 2, *form), jnp.float32),
        pltpu.SemaphoreType.DMA((2, 5)),
        pltpu.SemaphoreType.DMA((2,)),
    ]
    if last:
        aliases = {len(operands): 0}
        operands.append(out)
        specs.append(ANY)
        out_shape = jax.ShapeDtypeStruct(out.shape, out.dtype)
        out_specs = ANY
    else:
        aliases = {}
        operands += [deposit, *packed]
        specs += [VMEM] * 3
        out_shape = (jax.ShapeDtypeStruct((comps, 2, *form), jnp.float32),) * 2
        out_shape += (jax.ShapeDtypeStruct((2 * comps, slabs, lanes), jnp.float32),) * 2
        out_specs = (ANY, ANY, VMEM, VMEM)
    cells = comps * 4 * rows * lanes
    return pl.pallas_call(
        functools.partial(boundary_kernel, last, groups, slabs),
        out_shape=out_shape,
        in_specs=specs,
        out_specs=out_specs,
        scratch_shapes=scratch,
        input_output_aliases=aliases,
        compiler_params=params(),
        cost_estimate=cost(50 * cells, 4 * 6 * cells),
        name="boundary",
    )(*operands)


def speeds_kernel(velocity, sz, fall, wind, sems):
    step = pl.program_id(0)
    part, count, lanes = sz.shape[0], wind.shape[1], wind.shape[3]
    lane = lax.broadcasted_iota(jnp.int32, (8, lanes), 1)
    is_first, is_last = lane == 0, lane == lanes - 1

    @pl.when(step == 0)
    def _():
        for j in range(wind.shape[0] // part):
            span = pl.ds(j * part, part)
            start_sets([(lambda n: velocity.at[2, span, n], lambda n: wind.at[span, :, n])], sems.at[j])

    arrived(wind.at[pl.ds(step * part, part)], sems.at[step])

    def one(x, _):
        here = [FACTOR * wind[step * part + x, t] for t in range(count)]
        over = [pltpu.roll(tile, lanes - 1, 1) for tile in here]
        under = [pltpu.roll(tile, 1, 1) for tile in here]
        upper = [jnp.where(is_last, jnp.maximum(a, 0.0), a + b) for a, b in zip(here, over)]
        lower = [jnp.where(is_first, jnp.minimum(a, 0.0), a + b) for a, b in zip(here, under)]
        for t in range(count):
            sz[x, t] = upper[t]
            fall[x, t] = lower[t]
        return 0

    lax.fori_loop(0, part, one, 0)


def face_speeds(velocity):
    _, slabs, _, tiles, lanes = velocity.shape
    part = 8
    return pl.pallas_call(
        speeds_kernel,
        grid=(slabs // part,),
        out_shape=(jax.ShapeDtypeStruct((slabs, tiles, 8, lanes), jnp.float32),) * 2,
        in_specs=[ANY],
        out_specs=(pl.BlockSpec((part, tiles, 8, lanes), lambda i: (i, 0, 0, 0)),) * 2,
        scratch_shapes=[
            pltpu.VMEM((slabs, tiles, 8, lanes), jnp.float32),
            pltpu.SemaphoreType.DMA((slabs // part,)),
        ],
        compiler_params=params(),
        cost_estimate=cost(8 * slabs * 8 * tiles * lanes, 12 * slabs * 8 * tiles * lanes),
        name="face_speeds",
    )(velocity)


def x_copies(state, velocity, low, high, sems):
    comps, slabs = state.shape[0], state.shape[1]
    copies = []
    for n, (target, first, edge) in enumerate(((low, 0, 0), (high, slabs - 2, slabs - 1))):
        pairs = [(state.at[c, pl.ds(first, 2)], target.at[pl.ds(2 * c, 2)]) for c in range(comps)]
        pairs.append((velocity.at[0, pl.ds(edge, 1)], target.at[pl.ds(2 * comps, 1)]))
        copies += [pltpu.make_async_copy(*pair, sems.at[n, i]) for i, pair in enumerate(pairs)]
    return copies


def as_column(row):
    count = row.shape[1]
    shape = (count, count)
    same = lax.broadcasted_iota(jnp.int32, shape, 0) == lax.broadcasted_iota(jnp.int32, shape, 1)
    return jnp.sum(jnp.where(same, row, 0.0), axis=1, keepdims=True)


def stress_kernel(wind, stress, gathered):
    step, steps = pl.program_id(0), pl.num_programs(0)
    part, rows, lanes = wind.shape[1:]
    slabs = stress.shape[0]
    lane = lax.broadcasted_iota(jnp.int32, (rows, lanes), 1)
    weight = jnp.zeros((rows, lanes), jnp.float32)
    for level, value in enumerate(profile_weights):
        weight = jnp.where(lane == level, value, weight)
    total = jnp.zeros((rows, lanes), jnp.float32)
    for x in range(part):
        east, north = wind[0, x], wind[1, x]
        friction = jnp.where(lane < LEVELS, weight * (east * east + north * north), 0.0)
        total = total + pltpu.roll(friction, LEVELS * x, 1) if x else friction

    @pl.when(step == 0)
    def _():
        gathered[...] = total

    @pl.when(step > 0)
    def _():
        gathered[...] += pltpu.roll(total, LEVELS * part * step, 1)

    @pl.when(step == steps - 1)
    def _():
        gathered[...] = gathered[...].T
        total = gathered[pl.ds(0, slabs, stride=LEVELS), :]
        for level in range(1, LEVELS):
            total = total + gathered[pl.ds(level, slabs, stride=LEVELS), :]
        stress[...] = total


def tile_stress(velocity):
    _, slabs, rows, lanes = velocity.shape
    part = 8
    return pl.pallas_call(
        stress_kernel,
        grid=(slabs // part,),
        out_shape=jax.ShapeDtypeStruct((slabs, lanes), jnp.float32),
        in_specs=[pl.BlockSpec((2, part, rows, lanes), lambda i: (0, i, 0, 0))],
        out_specs=pl.BlockSpec((slabs, lanes), lambda i: (0, 0)),
        scratch_shapes=[pltpu.VMEM((rows, lanes), jnp.float32)],
        compiler_params=params(),
        cost_estimate=cost(10 * slabs * rows * lanes, 80 * slabs * rows * lanes),
        name="tile_stress",
    )(velocity)


def pack_kernel(low_in, high_in, v_low, v_high, state, velocity, low, high, x_low, x_high, sems):
    step, steps = pl.program_id(0), pl.num_programs(0)
    comps, part = low_in.shape[:2]

    @pl.when(step == 0)
    def _():
        for copy in x_copies(state, velocity, x_low, x_high, sems):
            copy.start()

    for x in range(part):
        for c in range(comps):
            for r in range(2):
                low[2 * c + r, x : x + 1, :] = low_in[c, x, r : r + 1, :]
                high[2 * c + r, x : x + 1, :] = high_in[c, x, 6 + r : 7 + r, :]
        low[2 * comps, x : x + 1, :] = v_low[0, x, 0:1, :]
        high[2 * comps, x : x + 1, :] = v_high[0, x, 7:8, :]

    @pl.when(step == steps - 1)
    def _():
        for copy in x_copies(state, velocity, x_low, x_high, sems):
            copy.wait()


def pack(state, velocity):
    comps, slabs, rows, lanes = state.shape
    part = 8
    last = rows // 8 - 1
    packed = jax.ShapeDtypeStruct((2 * comps + 1, slabs, lanes), jnp.float32)
    packed_spec = pl.BlockSpec((2 * comps + 1, part, lanes), lambda i: (0, i, 0))
    x_packed = jax.ShapeDtypeStruct((2 * comps + 1, rows, lanes), jnp.float32)
    return pl.pallas_call(
        pack_kernel,
        grid=(slabs // part,),
        out_shape=(packed, packed, x_packed, x_packed),
        in_specs=[
            pl.BlockSpec((comps, part, 8, lanes), lambda i: (0, i, 0, 0)),
            pl.BlockSpec((comps, part, 8, lanes), lambda i: (0, i, last, 0)),
            pl.BlockSpec((1, part, 8, lanes), lambda i: (1, i, 0, 0)),
            pl.BlockSpec((1, part, 8, lanes), lambda i: (1, i, last, 0)),
            ANY,
            ANY,
        ],
        out_specs=(packed_spec, packed_spec, ANY, ANY),
        scratch_shapes=[pltpu.SemaphoreType.DMA((2, comps + 1))],
        compiler_params=params(),
        cost_estimate=cost(1, 12 * (2 * comps + 1) * rows * lanes),
        name="pack",
    )(state, state, velocity, velocity, state, velocity)


def census_kernel(stress, threshold, tile_owner, parcel_owner, count, share, copies):
    groups, height, lanes = copies.shape
    slabs = stress.shape[0]
    owners = parcel_owner[...].astype(jnp.float32)
    shape = (groups, slabs)
    place = (owners == lax.broadcasted_iota(jnp.int32, shape, 0).astype(jnp.float32)).astype(jnp.float32)
    live = as_column(count[...].astype(jnp.float32))
    shape = (slabs, lanes)
    reach = lax.broadcasted_iota(jnp.int32, shape, 1).astype(jnp.float32) < live
    masses = jnp.where(reach, share[0], 0.0)
    copies[0, 0:slabs] = stress[...]
    copies[0, slabs : slabs + 8] = jnp.zeros((8, lanes), jnp.float32)
    copies[0, slabs : slabs + 1] = threshold[...]
    copies[0, slabs + 1 : slabs + 2, 0:slabs] = tile_owner[...].astype(jnp.float32)
    copies[0, slabs + 8 : height] = jnp.dot(place, masses, precision=HIGHEST, preferred_element_type=jnp.float32)
    whole = copies[0]
    for g in range(1, groups):
        copies[g] = whole


def census(groups, stress, *small):
    slabs, lanes = stress.shape
    return pl.pallas_call(
        census_kernel,
        out_shape=jax.ShapeDtypeStruct((groups, slabs + 8 + groups, lanes), jnp.float32),
        in_specs=[VMEM] * 6,
        out_specs=VMEM,
        compiler_params=params(),
        cost_estimate=cost(10**6, 10**6),
        name="census",
    )(stress, *small)


def deposit_kernel(slabs, me, gathered, low_in, high_in, flux_out, deposit, low, high, flux, dropped):
    groups, lanes = gathered.shape[0], gathered.shape[2]
    here = me[0]
    limits = jnp.concatenate([gathered[g, slabs : slabs + 1] for g in range(groups)], axis=0)
    total = jnp.zeros((groups, lanes), jnp.float32)
    shape = (groups, slabs)
    numbers = lax.broadcasted_iota(jnp.int32, shape, 0).astype(jnp.float32)
    for g in range(groups):
        owners = gathered[g, slabs + 1 : slabs + 2, 0:slabs]
        stress = gathered[g, 0:slabs]
        named = (owners == numbers).astype(jnp.float32)
        limit = lax.dot_general(
            named, limits, (((0,), (0,)), ((), ())), precision=HIGHEST, preferred_element_type=jnp.float32
        )
        lifting = jnp.maximum(stress - limit, 0.0)
        total = total + jnp.dot(named, lifting, precision=HIGHEST, preferred_element_type=jnp.float32)
    flux[...] = total / slabs
    flux_out[...] = flux[pl.ds(here, 1), :]
    dropped[...] = jnp.zeros_like(dropped)
    before, after = jnp.maximum(here - 1, 0), jnp.minimum(here + 1, groups - 1)
    has_before, has_after = here > 0, here < groups - 1
    base = slabs + 8
    for p in range(groups):
        x = p % slabs
        row = flux[p : p + 1, :]
        dropped[x + 2 : x + 3] += row * gathered[p, pl.ds(base + here, 1), :]
        if x >= slabs - 2:
            mass = row * gathered[p, pl.ds(base + before, 1), :]
            dropped[x - slabs + 2 : x - slabs + 3] += jnp.where(has_before, mass, 0.0)
        if x < 2:
            mass = row * gathered[p, pl.ds(base + after, 1), :]
            dropped[x + slabs + 2 : x + slabs + 3] += jnp.where(has_after, mass, 0.0)
    own = dropped[2 : 2 + slabs, :]
    dropped[...] = dropped[...].T
    count = deposit.shape[0]
    tiles = [tile_of(dropped, t, count) for t in range(count)]
    for t, tile in enumerate(tiles):
        deposit[t] = tile
    lane = lax.broadcasted_iota(jnp.int32, (slabs, lanes), 1)
    rows = lanes
    dust = low.shape[0] - 3
    low[...] = low_in[...]
    high[...] = high_in[...]
    for r in range(2):
        low[dust + r] += jnp.where(lane == 0, own[:, r : r + 1], 0.0)
        high[dust + r] += jnp.where(lane == 0, own[:, rows - 2 + r : rows - 1 + r], 0.0)


def settle(me, gathered, low, high, slabs):
    groups, _, lanes = gathered.shape
    edge = jax.ShapeDtypeStruct(low.shape, jnp.float32)
    return pl.pallas_call(
        functools.partial(deposit_kernel, slabs),
        out_shape=(
            jax.ShapeDtypeStruct((1, lanes), jnp.float32),
            jax.ShapeDtypeStruct((lanes // 8, 8, lanes), jnp.float32),
            edge,
            edge,
        ),
        in_specs=[SMEM, VMEM, VMEM, VMEM],
        out_specs=(VMEM, VMEM, VMEM, VMEM),
        scratch_shapes=[
            pltpu.VMEM((groups, lanes), jnp.float32),
            pltpu.VMEM((lanes, lanes), jnp.float32),
        ],
        compiler_params=params(),
        cost_estimate=cost(10**6, 10**6),
        name="settle",
    )(me, gathered, low, high)


def exchange(low, high, axis):
    count = lax.axis_size(axis)
    forward = [(i, i + 1) for i in range(count - 1)]
    backward = [(target, source) for source, target in forward]
    return lax.ppermute(high, axis, forward), lax.ppermute(low, axis, backward)


def shards(state, velocity, threshold, tile_owner, parcel_owner, parcel_count, parcel_share):
    groups = lax.axis_size("gx")
    slabs = state.shape[1]
    me = lax.axis_index("gx").astype(jnp.int32).reshape(1)

    stress = tile_stress(velocity)
    low, high, own_low, own_high = pack(state, velocity)
    copies = census(
        groups, stress, threshold, tile_owner[:, :, 0], parcel_owner[:, :, 0], parcel_count, parcel_share
    )
    rows, lanes = state.shape[2:]

    def sets(array):
        return array.reshape(*array.shape[:-2], 8, rows // 8, lanes)

    velocity = sets(velocity)
    speeds = face_speeds(velocity)
    gathered = lax.all_to_all(copies, "gx", split_axis=0, concat_axis=0, tiled=True)
    flux, deposit, low, high = settle(me, gathered, low, high, slabs)
    below, above = exchange(low, high, "gy")
    own_low, own_high, _ = lax.optimization_barrier((own_low, own_high, gathered))
    x_low, x_high = exchange(own_low, own_high, "gx")
    x_low, x_high = sets(x_low), sets(x_high)
    u_edges = (x_low, x_high)
    middle, pack_low, pack_high = interior(groups, [sets(state)], velocity, speeds, below, above, below, above, deposit)
    end_low, end_high, y_low, y_high = boundary(
        groups, [sets(state), x_low, x_high], velocity, speeds, u_edges, below, above, below, above,
        deposit=deposit, packed=(pack_low, pack_high),
    )
    x2_low, x2_high = exchange(end_low, end_high, "gx")
    below2, above2 = exchange(y_low, y_high, "gy")
    (inside,) = interior(groups, [middle, end_low, end_high], velocity, speeds, below2, above2, below, above)
    fields = boundary(
        groups, [middle, end_low, end_high, x2_low, x2_high], velocity, speeds, u_edges, below2, above2, below, above,
        out=inside,
    )
    return fields.reshape(state.shape), flux


def solution(mesh):
    return jax.shard_map(
        shards,
        mesh=mesh,
        in_specs=(
            P(None, "gx", "gy", None),
            P(None, "gx", "gy", None),
            P("gx", "gy"),
            P("gy", "gx", None),
            P("gy", "gx", None),
            P("gy", "gx"),
            P("gy", "gx", None),
        ),
        out_specs=(P(None, "gx", "gy", None), P("gx", "gy")),
        check_vma=False,
    )
```

```python
import functools

import jax
import jax.numpy as jnp
from jax import lax
from jax.experimental import pallas as pl
from jax.experimental.pallas import tpu as pltpu
from jax.sharding import PartitionSpec as P

LEVELS = 4
profile_weights = (0.4, 0.3, 0.2, 0.1)
time_step = 0.1
FACTOR = 0.25 * time_step

VMEM_LIMIT = 48 * 1024 * 1024
PAIR = 2
HIGHEST = lax.Precision.HIGHEST
ANY = pl.BlockSpec(memory_space=pl.ANY)
VMEM = pl.BlockSpec(memory_space=pltpu.VMEM)
SMEM = pl.BlockSpec(memory_space=pltpu.SMEM)


def params():
    return pltpu.CompilerParams(vmem_limit_bytes=VMEM_LIMIT)


def cost(flops, moved):
    return pl.CostEstimate(flops=int(flops), bytes_accessed=int(moved), transcendentals=0)


def minmod(a, b):
    return jnp.maximum(jnp.minimum(a, b), jnp.minimum(jnp.maximum(a, b), 0.0))


def tile_of(ref, t, tiles):
    return ref[pl.ds(t, 8, stride=tiles), :]


class Slabs:
    def __init__(self, q, uv, sz, fall, fx, lx, block, x_at, at, halo, x, kept=None):
        self.q, self.uv, self.sz, self.falls, self.fx, self.lx = q, uv, sz, fall, fx, lx
        self.block, self.x_at, self.at, self.kept = block, x_at, at, kept
        self.halo, self.x = halo, x
        self.comps, self.tiles, self.lanes = q.shape[1], sz.shape[2], q.shape[-1]

    def field(self, c, slab, t):
        return self.q[self.block, c, slab, t]

    def row(self, k, which, number):
        return self.halo[which][number, pl.ds(self.x + k, 1), :]

    def centre(self, c, k, t):
        slab = k + 2
        if 0 <= t < self.tiles:
            return self.field(c, slab, t)
        row = lax.broadcasted_iota(jnp.int32, (8, self.lanes), 0)
        if t < 0:
            moved = pltpu.roll(self.field(c, slab, t + self.tiles), 1, 0)
            return jnp.where(row == 0, self.row(k, 0, 2 * c + t + 2), moved)
        t -= self.tiles
        return jnp.where(row == 7, self.row(k, 1, 2 * c + t), pltpu.roll(self.field(c, slab, t), 7, 0))

    def east(self, k, t):
        here = k + self.x_at
        return FACTOR * (self.uv[self.block, 0, here, t] + self.uv[self.block, 0, here + 1, t])

    def wind(self, k, t):
        inner = self.uv[self.block, 1, k + self.x_at, t % self.tiles]
        if 0 <= t < self.tiles:
            return inner
        row = lax.broadcasted_iota(jnp.int32, (8, self.lanes), 0)
        end, turn, which = (0, 1, 2) if t < 0 else (7, 7, 3)
        return jnp.where(row == end, self.row(k, which, 2 * self.comps), pltpu.roll(inner, turn, 0))

    def north(self, k, t):
        return FACTOR * (self.wind(k, t) + self.wind(k, t + 1))

    def up(self, k, t):
        return self.sz[self.block, k + self.at, t]

    def down(self, k, t):
        return self.falls[self.block, k + self.at, t]


def each(function, *lists):
    return [function(*items) for items in zip(*lists)]


def minmods(a, b):
    low, high = each(jnp.minimum, a, b), each(jnp.maximum, a, b)
    high = each(lambda x: jnp.minimum(x, 0.0), high)
    return each(jnp.maximum, low, high)


def difference(a, b):
    return each(lambda x, y: x - y, a, b)


def total_of(a, b):
    return each(lambda x, y: x + y, a, b)


def face_flux(speeds, masks, low_side, high_side):
    picked = each(jnp.where, masks, low_side, high_side)
    return each(lambda x, y: x * y, speeds, picked)


def staged(jobs):
    waiting = []
    for job in jobs:
        stores = job()
        for ref, index, value in waiting:
            ref[index] = value
        waiting = stores
    for ref, index, value in waiting:
        ref[index] = value


def first_face(f):
    def job(ts):
        spots = [(t, c) for t in ts for c in range(f.comps)]
        speeds = {t: f.east(-1, t) for t in ts}
        masks = {t: speeds[t] > 0 for t in ts}
        a, b, q0, q1 = [[f.field(c, slab, t) for t, c in spots] for slab in range(4)]
        middle = difference(q0, b)
        left = total_of(total_of(b, b), minmods(middle, difference(b, a)))
        slope = minmods(difference(q1, q0), middle)
        twice = total_of(q0, q0)
        flux = face_flux([speeds[t] for t, _ in spots], [masks[t] for t, _ in spots], left, difference(twice, slope))
        stores = [(f.fx, spot, x) for spot, x in zip(spots, flux)]
        if f.kept is not None:
            stores += [(f.kept[0], spot, x) for spot, x in zip(spots, twice)]
            stores += [(f.kept[1], spot, x) for spot, x in zip(spots, difference(q1, q0))]
        return stores + [(f.lx, spot, x) for spot, x in zip(spots, total_of(twice, slope))]

    staged([functools.partial(job, range(t, t + PAIR)) for t in range(0, f.tiles, PAIR)])


def slab_step(f, k, put, group_size=4):
    slab = k + 2
    lane = lax.broadcasted_iota(jnp.int32, (8, f.lanes), 1)
    top = f.lanes - 1
    is_first, is_last = lane == 0, lane == top
    carry = []
    speed = f.north(k, -1)
    for c in range(f.comps):
        a, b, q0, q1 = [f.centre(c, k, t) for t in (-2, -1, 0, 1)]
        middle, ahead = q0 - b, q1 - q0
        left_state = (b + b) + minmod(middle, b - a)
        slope = minmod(ahead, middle)
        twice = q0 + q0
        flux = speed * jnp.where(speed > 0, left_state, twice - slope)
        carry.append((q0, q1, ahead, twice, twice + slope, flux))
    states, doubles = {}, {}

    def vertical(t):
        for c in range(f.comps):
            q0 = f.field(c, slab, t)
            over = jnp.where(is_last, 0.0, pltpu.roll(q0, top, 1))
            under = jnp.where(is_first, 0.0, pltpu.roll(q0, 1, 1))
            slope = minmod(over - q0, q0 - under)
            if f.kept is not None:
                doubles[c, t] = f.kept[0][t, c]
            twice = double(c, t, q0)
            states[t, c] = (twice - slope, twice + slope)

    def flush(held):
        for c, t, flux_x, left_x, twice_x, step_x, value in held:
            f.fx[t, c], f.lx[t, c] = flux_x, left_x
            if f.kept is not None:
                f.kept[0][t, c], f.kept[1][t, c] = twice_x, step_x
            put(c, t, value)

    def double(c, t, tile):
        if f.kept is None or not 0 <= t < f.tiles:
            return tile + tile
        return doubles[c, t]

    held = []
    for t in range(group_size):
        vertical(t)
    for begin in range(0, f.tiles, group_size):
        group = range(begin, min(begin + group_size, f.tiles))
        for t in range(begin + group_size, min(begin + 2 * group_size, f.tiles)):
            vertical(t)
        loaded = {}
        for t in group:
            loaded[t] = (f.east(k, t), f.north(k, t), f.up(k, t), f.down(k, t))
            for c in range(f.comps):
                loaded[t, c] = (
                    f.centre(c, k, t + 2), f.field(c, slab + 1, t), f.field(c, slab + 2, t),
                    f.fx[t, c], f.lx[t, c], f.kept[1][t, c] if f.kept is not None else None,
                )
        flush(held)
        held = []
        for t in group:
            speed_x, speed_y, speed_z, fall = loaded[t]
            go_x, go_y, go_z, go_fall = speed_x > 0, speed_y > 0, speed_z > 0, fall > 0
            for c in range(f.comps):
                y2, x1, x2, flux_w, left_w, step_w = loaded[t, c]
                q0, y1, ahead, twice, left_y, flux_y = carry[c]
                beyond = y2 - y1
                slope = minmod(beyond, ahead)
                twice_y = double(c, t + 1, y1)
                flux_next = speed_y * jnp.where(go_y, left_y, twice_y - slope)
                total = flux_next - flux_y
                carry[c] = (y1, y2, beyond, twice_y, twice_y + slope, flux_next)
                step_x = x2 - x1
                slope = minmod(step_x, x1 - q0 if step_w is None else step_w)
                twice_x = x1 + x1
                flux_x = speed_x * jnp.where(go_x, left_w, twice_x - slope)
                left_x = twice_x + slope
                total = total + (flux_x - flux_w)
                lower, upper = states[t, c]
                flux_z = speed_z * jnp.where(go_z, upper, pltpu.roll(lower, top, 1))
                flux_below = fall * jnp.where(go_fall, pltpu.roll(upper, 1, 1), lower)
                total = total + (flux_z - flux_below)
                held.append((c, t, flux_x, left_x, twice_x, step_x, q0 - total))
    flush(held)


def dust_job(q, block, slab, dust):
    c, spots = q.shape[1] - 1, range(q.shape[3])
    tiles = total_of([q[block, c, slab, t] for t in spots], dust(spots))
    return [(q, (block, c, slab, t), tile) for t, tile in zip(spots, tiles)]


def falling(deposit, column):
    lanes = deposit.shape[-1]

    def dust(spots):
        parts = [pltpu.roll(deposit[t], lanes - column, 1) for t in spots]
        lane = lax.broadcasted_iota(jnp.int32, parts[0].shape, 1)
        return [jnp.where(lane == 0, part, 0.0) for part in parts]

    return dust


def pack_edges(packs, stage_slab, comps, x):
    x = pl.ds(x, 1)
    stores = []
    for c in range(comps):
        tiles = stage_slab(c)
        count = tiles.shape[0]
        for r in range(2):
            stores.append((packs[0], (2 * c + r, x), tiles[r, 0:1, :]))
            stores.append((packs[1], (2 * c + r, x), tiles[count - 2 + r, 7:8, :]))
    staged([lambda: stores])


def start(source, target, sem):
    pltpu.make_async_copy(source, target, sem).start()


def start_sets(pairs, sem):
    for source, target in pairs:
        for number in range(8):
            start(source(number), target(number), sem)


def arrived(spot, sem):
    pltpu.make_async_copy(spot, spot, sem).wait()


def interior_kernel(last, groups, count, *refs):
    refs = list(refs)
    fields, velocity, speeds = refs[:count], refs[count], refs[count + 1 : count + 3]
    below, above, v_below, v_above = refs[count + 3 : count + 7]
    del refs[: count + 7]
    deposit = None if last else refs.pop(0)
    out = refs.pop(0)
    packs = None if last else (refs.pop(0), refs.pop(0))
    q, uv, sz, fall, fx, lx, stage, in_sem, out_sem = refs[:9]
    kept = refs[9:11]
    comps, slabs, tiles = q.shape[1], q.shape[2], sz.shape[2]
    chunk, flight = (8, 3) if last else (4, 6)
    chunks = slabs // chunk

    def fetch(j, first, final):
        span = pl.ds(j * chunk, chunk)
        if last:
            middle, low, high = fields
            begin, size = j * chunk, chunk
            if first:
                begin, size = begin + 2, size - 2
                start(low, q.at[0, :, pl.ds(0, 2)], in_sem.at[j, 0])
            if final:
                size -= 2
                start(high, q.at[0, :, pl.ds(slabs - 2, 2)], in_sem.at[j, 0])
            part = pl.ds(begin, size)
            start(middle.at[:, part], q.at[0, :, part], in_sem.at[j, 0])
        else:
            pair = (lambda n: fields[0].at[:, span, n], lambda n: q.at[0, :, span, :, n])
            start_sets([pair], in_sem.at[j, 0])
        pair = (lambda n: velocity.at[pl.ds(0, 2), span, n], lambda n: uv.at[0, :, span, :, n])
        start_sets([pair], in_sem.at[j, 1])
        for n, (source, target) in enumerate(zip(speeds, (sz, fall))):
            start(source.at[span], target.at[0, span], in_sem.at[j, n + 2])

    for j in range(flight):
        fetch(j, j == 0, False)

    def arrive(j):
        span = pl.ds(j * chunk, chunk)
        arrived(q.at[0, :, span], in_sem.at[j, 0])
        for n, spot in enumerate((uv.at[0, :, span], sz.at[0, span], fall.at[0, span])):
            arrived(spot, in_sem.at[j, n + 1])
        later = j + flight

        @pl.when(later < chunks - 1)
        def _():
            fetch(later, False, False)

        @pl.when(later == chunks - 1)
        def _():
            fetch(chunks - 1, False, True)

        def complete(x, _):
            staged([functools.partial(dust_job, q, 0, x, falling(deposit, x + 2))])
            return 0

        if not last:
            lax.fori_loop(j * chunk, jnp.minimum((j + 1) * chunk, groups), complete, 0)

    f = Slabs(q, uv, sz, fall, fx, lx, 0, 2, 2, (below, above, v_below, v_above), 2, kept)
    arrive(jnp.int32(0))
    first_face(f)

    def step(k, _):
        @pl.when((k + 4) % chunk == 0)
        def _():
            arrive((k + 4) // chunk)

        def put(c, t, value):
            stage[c, k, t] = value

        slab_step(f, k, put)
        if last:
            start_sets([(lambda n: stage.at[:, k, :, n], lambda n: out.at[:, k + 2, n])], out_sem)
        else:
            start(stage.at[:, k], out.at[:, k + 2], out_sem)
        if not last:
            pack_edges(packs, lambda c: stage.at[c, k], comps, k + 2)
        return 0

    if not last:
        for pack in packs:
            pack[...] = jnp.zeros_like(pack)
    lax.fori_loop(0, slabs - 4, step, 0)
    arrived(stage, out_sem)


def interior(groups, fields, velocity, speeds, below, above, v_below, v_above, deposit=None):
    last = deposit is None
    slabs, tiles, _, lanes = speeds[0].shape
    rows, comps = 8 * tiles, fields[0].shape[0]
    operands = list(fields) + [velocity, *speeds, below, above, v_below, v_above]
    specs = [ANY] * (len(fields) + 3) + [VMEM] * 4
    form = (8, tiles, lanes) if last else (tiles, 8, lanes)
    out_shape = [jax.ShapeDtypeStruct((comps, slabs, *form), jnp.float32)]
    out_specs = [ANY]
    scratch = [
        pltpu.VMEM((1, comps, slabs, tiles, 8, lanes), jnp.float32),
        pltpu.VMEM((1, 2, slabs, tiles, 8, lanes), jnp.float32),
        *[pltpu.VMEM((1, slabs, tiles, 8, lanes), jnp.float32)] * 2,
        pltpu.VMEM((tiles, comps, 8, lanes), jnp.float32),
        pltpu.VMEM((tiles, comps, 8, lanes), jnp.float32),
        pltpu.VMEM((comps, slabs - 4, tiles, 8, lanes), jnp.float32),
        pltpu.SemaphoreType.DMA((slabs // 4, 5)),
        pltpu.SemaphoreType.DMA,
    ]
    scratch += [pltpu.VMEM((tiles, comps, 8, lanes), jnp.float32)] * 2
    if not last:
        out_shape += [jax.ShapeDtypeStruct((2 * comps, slabs, lanes), jnp.float32)] * 2
        out_specs += [VMEM] * 2
        operands.append(deposit)
        specs.append(VMEM)
    cells = comps * (slabs - 4) * rows * lanes
    return pl.pallas_call(
        functools.partial(interior_kernel, last, groups, len(fields)),
        out_shape=tuple(out_shape),
        in_specs=specs,
        out_specs=tuple(out_specs),
        scratch_shapes=scratch,
        compiler_params=params(),
        cost_estimate=cost(40 * cells, 4 * (2 * cells + 4 * slabs * rows * lanes)),
        name="interior",
    )(*operands)


def boundary_kernel(last, groups, slabs, *refs):
    refs = list(refs)
    count = 5 if last else 3
    fields, velocity, speeds = refs[:count], refs[count], refs[count + 1 : count + 3]
    u_outer = refs[count + 3 : count + 5]
    below, above, v_below, v_above = refs[count + 5 : count + 9]
    del refs[: count + 9]
    if last:
        out = refs[1]
        del refs[:2]
    else:
        deposit, packed, ends, packs = refs[0], refs[1:3], refs[3:5], refs[5:7]
        del refs[:7]
    q, uv, sz, fall, fx, lx, stage, in_sem, out_sem = refs
    comps, tiles = q.shape[1], sz.shape[2]

    if last:
        middle, end_low, end_high, x_low, x_high = fields
        for block, at, source in (
            (0, 0, x_low), (0, 2, end_low), (0, 4, middle.at[:, pl.ds(2, 2)]),
            (1, 0, middle.at[:, pl.ds(slabs - 4, 2)]), (1, 2, end_high), (1, 4, x_high),
        ):
            start(source, q.at[block, :, pl.ds(at, 2)], in_sem.at[block, 0])
    else:
        state, x_low, x_high = fields
        for block, at, first in ((0, 2, 0), (1, 0, slabs - 4)):
            pair = (
                lambda n: state.at[:, pl.ds(first, 4), n], lambda n: q.at[block, :, pl.ds(at, 4), :, n]
            )
            start_sets([pair], in_sem.at[block, 0])
        for block, at, halo in ((0, 0, x_low), (1, 4, x_high)):
            pairs = [
                (lambda n, c=c: halo.at[pl.ds(2 * c, 2), n], lambda n, c=c: q.at[block, c, pl.ds(at, 2), :, n])
                for c in range(comps)
            ]
            start_sets(pairs, in_sem.at[block, 0])
    edge = pl.ds(2 * comps, 1)
    for block in range(2):
        outer, first, at = 3 * block, block * (slabs - 3), 1 - block
        pairs = [
            (lambda n: u_outer[block].at[edge, n], lambda n: uv.at[block, 0, pl.ds(outer, 1), :, n]),
            (
                lambda n: velocity.at[pl.ds(0, 2), pl.ds(first, 3), n],
                lambda n: uv.at[block, :, pl.ds(at, 3), :, n],
            ),
        ]
        for number, pair in enumerate(pairs):
            start_sets([pair], in_sem.at[block, number + 1])
        span = pl.ds(block * (slabs - 2), 2)
        for n, target in enumerate((sz, fall)):
            start(speeds[n].at[span], target.at[block], in_sem.at[block, n + 3])
    if not last:
        packs[0][...] = packed[0][...]
        packs[1][...] = packed[1][...]

    def one(block, _):
        begin = block * (slabs - 2)
        arrived(q.at[block], in_sem.at[block, 0])
        spots = (uv.at[block, 0, pl.ds(0, 1)], uv.at[block, :, pl.ds(0, 3)], sz.at[block], fall.at[block])
        for n, spot in enumerate(spots):
            arrived(spot, in_sem.at[block, n + 1])

        def complete(slab, _):
            x = begin + slab - 2
            lands = (x >= slabs) | ((x >= 0) & (x < groups)) | (x + slabs < groups)

            @pl.when(lands)
            def _():
                staged([functools.partial(dust_job, q, block, slab, falling(deposit, x + 2))])

            return 0

        if not last:
            lax.fori_loop(0, 6, complete, 0)
        f = Slabs(q, uv, sz, fall, fx, lx, block, 1, 0, (below, above, v_below, v_above), begin)
        first_face(f)

        def step(k, _):
            def put(c, t, value):
                stage[block, c, k, t] = value

            slab_step(f, k, put)
            if not last:
                pack_edges(packs, lambda c: stage.at[block, c, k], comps, begin + k)
            return 0

        lax.fori_loop(0, 2, step, 0)
        if last:
            span = pl.ds(begin, 2)
            pair = (lambda n: stage.at[block, :, :, :, n], lambda n: out.at[:, span, n])
            start_sets([pair], out_sem.at[block])
        else:
            for number in range(2):

                @pl.when(block == number)
                def _():
                    start(stage.at[number], ends[number], out_sem.at[number])

        return 0

    lax.fori_loop(0, 2, one, 0)
    for block in range(2):
        arrived(stage.at[block], out_sem.at[block])


def boundary(groups, fields, velocity, speeds, u_outer, below, above, v_below, v_above, *, deposit=None, packed=None, out=None):
    last = out is not None
    slabs, tiles, _, lanes = speeds[0].shape
    rows, comps = 8 * tiles, fields[0].shape[0]
    operands = list(fields) + [velocity, *speeds, *u_outer, below, above, v_below, v_above]
    specs = [ANY] * (len(fields) + 5) + [VMEM] * 4
    form = (tiles, 8, lanes)
    scratch = [
        pltpu.VMEM((2, comps, 6, tiles, 8, lanes), jnp.float32),
        pltpu.VMEM((2, 2, 4, tiles, 8, lanes), jnp.float32),
        *[pltpu.VMEM((2, 2, tiles, 8, lanes), jnp.float32)] * 2,
        pltpu.VMEM((tiles, comps, 8, lanes), jnp.float32),
        pltpu.VMEM((tiles, comps, 8, lanes), jnp.float32),
        pltpu.VMEM((2, comps, 2, *form), jnp.float32),
        pltpu.SemaphoreType.DMA((2, 5)),
        pltpu.SemaphoreType.DMA((2,)),
    ]
    if last:
        aliases = {len(operands): 0}
        operands.append(out)
        specs.append(ANY)
        out_shape = jax.ShapeDtypeStruct(out.shape, out.dtype)
        out_specs = ANY
    else:
        aliases = {}
        operands += [deposit, *packed]
        specs += [VMEM] * 3
        out_shape = (jax.ShapeDtypeStruct((comps, 2, *form), jnp.float32),) * 2
        out_shape += (jax.ShapeDtypeStruct((2 * comps, slabs, lanes), jnp.float32),) * 2
        out_specs = (ANY, ANY, VMEM, VMEM)
    cells = comps * 4 * rows * lanes
    return pl.pallas_call(
        functools.partial(boundary_kernel, last, groups, slabs),
        out_shape=out_shape,
        in_specs=specs,
        out_specs=out_specs,
        scratch_shapes=scratch,
        input_output_aliases=aliases,
        compiler_params=params(),
        cost_estimate=cost(50 * cells, 4 * 6 * cells),
        name="boundary",
    )(*operands)


def speeds_kernel(velocity, sz, fall, wind, sems):
    step = pl.program_id(0)
    part, count, lanes = sz.shape[0], wind.shape[1], wind.shape[3]
    lane = lax.broadcasted_iota(jnp.int32, (8, lanes), 1)
    is_first, is_last = lane == 0, lane == lanes - 1

    @pl.when(step == 0)
    def _():
        for j in range(wind.shape[0] // part):
            span = pl.ds(j * part, part)
            start_sets([(lambda n: velocity.at[2, span, n], lambda n: wind.at[span, :, n])], sems.at[j])

    arrived(wind.at[pl.ds(step * part, part)], sems.at[step])

    def one(x, _):
        here = [FACTOR * wind[step * part + x, t] for t in range(count)]
        over = [pltpu.roll(tile, lanes - 1, 1) for tile in here]
        under = [pltpu.roll(tile, 1, 1) for tile in here]
        upper = [jnp.where(is_last, jnp.maximum(a, 0.0), a + b) for a, b in zip(here, over)]
        lower = [jnp.where(is_first, jnp.minimum(a, 0.0), a + b) for a, b in zip(here, under)]
        for t in range(count):
            sz[x, t] = upper[t]
            fall[x, t] = lower[t]
        return 0

    lax.fori_loop(0, part, one, 0)


def face_speeds(velocity):
    _, slabs, _, tiles, lanes = velocity.shape
    part = 8
    return pl.pallas_call(
        speeds_kernel,
        grid=(slabs // part,),
        out_shape=(jax.ShapeDtypeStruct((slabs, tiles, 8, lanes), jnp.float32),) * 2,
        in_specs=[ANY],
        out_specs=(pl.BlockSpec((part, tiles, 8, lanes), lambda i: (i, 0, 0, 0)),) * 2,
        scratch_shapes=[
            pltpu.VMEM((slabs, tiles, 8, lanes), jnp.float32),
            pltpu.SemaphoreType.DMA((slabs // part,)),
        ],
        compiler_params=params(),
        cost_estimate=cost(8 * slabs * 8 * tiles * lanes, 12 * slabs * 8 * tiles * lanes),
        name="face_speeds",
    )(velocity)


def x_copies(state, velocity, low, high, sems):
    comps, slabs = state.shape[0], state.shape[1]
    copies = []
    for n, (target, first, edge) in enumerate(((low, 0, 0), (high, slabs - 2, slabs - 1))):
        pairs = [(state.at[c, pl.ds(first, 2)], target.at[pl.ds(2 * c, 2)]) for c in range(comps)]
        pairs.append((velocity.at[0, pl.ds(edge, 1)], target.at[pl.ds(2 * comps, 1)]))
        copies += [pltpu.make_async_copy(*pair, sems.at[n, i]) for i, pair in enumerate(pairs)]
    return copies


def as_column(row):
    count = row.shape[1]
    shape = (count, count)
    same = lax.broadcasted_iota(jnp.int32, shape, 0) == lax.broadcasted_iota(jnp.int32, shape, 1)
    return jnp.sum(jnp.where(same, row, 0.0), axis=1, keepdims=True)


def stress_kernel(wind, state, velocity, stress, x_low, x_high, gathered, sems):
    step, steps = pl.program_id(0), pl.num_programs(0)
    part, rows, lanes = wind.shape[1:]
    slabs = stress.shape[0]

    @pl.when(step == 0)
    def _():
        for copy in x_copies(state, velocity, x_low, x_high, sems):
            copy.start()

    lane = lax.broadcasted_iota(jnp.int32, (rows, lanes), 1)
    weight = jnp.zeros((rows, lanes), jnp.float32)
    for level, value in enumerate(profile_weights):
        weight = jnp.where(lane == level, value, weight)
    total = jnp.zeros((rows, lanes), jnp.float32)
    for x in range(part):
        east, north = wind[0, x], wind[1, x]
        friction = jnp.where(lane < LEVELS, weight * (east * east + north * north), 0.0)
        total = total + pltpu.roll(friction, LEVELS * x, 1) if x else friction

    @pl.when(step == 0)
    def _():
        gathered[...] = total

    @pl.when(step > 0)
    def _():
        gathered[...] += pltpu.roll(total, LEVELS * part * step, 1)

    @pl.when(step == steps - 1)
    def _():
        gathered[...] = gathered[...].T
        total = gathered[pl.ds(0, slabs, stride=LEVELS), :]
        for level in range(1, LEVELS):
            total = total + gathered[pl.ds(level, slabs, stride=LEVELS), :]
        stress[...] = total
        for copy in x_copies(state, velocity, x_low, x_high, sems):
            copy.wait()


def tile_stress(state, velocity):
    comps, slabs, rows, lanes = state.shape
    x_packed = jax.ShapeDtypeStruct((2 * comps + 1, rows, lanes), jnp.float32)
    part = 8
    return pl.pallas_call(
        stress_kernel,
        grid=(slabs // part,),
        out_shape=(jax.ShapeDtypeStruct((slabs, lanes), jnp.float32), x_packed, x_packed),
        in_specs=[pl.BlockSpec((2, part, rows, lanes), lambda i: (0, i, 0, 0)), ANY, ANY],
        out_specs=(pl.BlockSpec((slabs, lanes), lambda i: (0, 0)), ANY, ANY),
        scratch_shapes=[pltpu.VMEM((rows, lanes), jnp.float32), pltpu.SemaphoreType.DMA((2, comps + 1))],
        compiler_params=params(),
        cost_estimate=cost(10 * slabs * rows * lanes, 8 * slabs * rows * lanes),
        name="tile_stress",
    )(velocity, state, velocity)


def pack_kernel(low_in, high_in, v_low, v_high, low, high):
    comps, part = low_in.shape[:2]

    for x in range(part):
        for c in range(comps):
            for r in range(2):
                low[2 * c + r, x : x + 1, :] = low_in[c, x, r : r + 1, :]
                high[2 * c + r, x : x + 1, :] = high_in[c, x, 6 + r : 7 + r, :]
        low[2 * comps, x : x + 1, :] = v_low[0, x, 0:1, :]
        high[2 * comps, x : x + 1, :] = v_high[0, x, 7:8, :]


def pack(state, velocity):
    comps, slabs, rows, lanes = state.shape
    part = 8
    last = rows // 8 - 1
    packed = jax.ShapeDtypeStruct((2 * comps + 1, slabs, lanes), jnp.float32)
    packed_spec = pl.BlockSpec((2 * comps + 1, part, lanes), lambda i: (0, i, 0))
    return pl.pallas_call(
        pack_kernel,
        grid=(slabs // part,),
        out_shape=(packed, packed),
        in_specs=[
            pl.BlockSpec((comps, part, 8, lanes), lambda i: (0, i, 0, 0)),
            pl.BlockSpec((comps, part, 8, lanes), lambda i: (0, i, last, 0)),
            pl.BlockSpec((1, part, 8, lanes), lambda i: (1, i, 0, 0)),
            pl.BlockSpec((1, part, 8, lanes), lambda i: (1, i, last, 0)),
        ],
        out_specs=(packed_spec, packed_spec),
        compiler_params=params(),
        cost_estimate=cost(1, 12 * (2 * comps + 1) * rows * lanes),
        name="pack",
    )(state, state, velocity, velocity)


def census_kernel(stress, threshold, tile_owner, parcel_owner, count, share, copies):
    groups, height, lanes = copies.shape
    slabs = stress.shape[0]
    owners = parcel_owner[...].astype(jnp.float32)
    shape = (groups, slabs)
    place = (owners == lax.broadcasted_iota(jnp.int32, shape, 0).astype(jnp.float32)).astype(jnp.float32)
    live = as_column(count[...].astype(jnp.float32))
    shape = (slabs, lanes)
    reach = lax.broadcasted_iota(jnp.int32, shape, 1).astype(jnp.float32) < live
    masses = jnp.where(reach, share[0], 0.0)
    copies[0, 0:slabs] = stress[...]
    copies[0, slabs : slabs + 8] = jnp.zeros((8, lanes), jnp.float32)
    copies[0, slabs : slabs + 1] = threshold[...]
    copies[0, slabs + 1 : slabs + 2, 0:slabs] = tile_owner[...].astype(jnp.float32)
    copies[0, slabs + 8 : height] = jnp.dot(place, masses, precision=HIGHEST, preferred_element_type=jnp.float32)
    whole = copies[0]
    for g in range(1, groups):
        copies[g] = whole


def census(groups, stress, *small):
    slabs, lanes = stress.shape
    return pl.pallas_call(
        census_kernel,
        out_shape=jax.ShapeDtypeStruct((groups, slabs + 8 + groups, lanes), jnp.float32),
        in_specs=[VMEM] * 6,
        out_specs=VMEM,
        compiler_params=params(),
        cost_estimate=cost(10**6, 10**6),
        name="census",
    )(stress, *small)


def deposit_kernel(slabs, me, gathered, low_in, high_in, flux_out, deposit, low, high, flux, dropped):
    groups, lanes = gathered.shape[0], gathered.shape[2]
    here = me[0]
    limits = jnp.concatenate([gathered[g, slabs : slabs + 1] for g in range(groups)], axis=0)
    total = jnp.zeros((groups, lanes), jnp.float32)
    shape = (groups, slabs)
    numbers = lax.broadcasted_iota(jnp.int32, shape, 0).astype(jnp.float32)
    for g in range(groups):
        owners = gathered[g, slabs + 1 : slabs + 2, 0:slabs]
        stress = gathered[g, 0:slabs]
        named = (owners == numbers).astype(jnp.float32)
        limit = lax.dot_general(
            named, limits, (((0,), (0,)), ((), ())), precision=HIGHEST, preferred_element_type=jnp.float32
        )
        lifting = jnp.maximum(stress - limit, 0.0)
        total = total + jnp.dot(named, lifting, precision=HIGHEST, preferred_element_type=jnp.float32)
    flux[...] = total / slabs
    flux_out[...] = flux[pl.ds(here, 1), :]
    dropped[...] = jnp.zeros_like(dropped)
    before, after = jnp.maximum(here - 1, 0), jnp.minimum(here + 1, groups - 1)
    has_before, has_after = here > 0, here < groups - 1
    base = slabs + 8
    for p in range(groups):
        x = p % slabs
        row = flux[p : p + 1, :]
        dropped[x + 2 : x + 3] += row * gathered[p, pl.ds(base + here, 1), :]
        if x >= slabs - 2:
            mass = row * gathered[p, pl.ds(base + before, 1), :]
            dropped[x - slabs + 2 : x - slabs + 3] += jnp.where(has_before, mass, 0.0)
        if x < 2:
            mass = row * gathered[p, pl.ds(base + after, 1), :]
            dropped[x + slabs + 2 : x + slabs + 3] += jnp.where(has_after, mass, 0.0)
    own = dropped[2 : 2 + slabs, :]
    dropped[...] = dropped[...].T
    count = deposit.shape[0]
    tiles = [tile_of(dropped, t, count) for t in range(count)]
    for t, tile in enumerate(tiles):
        deposit[t] = tile
    lane = lax.broadcasted_iota(jnp.int32, (slabs, lanes), 1)
    rows = lanes
    dust = low.shape[0] - 3
    low[...] = low_in[...]
    high[...] = high_in[...]
    for r in range(2):
        low[dust + r] += jnp.where(lane == 0, own[:, r : r + 1], 0.0)
        high[dust + r] += jnp.where(lane == 0, own[:, rows - 2 + r : rows - 1 + r], 0.0)


def settle(me, gathered, low, high, slabs):
    groups, _, lanes = gathered.shape
    edge = jax.ShapeDtypeStruct(low.shape, jnp.float32)
    return pl.pallas_call(
        functools.partial(deposit_kernel, slabs),
        out_shape=(
            jax.ShapeDtypeStruct((1, lanes), jnp.float32),
            jax.ShapeDtypeStruct((lanes // 8, 8, lanes), jnp.float32),
            edge,
            edge,
        ),
        in_specs=[SMEM, VMEM, VMEM, VMEM],
        out_specs=(VMEM, VMEM, VMEM, VMEM),
        scratch_shapes=[
            pltpu.VMEM((groups, lanes), jnp.float32),
            pltpu.VMEM((lanes, lanes), jnp.float32),
        ],
        compiler_params=params(),
        cost_estimate=cost(10**6, 10**6),
        name="settle",
    )(me, gathered, low, high)


def exchange(low, high, axis):
    count = lax.axis_size(axis)
    forward = [(i, i + 1) for i in range(count - 1)]
    backward = [(target, source) for source, target in forward]
    return lax.ppermute(high, axis, forward), lax.ppermute(low, axis, backward)


def shards(state, velocity, threshold, tile_owner, parcel_owner, parcel_count, parcel_share):
    groups = lax.axis_size("gx")
    slabs = state.shape[1]
    me = lax.axis_index("gx").astype(jnp.int32).reshape(1)

    stress, own_low, own_high = tile_stress(state, velocity)
    low, high = pack(state, velocity)
    copies = census(
        groups, stress, threshold, tile_owner[:, :, 0], parcel_owner[:, :, 0], parcel_count, parcel_share
    )
    rows, lanes = state.shape[2:]

    def sets(array):
        return array.reshape(*array.shape[:-2], 8, rows // 8, lanes)

    velocity = sets(velocity)
    speeds = face_speeds(velocity)
    gathered = lax.all_to_all(copies, "gx", split_axis=0, concat_axis=0, tiled=True)
    flux, deposit, low, high = settle(me, gathered, low, high, slabs)
    below, above = exchange(low, high, "gy")
    own_low, own_high, _ = lax.optimization_barrier((own_low, own_high, gathered))
    x_low, x_high = exchange(own_low, own_high, "gx")
    x_low, x_high = sets(x_low), sets(x_high)
    u_edges = (x_low, x_high)
    middle, pack_low, pack_high = interior(groups, [sets(state)], velocity, speeds, below, above, below, above, deposit)
    end_low, end_high, y_low, y_high = boundary(
        groups, [sets(state), x_low, x_high], velocity, speeds, u_edges, below, above, below, above,
        deposit=deposit, packed=(pack_low, pack_high),
    )
    x2_low, x2_high = exchange(end_low, end_high, "gx")
    below2, above2 = exchange(y_low, y_high, "gy")
    (inside,) = interior(groups, [middle, end_low, end_high], velocity, speeds, below2, above2, below, above)
    fields = boundary(
        groups, [middle, end_low, end_high, x2_low, x2_high], velocity, speeds, u_edges, below2, above2, below, above,
        out=inside,
    )
    return fields.reshape(state.shape), flux


def solution(mesh):
    return jax.shard_map(
        shards,
        mesh=mesh,
        in_specs=(
            P(None, "gx", "gy", None),
            P(None, "gx", "gy", None),
            P("gx", "gy"),
            P("gy", "gx", None),
            P("gy", "gx", None),
            P("gy", "gx"),
            P("gy", "gx", None),
        ),
        out_specs=(P(None, "gx", "gy", None), P("gx", "gy")),
        check_vma=False,
    )
```

```python
import functools

import jax
import jax.numpy as jnp
from jax import lax
from jax.experimental import pallas as pl
from jax.experimental.pallas import tpu as pltpu
from jax.sharding import PartitionSpec as P

LEVELS = 4
profile_weights = (0.4, 0.3, 0.2, 0.1)
time_step = 0.1
FACTOR = 0.25 * time_step

VMEM_LIMIT = 48 * 1024 * 1024
PAIR = 2
HIGHEST = lax.Precision.HIGHEST
ANY = pl.BlockSpec(memory_space=pl.ANY)
VMEM = pl.BlockSpec(memory_space=pltpu.VMEM)
SMEM = pl.BlockSpec(memory_space=pltpu.SMEM)


def params():
    return pltpu.CompilerParams(vmem_limit_bytes=VMEM_LIMIT)


def cost(flops, moved):
    return pl.CostEstimate(flops=int(flops), bytes_accessed=int(moved), transcendentals=0)


def minmod(a, b):
    return jnp.maximum(jnp.minimum(a, b), jnp.minimum(jnp.maximum(a, b), 0.0))


def tile_of(ref, t, tiles):
    return ref[pl.ds(t, 8, stride=tiles), :]


class Slabs:
    def __init__(self, q, uv, sz, fall, fx, lx, block, x_at, at, halo, x, kept=None):
        self.q, self.uv, self.sz, self.falls, self.fx, self.lx = q, uv, sz, fall, fx, lx
        self.block, self.x_at, self.at, self.kept = block, x_at, at, kept
        self.halo, self.x = halo, x
        self.comps, self.tiles, self.lanes = q.shape[1], sz.shape[2], q.shape[-1]

    def field(self, c, slab, t):
        return self.q[self.block, c, slab, t]

    def row(self, k, which, number):
        return self.halo[which][number, pl.ds(self.x + k, 1), :]

    def centre(self, c, k, t):
        slab = k + 2
        if 0 <= t < self.tiles:
            return self.field(c, slab, t)
        row = lax.broadcasted_iota(jnp.int32, (8, self.lanes), 0)
        if t < 0:
            moved = pltpu.roll(self.field(c, slab, t + self.tiles), 1, 0)
            return jnp.where(row == 0, self.row(k, 0, 2 * c + t + 2), moved)
        t -= self.tiles
        return jnp.where(row == 7, self.row(k, 1, 2 * c + t), pltpu.roll(self.field(c, slab, t), 7, 0))

    def east(self, k, t):
        here = k + self.x_at
        return FACTOR * (self.uv[self.block, 0, here, t] + self.uv[self.block, 0, here + 1, t])

    def wind(self, k, t):
        inner = self.uv[self.block, 1, k + self.x_at, t % self.tiles]
        if 0 <= t < self.tiles:
            return inner
        row = lax.broadcasted_iota(jnp.int32, (8, self.lanes), 0)
        end, turn, which = (0, 1, 2) if t < 0 else (7, 7, 3)
        return jnp.where(row == end, self.row(k, which, 2 * self.comps), pltpu.roll(inner, turn, 0))

    def north(self, k, t):
        return FACTOR * (self.wind(k, t) + self.wind(k, t + 1))

    def up(self, k, t):
        return self.sz[self.block, k + self.at, t]

    def down(self, k, t):
        return self.falls[self.block, k + self.at, t]


def each(function, *lists):
    return [function(*items) for items in zip(*lists)]


def minmods(a, b):
    low, high = each(jnp.minimum, a, b), each(jnp.maximum, a, b)
    high = each(lambda x: jnp.minimum(x, 0.0), high)
    return each(jnp.maximum, low, high)


def difference(a, b):
    return each(lambda x, y: x - y, a, b)


def total_of(a, b):
    return each(lambda x, y: x + y, a, b)


def face_flux(speeds, masks, low_side, high_side):
    picked = each(jnp.where, masks, low_side, high_side)
    return each(lambda x, y: x * y, speeds, picked)


def staged(jobs):
    waiting = []
    for job in jobs:
        stores = job()
        for ref, index, value in waiting:
            ref[index] = value
        waiting = stores
    for ref, index, value in waiting:
        ref[index] = value


def first_face(f):
    def job(ts):
        spots = [(t, c) for t in ts for c in range(f.comps)]
        speeds = {t: f.east(-1, t) for t in ts}
        masks = {t: speeds[t] > 0 for t in ts}
        a, b, q0, q1 = [[f.field(c, slab, t) for t, c in spots] for slab in range(4)]
        middle = difference(q0, b)
        left = total_of(total_of(b, b), minmods(middle, difference(b, a)))
        slope = minmods(difference(q1, q0), middle)
        twice = total_of(q0, q0)
        flux = face_flux([speeds[t] for t, _ in spots], [masks[t] for t, _ in spots], left, difference(twice, slope))
        stores = [(f.fx, spot, x) for spot, x in zip(spots, flux)]
        if f.kept is not None:
            stores += [(f.kept[0], spot, x) for spot, x in zip(spots, twice)]
            stores += [(f.kept[1], spot, x) for spot, x in zip(spots, difference(q1, q0))]
        return stores + [(f.lx, spot, x) for spot, x in zip(spots, total_of(twice, slope))]

    staged([functools.partial(job, range(t, t + PAIR)) for t in range(0, f.tiles, PAIR)])


def slab_step(f, k, put, group_size=4):
    slab = k + 2
    lane = lax.broadcasted_iota(jnp.int32, (8, f.lanes), 1)
    top = f.lanes - 1
    is_first, is_last = lane == 0, lane == top
    carry = []
    speed = f.north(k, -1)
    for c in range(f.comps):
        a, b, q0, q1 = [f.centre(c, k, t) for t in (-2, -1, 0, 1)]
        middle, ahead = q0 - b, q1 - q0
        left_state = (b + b) + minmod(middle, b - a)
        slope = minmod(ahead, middle)
        twice = q0 + q0
        flux = speed * jnp.where(speed > 0, left_state, twice - slope)
        carry.append((q0, q1, ahead, twice, twice + slope, flux))
    states, doubles = {}, {}

    def vertical(t):
        for c in range(f.comps):
            q0 = f.field(c, slab, t)
            over = jnp.where(is_last, 0.0, pltpu.roll(q0, top, 1))
            under = jnp.where(is_first, 0.0, pltpu.roll(q0, 1, 1))
            slope = minmod(over - q0, q0 - under)
            if f.kept is not None:
                doubles[c, t] = f.kept[0][t, c]
            twice = double(c, t, q0)
            states[t, c] = (twice - slope, twice + slope)

    def flush(held):
        for c, t, flux_x, left_x, twice_x, step_x, value in held:
            f.fx[t, c], f.lx[t, c] = flux_x, left_x
            if f.kept is not None:
                f.kept[0][t, c], f.kept[1][t, c] = twice_x, step_x
            put(c, t, value)

    def double(c, t, tile):
        if f.kept is None or not 0 <= t < f.tiles:
            return tile + tile
        return doubles[c, t]

    held = []
    for t in range(group_size):
        vertical(t)
    for begin in range(0, f.tiles, group_size):
        group = range(begin, min(begin + group_size, f.tiles))
        for t in range(begin + group_size, min(begin + 2 * group_size, f.tiles)):
            vertical(t)
        loaded = {}
        for t in group:
            loaded[t] = (f.east(k, t), f.north(k, t), f.up(k, t), f.down(k, t))
            for c in range(f.comps):
                loaded[t, c] = (
                    f.centre(c, k, t + 2), f.field(c, slab + 1, t), f.field(c, slab + 2, t),
                    f.fx[t, c], f.lx[t, c], f.kept[1][t, c] if f.kept is not None else None,
                )
        flush(held)
        held = []
        for t in group:
            speed_x, speed_y, speed_z, fall = loaded[t]
            go_x, go_y, go_z, go_fall = speed_x > 0, speed_y > 0, speed_z > 0, fall > 0
            for c in range(f.comps):
                y2, x1, x2, flux_w, left_w, step_w = loaded[t, c]
                q0, y1, ahead, twice, left_y, flux_y = carry[c]
                beyond = y2 - y1
                slope = minmod(beyond, ahead)
                twice_y = double(c, t + 1, y1)
                flux_next = speed_y * jnp.where(go_y, left_y, twice_y - slope)
                total = flux_next - flux_y
                carry[c] = (y1, y2, beyond, twice_y, twice_y + slope, flux_next)
                step_x = x2 - x1
                slope = minmod(step_x, x1 - q0 if step_w is None else step_w)
                twice_x = x1 + x1
                flux_x = speed_x * jnp.where(go_x, left_w, twice_x - slope)
                left_x = twice_x + slope
                total = total + (flux_x - flux_w)
                lower, upper = states[t, c]
                flux_z = speed_z * jnp.where(go_z, upper, pltpu.roll(lower, top, 1))
                flux_below = fall * jnp.where(go_fall, pltpu.roll(upper, 1, 1), lower)
                total = total + (flux_z - flux_below)
                held.append((c, t, flux_x, left_x, twice_x, step_x, q0 - total))
    flush(held)


def dust_job(q, block, slab, dust):
    c, spots = q.shape[1] - 1, range(q.shape[3])
    tiles = total_of([q[block, c, slab, t] for t in spots], dust(spots))
    return [(q, (block, c, slab, t), tile) for t, tile in zip(spots, tiles)]


def falling(deposit, column):
    lanes = deposit.shape[-1]

    def dust(spots):
        parts = [pltpu.roll(deposit[t], lanes - column, 1) for t in spots]
        lane = lax.broadcasted_iota(jnp.int32, parts[0].shape, 1)
        return [jnp.where(lane == 0, part, 0.0) for part in parts]

    return dust


def pack_edges(packs, stage_slab, comps, x):
    x = pl.ds(x, 1)
    stores = []
    for c in range(comps):
        tiles = stage_slab(c)
        count = tiles.shape[0]
        for r in range(2):
            stores.append((packs[0], (2 * c + r, x), tiles[r, 0:1, :]))
            stores.append((packs[1], (2 * c + r, x), tiles[count - 2 + r, 7:8, :]))
    staged([lambda: stores])


def start(source, target, sem):
    pltpu.make_async_copy(source, target, sem).start()


def start_sets(pairs, sem):
    for source, target in pairs:
        for number in range(8):
            start(source(number), target(number), sem)


def arrived(spot, sem):
    pltpu.make_async_copy(spot, spot, sem).wait()


def interior_kernel(last, groups, count, *refs):
    refs = list(refs)
    fields, velocity, speeds = refs[:count], refs[count], refs[count + 1 : count + 3]
    below, above, v_below, v_above = refs[count + 3 : count + 7]
    del refs[: count + 7]
    deposit = None if last else refs.pop(0)
    out = refs.pop(0)
    packs = None if last else (refs.pop(0), refs.pop(0))
    q, uv, sz, fall, fx, lx, stage, in_sem, out_sem = refs[:9]
    kept = refs[9:11]
    comps, slabs, tiles = q.shape[1], q.shape[2], sz.shape[2]
    chunk, flight = (8, 3) if last else (4, 6)
    chunks = slabs // chunk

    def fetch(j, first, final):
        span = pl.ds(j * chunk, chunk)
        if last:
            middle, low, high = fields
            begin, size = j * chunk, chunk
            if first:
                begin, size = begin + 2, size - 2
                start(low, q.at[0, :, pl.ds(0, 2)], in_sem.at[j, 0])
            if final:
                size -= 2
                start(high, q.at[0, :, pl.ds(slabs - 2, 2)], in_sem.at[j, 0])
            part = pl.ds(begin, size)
            start(middle.at[:, part], q.at[0, :, part], in_sem.at[j, 0])
        else:
            pair = (lambda n: fields[0].at[:, span, n], lambda n: q.at[0, :, span, :, n])
            start_sets([pair], in_sem.at[j, 0])
        pair = (lambda n: velocity.at[pl.ds(0, 2), span, n], lambda n: uv.at[0, :, span, :, n])
        start_sets([pair], in_sem.at[j, 1])
        for n, (source, target) in enumerate(zip(speeds, (sz, fall))):
            start(source.at[span], target.at[0, span], in_sem.at[j, n + 2])

    for j in range(flight):
        fetch(j, j == 0, False)

    def arrive(j):
        span = pl.ds(j * chunk, chunk)
        arrived(q.at[0, :, span], in_sem.at[j, 0])
        for n, spot in enumerate((uv.at[0, :, span], sz.at[0, span], fall.at[0, span])):
            arrived(spot, in_sem.at[j, n + 1])
        later = j + flight

        @pl.when(later < chunks - 1)
        def _():
            fetch(later, False, False)

        @pl.when(later == chunks - 1)
        def _():
            fetch(chunks - 1, False, True)

        def complete(x, _):
            staged([functools.partial(dust_job, q, 0, x, falling(deposit, x + 2))])
            return 0

        if not last:
            lax.fori_loop(j * chunk, jnp.minimum((j + 1) * chunk, groups), complete, 0)

    f = Slabs(q, uv, sz, fall, fx, lx, 0, 2, 2, (below, above, v_below, v_above), 2, kept)
    arrive(jnp.int32(0))
    first_face(f)

    def step(k, _):
        @pl.when((k + 4) % chunk == 0)
        def _():
            arrive((k + 4) // chunk)

        def put(c, t, value):
            stage[c, k, t] = value

        slab_step(f, k, put)
        if last:
            start_sets([(lambda n: stage.at[:, k, :, n], lambda n: out.at[:, k + 2, n])], out_sem)
        else:
            start(stage.at[:, k], out.at[:, k + 2], out_sem)
        if not last:
            pack_edges(packs, lambda c: stage.at[c, k], comps, k + 2)
        return 0

    if not last:
        for pack in packs:
            pack[...] = jnp.zeros_like(pack)
    lax.fori_loop(0, slabs - 4, step, 0)
    arrived(stage, out_sem)


def interior(groups, fields, velocity, speeds, below, above, v_below, v_above, deposit=None):
    last = deposit is None
    slabs, tiles, _, lanes = speeds[0].shape
    rows, comps = 8 * tiles, fields[0].shape[0]
    operands = list(fields) + [velocity, *speeds, below, above, v_below, v_above]
    specs = [ANY] * (len(fields) + 3) + [VMEM] * 4
    form = (8, tiles, lanes) if last else (tiles, 8, lanes)
    out_shape = [jax.ShapeDtypeStruct((comps, slabs, *form), jnp.float32)]
    out_specs = [ANY]
    scratch = [
        pltpu.VMEM((1, comps, slabs, tiles, 8, lanes), jnp.float32),
        pltpu.VMEM((1, 2, slabs, tiles, 8, lanes), jnp.float32),
        *[pltpu.VMEM((1, slabs, tiles, 8, lanes), jnp.float32)] * 2,
        pltpu.VMEM((tiles, comps, 8, lanes), jnp.float32),
        pltpu.VMEM((tiles, comps, 8, lanes), jnp.float32),
        pltpu.VMEM((comps, slabs - 4, tiles, 8, lanes), jnp.float32),
        pltpu.SemaphoreType.DMA((slabs // 4, 5)),
        pltpu.SemaphoreType.DMA,
    ]
    scratch += [pltpu.VMEM((tiles, comps, 8, lanes), jnp.float32)] * 2
    if not last:
        out_shape += [jax.ShapeDtypeStruct((2 * comps, slabs, lanes), jnp.float32)] * 2
        out_specs += [VMEM] * 2
        operands.append(deposit)
        specs.append(VMEM)
    cells = comps * (slabs - 4) * rows * lanes
    return pl.pallas_call(
        functools.partial(interior_kernel, last, groups, len(fields)),
        out_shape=tuple(out_shape),
        in_specs=specs,
        out_specs=tuple(out_specs),
        scratch_shapes=scratch,
        compiler_params=params(),
        cost_estimate=cost(40 * cells, 4 * (2 * cells + 4 * slabs * rows * lanes)),
        name="interior",
    )(*operands)


def boundary_kernel(last, groups, slabs, *refs):
    refs = list(refs)
    count = 5 if last else 3
    fields, velocity, speeds = refs[:count], refs[count], refs[count + 1 : count + 3]
    u_outer = refs[count + 3 : count + 5]
    below, above, v_below, v_above = refs[count + 5 : count + 9]
    del refs[: count + 9]
    if last:
        out = refs[1]
        del refs[:2]
    else:
        deposit, packed, ends, packs = refs[0], refs[1:3], refs[3:5], refs[5:7]
        del refs[:7]
    q, uv, sz, fall, fx, lx, stage, in_sem, out_sem = refs
    comps, tiles = q.shape[1], sz.shape[2]

    if last:
        middle, end_low, end_high, x_low, x_high = fields
        for block, at, source in (
            (0, 0, x_low), (0, 2, end_low), (0, 4, middle.at[:, pl.ds(2, 2)]),
            (1, 0, middle.at[:, pl.ds(slabs - 4, 2)]), (1, 2, end_high), (1, 4, x_high),
        ):
            start(source, q.at[block, :, pl.ds(at, 2)], in_sem.at[block, 0])
    else:
        state, x_low, x_high = fields
        for block, at, first in ((0, 2, 0), (1, 0, slabs - 4)):
            pair = (
                lambda n: state.at[:, pl.ds(first, 4), n], lambda n: q.at[block, :, pl.ds(at, 4), :, n]
            )
            start_sets([pair], in_sem.at[block, 0])
        for block, at, halo in ((0, 0, x_low), (1, 4, x_high)):
            pairs = [
                (lambda n, c=c: halo.at[pl.ds(2 * c, 2), n], lambda n, c=c: q.at[block, c, pl.ds(at, 2), :, n])
                for c in range(comps)
            ]
            start_sets(pairs, in_sem.at[block, 0])
    edge = pl.ds(2 * comps, 1)
    for block in range(2):
        outer, first, at = 3 * block, block * (slabs - 3), 1 - block
        pairs = [
            (lambda n: u_outer[block].at[edge, n], lambda n: uv.at[block, 0, pl.ds(outer, 1), :, n]),
            (
                lambda n: velocity.at[pl.ds(0, 2), pl.ds(first, 3), n],
                lambda n: uv.at[block, :, pl.ds(at, 3), :, n],
            ),
        ]
        for number, pair in enumerate(pairs):
            start_sets([pair], in_sem.at[block, number + 1])
        span = pl.ds(block * (slabs - 2), 2)
        for n, target in enumerate((sz, fall)):
            start(speeds[n].at[span], target.at[block], in_sem.at[block, n + 3])
    if not last:
        packs[0][...] = packed[0][...]
        packs[1][...] = packed[1][...]

    def one(block, _):
        begin = block * (slabs - 2)
        arrived(q.at[block], in_sem.at[block, 0])
        spots = (uv.at[block, 0, pl.ds(0, 1)], uv.at[block, :, pl.ds(0, 3)], sz.at[block], fall.at[block])
        for n, spot in enumerate(spots):
            arrived(spot, in_sem.at[block, n + 1])

        def complete(slab, _):
            x = begin + slab - 2
            lands = (x >= slabs) | ((x >= 0) & (x < groups)) | (x + slabs < groups)

            @pl.when(lands)
            def _():
                staged([functools.partial(dust_job, q, block, slab, falling(deposit, x + 2))])

            return 0

        if not last:
            lax.fori_loop(0, 6, complete, 0)
        f = Slabs(q, uv, sz, fall, fx, lx, block, 1, 0, (below, above, v_below, v_above), begin)
        first_face(f)

        def step(k, _):
            def put(c, t, value):
                stage[block, c, k, t] = value

            slab_step(f, k, put)
            if not last:
                pack_edges(packs, lambda c: stage.at[block, c, k], comps, begin + k)
            return 0

        lax.fori_loop(0, 2, step, 0)
        if last:
            span = pl.ds(begin, 2)
            pair = (lambda n: stage.at[block, :, :, :, n], lambda n: out.at[:, span, n])
            start_sets([pair], out_sem.at[block])
        else:
            for number in range(2):

                @pl.when(block == number)
                def _():
                    start(stage.at[number], ends[number], out_sem.at[number])

        return 0

    lax.fori_loop(0, 2, one, 0)
    for block in range(2):
        arrived(stage.at[block], out_sem.at[block])


def boundary(groups, fields, velocity, speeds, u_outer, below, above, v_below, v_above, *, deposit=None, packed=None, out=None):
    last = out is not None
    slabs, tiles, _, lanes = speeds[0].shape
    rows, comps = 8 * tiles, fields[0].shape[0]
    operands = list(fields) + [velocity, *speeds, *u_outer, below, above, v_below, v_above]
    specs = [ANY] * (len(fields) + 5) + [VMEM] * 4
    form = (tiles, 8, lanes)
    scratch = [
        pltpu.VMEM((2, comps, 6, tiles, 8, lanes), jnp.float32),
        pltpu.VMEM((2, 2, 4, tiles, 8, lanes), jnp.float32),
        *[pltpu.VMEM((2, 2, tiles, 8, lanes), jnp.float32)] * 2,
        pltpu.VMEM((tiles, comps, 8, lanes), jnp.float32),
        pltpu.VMEM((tiles, comps, 8, lanes), jnp.float32),
        pltpu.VMEM((2, comps, 2, *form), jnp.float32),
        pltpu.SemaphoreType.DMA((2, 5)),
        pltpu.SemaphoreType.DMA((2,)),
    ]
    if last:
        aliases = {len(operands): 0}
        operands.append(out)
        specs.append(ANY)
        out_shape = jax.ShapeDtypeStruct(out.shape, out.dtype)
        out_specs = ANY
    else:
        aliases = {}
        operands += [deposit, *packed]
        specs += [VMEM] * 3
        out_shape = (jax.ShapeDtypeStruct((comps, 2, *form), jnp.float32),) * 2
        out_shape += (jax.ShapeDtypeStruct((2 * comps, slabs, lanes), jnp.float32),) * 2
        out_specs = (ANY, ANY, VMEM, VMEM)
    cells = comps * 4 * rows * lanes
    return pl.pallas_call(
        functools.partial(boundary_kernel, last, groups, slabs),
        out_shape=out_shape,
        in_specs=specs,
        out_specs=out_specs,
        scratch_shapes=scratch,
        input_output_aliases=aliases,
        compiler_params=params(),
        cost_estimate=cost(50 * cells, 4 * 6 * cells),
        name="boundary",
    )(*operands)


def speeds_kernel(velocity, sz, fall, wind, sems):
    step = pl.program_id(0)
    part, count, lanes = sz.shape[0], wind.shape[1], wind.shape[3]
    lane = lax.broadcasted_iota(jnp.int32, (8, lanes), 1)
    is_first, is_last = lane == 0, lane == lanes - 1

    @pl.when(step == 0)
    def _():
        for j in range(wind.shape[0] // part):
            span = pl.ds(j * part, part)
            start_sets([(lambda n: velocity.at[2, span, n], lambda n: wind.at[span, :, n])], sems.at[j])

    arrived(wind.at[pl.ds(step * part, part)], sems.at[step])

    def one(x, _):
        here = [FACTOR * wind[step * part + x, t] for t in range(count)]
        over = [pltpu.roll(tile, lanes - 1, 1) for tile in here]
        under = [pltpu.roll(tile, 1, 1) for tile in here]
        upper = [jnp.where(is_last, jnp.maximum(a, 0.0), a + b) for a, b in zip(here, over)]
        lower = [jnp.where(is_first, jnp.minimum(a, 0.0), a + b) for a, b in zip(here, under)]
        for t in range(count):
            sz[x, t] = upper[t]
            fall[x, t] = lower[t]
        return 0

    lax.fori_loop(0, part, one, 0)


def face_speeds(velocity):
    _, slabs, _, tiles, lanes = velocity.shape
    part = 8
    return pl.pallas_call(
        speeds_kernel,
        grid=(slabs // part,),
        out_shape=(jax.ShapeDtypeStruct((slabs, tiles, 8, lanes), jnp.float32),) * 2,
        in_specs=[ANY],
        out_specs=(pl.BlockSpec((part, tiles, 8, lanes), lambda i: (i, 0, 0, 0)),) * 2,
        scratch_shapes=[
            pltpu.VMEM((slabs, tiles, 8, lanes), jnp.float32),
            pltpu.SemaphoreType.DMA((slabs // part,)),
        ],
        compiler_params=params(),
        cost_estimate=cost(8 * slabs * 8 * tiles * lanes, 12 * slabs * 8 * tiles * lanes),
        name="face_speeds",
    )(velocity)


def x_copies(state, velocity, low, high, sems):
    comps, slabs = state.shape[0], state.shape[1]
    copies = []
    for n, (target, first, edge) in enumerate(((low, 0, 0), (high, slabs - 2, slabs - 1))):
        pairs = [(state.at[c, pl.ds(first, 2)], target.at[pl.ds(2 * c, 2)]) for c in range(comps)]
        pairs.append((velocity.at[0, pl.ds(edge, 1)], target.at[pl.ds(2 * comps, 1)]))
        copies += [pltpu.make_async_copy(*pair, sems.at[n, i]) for i, pair in enumerate(pairs)]
    return copies


def as_column(row):
    count = row.shape[1]
    shape = (count, count)
    same = lax.broadcasted_iota(jnp.int32, shape, 0) == lax.broadcasted_iota(jnp.int32, shape, 1)
    return jnp.sum(jnp.where(same, row, 0.0), axis=1, keepdims=True)


def survey_kernel(
    low_in, high_in, v_low, v_high, wind, state, velocity, low, high, stress, x_low, x_high, gathered, sems,
):
    step, steps = pl.program_id(0), pl.num_programs(0)

    @pl.when(step == 0)
    def _():
        for copy in x_copies(state, velocity, x_low, x_high, sems):
            copy.start()

    comps, part, rows, lanes = low_in.shape[0], wind.shape[1], wind.shape[2], wind.shape[3]
    slabs = stress.shape[0]
    for x in range(part):
        for c in range(comps):
            for r in range(2):
                low[2 * c + r, x : x + 1, :] = low_in[c, x, r : r + 1, :]
                high[2 * c + r, x : x + 1, :] = high_in[c, x, 6 + r : 7 + r, :]
        low[2 * comps, x : x + 1, :] = v_low[0, x, 0:1, :]
        high[2 * comps, x : x + 1, :] = v_high[0, x, 7:8, :]
    lane = lax.broadcasted_iota(jnp.int32, (rows, lanes), 1)
    weight = jnp.zeros((rows, lanes), jnp.float32)
    for level, value in enumerate(profile_weights):
        weight = jnp.where(lane == level, value, weight)
    total = jnp.zeros((rows, lanes), jnp.float32)
    for x in range(part):
        east, north = wind[0, x], wind[1, x]
        friction = jnp.where(lane < LEVELS, weight * (east * east + north * north), 0.0)
        total = total + pltpu.roll(friction, LEVELS * x, 1) if x else friction

    @pl.when(step == 0)
    def _():
        gathered[...] = total

    @pl.when(step > 0)
    def _():
        gathered[...] += pltpu.roll(total, LEVELS * part * step, 1)

    @pl.when(step == steps - 1)
    def _():
        gathered[...] = gathered[...].T
        total = gathered[pl.ds(0, slabs, stride=LEVELS), :]
        for level in range(1, LEVELS):
            total = total + gathered[pl.ds(level, slabs, stride=LEVELS), :]
        stress[...] = total
        for copy in x_copies(state, velocity, x_low, x_high, sems):
            copy.wait()


def survey(state, velocity):
    comps, slabs, rows, lanes = state.shape
    part = 8
    last = rows // 8 - 1
    packed = jax.ShapeDtypeStruct((2 * comps + 1, slabs, lanes), jnp.float32)
    packed_spec = pl.BlockSpec((2 * comps + 1, part, lanes), lambda i: (0, i, 0))
    x_packed = jax.ShapeDtypeStruct((2 * comps + 1, rows, lanes), jnp.float32)
    return pl.pallas_call(
        survey_kernel,
        grid=(slabs // part,),
        out_shape=(packed, packed, jax.ShapeDtypeStruct((slabs, lanes), jnp.float32), x_packed, x_packed),
        in_specs=[
            pl.BlockSpec((comps, part, 8, lanes), lambda i: (0, i, 0, 0)),
            pl.BlockSpec((comps, part, 8, lanes), lambda i: (0, i, last, 0)),
            pl.BlockSpec((1, part, 8, lanes), lambda i: (1, i, 0, 0)),
            pl.BlockSpec((1, part, 8, lanes), lambda i: (1, i, last, 0)),
            pl.BlockSpec((2, part, rows, lanes), lambda i: (0, i, 0, 0)),
            ANY,
            ANY,
        ],
        out_specs=(packed_spec, packed_spec, pl.BlockSpec((slabs, lanes), lambda i: (0, 0)), ANY, ANY),
        scratch_shapes=[pltpu.VMEM((rows, lanes), jnp.float32), pltpu.SemaphoreType.DMA((2, comps + 1))],
        compiler_params=params(),
        cost_estimate=cost(10 * slabs * rows * lanes, 10 * slabs * rows * lanes),
        name="survey",
    )(state, state, velocity, velocity, velocity, state, velocity)


def census_kernel(stress, threshold, tile_owner, parcel_owner, count, share, copies):
    groups, height, lanes = copies.shape
    slabs = stress.shape[0]
    owners = parcel_owner[...].astype(jnp.float32)
    shape = (groups, slabs)
    place = (owners == lax.broadcasted_iota(jnp.int32, shape, 0).astype(jnp.float32)).astype(jnp.float32)
    live = as_column(count[...].astype(jnp.float32))
    shape = (slabs, lanes)
    reach = lax.broadcasted_iota(jnp.int32, shape, 1).astype(jnp.float32) < live
    masses = jnp.where(reach, share[0], 0.0)
    copies[0, 0:slabs] = stress[...]
    copies[0, slabs : slabs + 8] = jnp.zeros((8, lanes), jnp.float32)
    copies[0, slabs : slabs + 1] = threshold[...]
    copies[0, slabs + 1 : slabs + 2, 0:slabs] = tile_owner[...].astype(jnp.float32)
    copies[0, slabs + 8 : height] = jnp.dot(place, masses, precision=HIGHEST, preferred_element_type=jnp.float32)
    whole = copies[0]
    for g in range(1, groups):
        copies[g] = whole


def census(groups, stress, *small):
    slabs, lanes = stress.shape
    return pl.pallas_call(
        census_kernel,
        out_shape=jax.ShapeDtypeStruct((groups, slabs + 8 + groups, lanes), jnp.float32),
        in_specs=[VMEM] * 6,
        out_specs=VMEM,
        compiler_params=params(),
        cost_estimate=cost(10**6, 10**6),
        name="census",
    )(stress, *small)


def deposit_kernel(slabs, me, gathered, low_in, high_in, flux_out, deposit, low, high, flux, dropped):
    groups, lanes = gathered.shape[0], gathered.shape[2]
    here = me[0]
    limits = jnp.concatenate([gathered[g, slabs : slabs + 1] for g in range(groups)], axis=0)
    total = jnp.zeros((groups, lanes), jnp.float32)
    shape = (groups, slabs)
    numbers = lax.broadcasted_iota(jnp.int32, shape, 0).astype(jnp.float32)
    for g in range(groups):
        owners = gathered[g, slabs + 1 : slabs + 2, 0:slabs]
        stress = gathered[g, 0:slabs]
        named = (owners == numbers).astype(jnp.float32)
        limit = lax.dot_general(
            named, limits, (((0,), (0,)), ((), ())), precision=HIGHEST, preferred_element_type=jnp.float32
        )
        lifting = jnp.maximum(stress - limit, 0.0)
        total = total + jnp.dot(named, lifting, precision=HIGHEST, preferred_element_type=jnp.float32)
    flux[...] = total / slabs
    flux_out[...] = flux[pl.ds(here, 1), :]
    dropped[...] = jnp.zeros_like(dropped)
    before, after = jnp.maximum(here - 1, 0), jnp.minimum(here + 1, groups - 1)
    has_before, has_after = here > 0, here < groups - 1
    base = slabs + 8
    for p in range(groups):
        x = p % slabs
        row = flux[p : p + 1, :]
        dropped[x + 2 : x + 3] += row * gathered[p, pl.ds(base + here, 1), :]
        if x >= slabs - 2:
            mass = row * gathered[p, pl.ds(base + before, 1), :]
            dropped[x - slabs + 2 : x - slabs + 3] += jnp.where(has_before, mass, 0.0)
        if x < 2:
            mass = row * gathered[p, pl.ds(base + after, 1), :]
            dropped[x + slabs + 2 : x + slabs + 3] += jnp.where(has_after, mass, 0.0)
    own = dropped[2 : 2 + slabs, :]
    dropped[...] = dropped[...].T
    count = deposit.shape[0]
    tiles = [tile_of(dropped, t, count) for t in range(count)]
    for t, tile in enumerate(tiles):
        deposit[t] = tile
    lane = lax.broadcasted_iota(jnp.int32, (slabs, lanes), 1)
    rows = lanes
    dust = low.shape[0] - 3
    low[...] = low_in[...]
    high[...] = high_in[...]
    for r in range(2):
        low[dust + r] += jnp.where(lane == 0, own[:, r : r + 1], 0.0)
        high[dust + r] += jnp.where(lane == 0, own[:, rows - 2 + r : rows - 1 + r], 0.0)


def settle(me, gathered, low, high, slabs):
    groups, _, lanes = gathered.shape
    edge = jax.ShapeDtypeStruct(low.shape, jnp.float32)
    return pl.pallas_call(
        functools.partial(deposit_kernel, slabs),
        out_shape=(
            jax.ShapeDtypeStruct((1, lanes), jnp.float32),
            jax.ShapeDtypeStruct((lanes // 8, 8, lanes), jnp.float32),
            edge,
            edge,
        ),
        in_specs=[SMEM, VMEM, VMEM, VMEM],
        out_specs=(VMEM, VMEM, VMEM, VMEM),
        scratch_shapes=[
            pltpu.VMEM((groups, lanes), jnp.float32),
            pltpu.VMEM((lanes, lanes), jnp.float32),
        ],
        compiler_params=params(),
        cost_estimate=cost(10**6, 10**6),
        name="settle",
    )(me, gathered, low, high)


def exchange(low, high, axis):
    count = lax.axis_size(axis)
    forward = [(i, i + 1) for i in range(count - 1)]
    backward = [(target, source) for source, target in forward]
    return lax.ppermute(high, axis, forward), lax.ppermute(low, axis, backward)


def shards(state, velocity, threshold, tile_owner, parcel_owner, parcel_count, parcel_share):
    groups = lax.axis_size("gx")
    slabs = state.shape[1]
    me = lax.axis_index("gx").astype(jnp.int32).reshape(1)

    low, high, stress, own_low, own_high = survey(state, velocity)
    copies = census(
        groups, stress, threshold, tile_owner[:, :, 0], parcel_owner[:, :, 0], parcel_count, parcel_share
    )
    rows, lanes = state.shape[2:]

    def sets(array):
        return array.reshape(*array.shape[:-2], 8, rows // 8, lanes)

    velocity = sets(velocity)
    speeds = face_speeds(velocity)
    gathered = lax.all_to_all(copies, "gx", split_axis=0, concat_axis=0, tiled=True)
    flux, deposit, low, high = settle(me, gathered, low, high, slabs)
    below, above = exchange(low, high, "gy")
    own_low, own_high, _ = lax.optimization_barrier((own_low, own_high, gathered))
    x_low, x_high = exchange(own_low, own_high, "gx")
    x_low, x_high = sets(x_low), sets(x_high)
    u_edges = (x_low, x_high)
    middle, pack_low, pack_high = interior(groups, [sets(state)], velocity, speeds, below, above, below, above, deposit)
    end_low, end_high, y_low, y_high = boundary(
        groups, [sets(state), x_low, x_high], velocity, speeds, u_edges, below, above, below, above,
        deposit=deposit, packed=(pack_low, pack_high),
    )
    x2_low, x2_high = exchange(end_low, end_high, "gx")
    below2, above2 = exchange(y_low, y_high, "gy")
    (inside,) = interior(groups, [middle, end_low, end_high], velocity, speeds, below2, above2, below, above)
    fields = boundary(
        groups, [middle, end_low, end_high, x2_low, x2_high], velocity, speeds, u_edges, below2, above2, below, above,
        out=inside,
    )
    return fields.reshape(state.shape), flux


def solution(mesh):
    return jax.shard_map(
        shards,
        mesh=mesh,
        in_specs=(
            P(None, "gx", "gy", None),
            P(None, "gx", "gy", None),
            P("gx", "gy"),
            P("gy", "gx", None),
            P("gy", "gx", None),
            P("gy", "gx"),
            P("gy", "gx", None),
        ),
        out_specs=(P(None, "gx", "gy", None), P("gx", "gy")),
        check_vma=False,
    )
```
